32 devices in a mesh: seq: 8 (over z, x), wshard: 4 (over y, core).
Axes of the slice: x: 2, y: 2, z: 4, core: 2. Of those that a mesh axis runs over, the one named last changes fastest.
Arguments:
- tokens: float32 [32, 1024, 768], P('wshard', 'seq'), may hold values from -54 to 54, as said below
- cotangent: float32 [32, 1024, 768], P('wshard', 'seq'), may hold values from -6 to 6
- qkv_master: float32 [768, 2304], P('wshard'), may hold values from -0.21875 to 0.21875
- proj_master: float32 [768, 768], P('wshard'), may hold values from -2.5 to 2.5
- wide_master: float32 [768, 2304], P('wshard'), may hold values from -0.21875 to 0.21875
- down_master: float32 [1152, 768], P('wshard'), may hold values from -0.1875 to 0.1875
- norm_gains: float32 [2, 768], P(None, 'wshard'), may hold values from 0.5 to 1.5
- qkv_first: float32 [768, 2304], P('wshard'), may hold values from -128 to 128
- proj_first: float32 [768, 768], P('wshard'), may hold values from -10 to 10
- wide_first: float32 [768, 2304], P('wshard'), may hold values from -64 to 64
- down_first: float32 [1152, 768], P('wshard'), may hold values from -80 to 80
- gains_first: float32 [2, 768], P(None, 'wshard'), may hold values from -128 to 128
- qkv_second: float32 [768, 2304], P('wshard'), may hold values from 668.4672 to 2673.869
- proj_second: float32 [768, 768], P('wshard'), may hold values from 5.1816 to 20.7264
- wide_second: float32 [768, 2304], P('wshard'), may hold values from 240.51712 to 963.3792
- down_second: float32 [1152, 768], P('wshard'), may hold values from 282.46017 to 1130.496
- gains_second: float32 [2, 768], P(None, 'wshard'), may hold values from 668.4672 to 2673.869
Outputs:
- layer_output: float32 [32, 1024, 768], P('wshard', 'seq')
- input_grad: float32 [32, 1024, 768], P('wshard', 'seq')
- qkv_next: float32 [768, 2304], P('wshard')
- proj_next: float32 [768, 768], P('wshard')
- wide_next: float32 [768, 2304], P('wshard')
- down_next: float32 [1152, 768], P('wshard')
- gains_next: float32 [2, 768], P(None, 'wshard')
- qkv_moment: float32 [768, 2304], P('wshard')
- proj_moment: float32 [768, 768], P('wshard')
- wide_moment: float32 [768, 2304], P('wshard')
- down_moment: float32 [1152, 768], P('wshard')
- gains_moment: float32 [2, 768], P(None, 'wshard')
- qkv_square: float32 [768, 2304], P('wshard')
- proj_square: float32 [768, 768], P('wshard')
- wide_square: float32 [768, 2304], P('wshard')
- down_square: float32 [1152, 768], P('wshard')
- gains_square: float32 [2, 768], P(None, 'wshard')
The draws below stay inside these ranges and needn't reach their ends.
Inputs may be any that keep to these rules, and one draw needn't show every extreme that they name: `tokens`: activations of the layer's input.
All inputs are finite; a program needn't handle non-finite values.
Results may differ from the reference program's by a relative error of at most 0.035.
Values may be sent and summed in bfloat16 or wider, within the bound.
No kernel may reach another device: no remote copies, remote signals or barrier semaphores. Data moves between devices by JAX's collectives and lax.ppermute only.
A program may use at most 192 MiB of HBM per device.

```python
import math
import jax
import jax.numpy as jnp
from jax import lax

D = 768
HEADS = 12
HEAD = 64
FF = 1152
WINDOW = 128
STEP = 10
LENGTH = 1024
SEQ_ALL = 32
TOKENS = 32768


def draw_tokens(key, part):
    key = jax.random.fold_in(key, 7)
    keys = jax.random.split(key, 3)
    row_scale = jnp.exp(jax.random.uniform(keys[0], (SEQ_ALL, LENGTH, 1), jnp.float32, math.log(0.3), math.log(3.0)))
    col_scale = jnp.exp(jax.random.uniform(keys[1], (1, 1, D), jnp.float32, math.log(0.3), math.log(3.0)))
    noise = jnp.clip(jax.random.normal(keys[2], (SEQ_ALL, LENGTH, D), jnp.float32), -6.0, 6.0)
    return noise * row_scale * col_scale


def steps_of(own_key, shape, cuts, least, high):
    level = 1.0
    for position, blocks in cuts:
        draws = jax.random.uniform(jax.random.fold_in(jax.random.fold_in(own_key, 6), position), (blocks,), jnp.float32, least / len(cuts), high / len(cuts))
        level = level * jnp.repeat(jnp.exp(draws), shape[position] // blocks).reshape((-1,) + (1,) * (len(shape) - 1 - position))
    return level


def scatter_about(stream_key, dims, deviation, bound, cuts=(), kind=jnp.bfloat16):
    array = deviation * jax.random.normal(stream_key, dims, jnp.float32)
    if cuts:
        array = array * steps_of(stream_key, dims, cuts, -0.22, 0.18)
    return jnp.clip(array, -bound, bound).astype(kind)


def setup_inputs(seed: int = 0) -> dict:
    streams_of = jax.random.split(jax.random.key(seed), 18)
    return {
        "tokens": draw_tokens(jax.random.fold_in(streams_of[17], 71), 0),
        "cotangent": scatter_about(streams_of[1], (SEQ_ALL, LENGTH, D), 1.0, 6.0, ((0, 4), (1, 8)), jnp.float32),
        "qkv_master": scatter_about(streams_of[2], (D, 3 * D), D ** -0.5, 0.21875, ((0, 4),), jnp.float32),
        "proj_master": scatter_about(streams_of[3], (D, D), (max(D // WINDOW, 1)) ** -0.5, 2.5, ((0, 4),), jnp.float32),
        "wide_master": scatter_about(streams_of[4], (D, 2 * FF), D ** -0.5, 0.21875, ((0, 4),), jnp.float32),
        "down_master": scatter_about(streams_of[5], (FF, D), FF ** -0.5, 0.1875, ((0, 4),), jnp.float32),
        "norm_gains": jnp.clip(1.0 + 0.1 * jax.random.normal(streams_of[6], (2, D), jnp.float32), 0.5, 1.5),
        "qkv_first": scatter_about(streams_of[7], (D, 3 * D), (0.111 * TOKENS ** 0.5), 128.0, ((0, 4),), jnp.float32),
        "proj_first": scatter_about(streams_of[8], (D, D), (0.111 * (TOKENS // (WINDOW + 1)) ** 0.5), 10.0, ((0, 4),), jnp.float32),
        "wide_first": scatter_about(streams_of[9], (D, 2 * FF), (0.0666 * TOKENS ** 0.5), 64.0, ((0, 4),), jnp.float32),
        "down_first": scatter_about(streams_of[10], (FF, D), (0.0722 * TOKENS ** 0.5), 80.0, ((0, 4),), jnp.float32),
        "gains_first": scatter_about(streams_of[11], (2, D), (0.111 * TOKENS ** 0.5), 128.0, ((1, 4),), jnp.float32),
        "qkv_second": jnp.clip(jnp.exp(math.log(2673.869) - 1.3862944 * jax.random.uniform(streams_of[12], (D, 3 * D), jnp.float32) ** steps_of(streams_of[12], (D, 3 * D), ((0, 4),), -0.2, 0.2)), 668.4672, 2673.869),
        "proj_second": jnp.clip(jnp.exp(math.log(20.7264) - 1.3862944 * jax.random.uniform(streams_of[13], (D, D), jnp.float32) ** steps_of(streams_of[13], (D, D), ((0, 4),), -0.2, 0.2)), 5.1816, 20.7264),
        "wide_second": jnp.clip(jnp.exp(math.log(963.3792) - 1.3876558 * jax.random.uniform(streams_of[14], (D, 2 * FF), jnp.float32) ** steps_of(streams_of[14], (D, 2 * FF), ((0, 4),), -0.2, 0.2)), 240.51712, 963.3792),
        "down_second": jnp.clip(jnp.exp(math.log(1130.496) - 1.3868742 * jax.random.uniform(streams_of[15], (FF, D), jnp.float32) ** steps_of(streams_of[15], (FF, D), ((0, 4),), -0.2, 0.2)), 282.46017, 1130.496),
        "gains_second": jnp.clip(jnp.exp(math.log(2673.869) - 1.3862944 * jax.random.uniform(streams_of[16], (2, D), jnp.float32) ** steps_of(streams_of[16], (2, D), ((1, 4),), -0.2, 0.2)), 668.4672, 2673.869),
    }


@jax.custom_vjp
def low(v):
    return lax.optimization_barrier(v.astype(jnp.bfloat16)).astype(jnp.float32)

@jax.custom_vjp
def low_back(v):
    return v

def low_keep(v):
    return (low(v), None)

def low_pass(kept, grad):
    return (grad,)

def back_keep(v):
    return (v, None)

def back_low(kept, grad):
    return (low(grad),)
low.defvjp(low_keep, low_pass)
low_back.defvjp(back_keep, back_low)

def project(left_neighbour, right_neighbour):
    return jnp.einsum('bnh,hm->bnm', left_neighbour, right_neighbour, precision=lax.Precision.HIGHEST)

def layer_norm(value, gain):
    centred = value - lax.optimization_barrier(jnp.mean(value, axis=-1, keepdims=True))
    inverse = lax.rsqrt(lax.optimization_barrier(jnp.mean(centred * centred, axis=-1, keepdims=True)) + 1e-05)
    return centred * inverse * gain

def rope_tables(positions, head):
    freqs = 10000.0 ** (-jnp.arange(0, head, 2).astype(jnp.float32) / head)
    angles = positions.astype(jnp.float32)[:, None] * freqs[None, :]
    angles = jnp.concatenate([angles, angles], axis=-1)[:, None, :]
    return (jnp.cos(angles), jnp.sin(angles))

def rotary(value, cosine, sine):
    half = value.shape[-1] // 2
    turned = jnp.concatenate([-value[..., half:], value[..., :half]], axis=-1)
    return value * cosine + turned * sine

def window_mask(total, tiles, window):
    half = window // 2
    row = jnp.arange(window)[:, None]
    col = jnp.arange(2 * window)[None, :]
    band = (col >= row) & (col <= row + window)
    place = jnp.arange(tiles)[:, None] * window + jnp.arange(2 * window)[None, :] - half
    inside = (place >= 0) & (place < total)
    return (band[None, :, :] & inside[:, None, :])[:, None, :, :]

def attend_one(triple):
    query, key, value = triple
    length = query.shape[0]
    tiles = length // WINDOW
    half = WINDOW // 2
    scale = HEAD ** (-0.5)
    key_pad = jnp.pad(key, ((half, half), (0, 0), (0, 0)))
    value_pad = jnp.pad(value, ((half, half), (0, 0), (0, 0)))
    key_blocks = key_pad.reshape(tiles + 1, WINDOW, HEADS, HEAD)
    value_blocks = value_pad.reshape(tiles + 1, WINDOW, HEADS, HEAD)
    key_tiles = jnp.concatenate([key_blocks[:-1], key_blocks[1:]], axis=1)
    value_tiles = jnp.concatenate([value_blocks[:-1], value_blocks[1:]], axis=1)
    query_tiles = query.reshape(tiles, WINDOW, HEADS, HEAD)
    raw = jnp.einsum('tqhe,tkhe->thqk', query_tiles, key_tiles, precision=lax.Precision.HIGHEST)
    scores = low_back(raw * scale)
    mask = window_mask(length, tiles, WINDOW)
    scores = jnp.where(mask, scores, -1e+30)
    prob = low(jax.nn.softmax(scores, axis=-1))
    out = jnp.einsum('thqk,tkhe->tqhe', prob, value_tiles, precision=lax.Precision.HIGHEST)
    return out.reshape(length, HEADS * HEAD)

def forward(tokens, qkv_master, proj_master, wide_master, down_master, norm_gains):
    gains = low(norm_gains)
    sequences, length, width = tokens.shape
    normed = low(layer_norm(tokens, gains[0]))
    query_key_value = low_back(project(normed, low(qkv_master)))
    query = query_key_value[..., :width].reshape(sequences, length, HEADS, HEAD)
    key = query_key_value[..., width:2 * width].reshape(sequences, length, HEADS, HEAD)
    value = query_key_value[..., 2 * width:].reshape(sequences, length, HEADS, HEAD)
    cosine, sine = rope_tables(jnp.arange(length, dtype=jnp.int32), HEAD)
    query = low(rotary(query, cosine, sine))
    key = low(rotary(key, cosine, sine))
    value = low(value)
    attended = lax.map(jax.checkpoint(attend_one), (query, key, value))
    attended = low_back(low(attended))
    hidden_state_rows = tokens + low_back(project(attended, low(proj_master)))
    normed2 = low(layer_norm(hidden_state_rows, gains[1]))
    joined_sides = low_back(project(normed2, low(wide_master)))
    inner = low(jax.nn.gelu(joined_sides[..., :FF], approximate=False) * joined_sides[..., FF:])
    return hidden_state_rows + low_back(project(inner, low(down_master)))

def adamw(master, grad, first, second, rate):
    moment = 0.9 * first + 0.1 * grad
    square = 0.98 * second + 0.02 * grad * grad
    fixed_first = moment / (1.0 - 0.9 ** STEP)
    fixed_second = square / (1.0 - 0.98 ** STEP)
    update = fixed_first / (jnp.sqrt(fixed_second) + 1e-06) + 1e-05 * master
    return (master - rate * update, moment, square)

def reference(tokens, cotangent, qkv_master, proj_master, wide_master, down_master, norm_gains, qkv_first, proj_first, wide_first, down_first, gains_first, qkv_second, proj_second, wide_second, down_second, gains_second):
    layer_output, pullback = jax.vjp(forward, tokens, qkv_master, proj_master, wide_master, down_master, norm_gains)
    grads = pullback(cotangent)
    input_grad = grads[0]
    rates = (2.0 * D ** (-0.5), 2.0 * max(D // WINDOW, 1) ** (-0.5), 2.0 * D ** (-0.5), 2.0 * FF ** (-0.5), 1.0)
    masters = (qkv_master, proj_master, wide_master, down_master, norm_gains)
    firsts = (qkv_first, proj_first, wide_first, down_first, gains_first)
    seconds = (qkv_second, proj_second, wide_second, down_second, gains_second)
    results = [adamw(masters[i], grads[i + 1], firsts[i], seconds[i], rates[i]) for i in range(5)]
    return (layer_output, input_grad, results[0][0], results[1][0], results[2][0], results[3][0], results[4][0], results[0][1], results[1][1], results[2][1], results[3][1], results[4][1], results[0][2], results[1][2], results[2][2], results[3][2], results[4][2])
```

```python
import jax
import jax.numpy as jnp
from jax import lax
from jax.sharding import PartitionSpec as P

D = 768
HEADS = 12
HEAD = 64
FF = 1152
WINDOW = 128
STEP = 10


def extended(cells, sides, width):
    for axis, dim in sides:
        count = lax.axis_size(axis)
        ends = count - 1
        head = lax.slice_in_dim(cells, 0, width, axis=dim)
        tail = lax.slice_in_dim(cells, cells.shape[dim] - width, cells.shape[dim], axis=dim)
        cells = jnp.concatenate(
            [
                lax.ppermute(tail, axis, [(i, (i + 1) % count) for i in range(ends)]),
                cells,
                lax.ppermute(head, axis, [((i + 1) % count, i) for i in range(ends)]),
            ],
            axis=dim,
        )
    return cells


def passed_along(value, axis, steps):
    count = lax.axis_size(axis)
    first, last = (max(0, -steps), min(count, count - steps))
    return lax.ppermute(value, axis, [(source, source + steps) for source in range(first, last)])


def layer_norm(value, gain):
    centred = value - jnp.mean(value, axis=-1, keepdims=True)
    inverse = lax.rsqrt(jnp.mean(centred * centred, axis=-1, keepdims=True) + 1e-05)
    return centred * inverse * gain


def geglu(gate, upward):
    return jax.nn.gelu(gate, approximate=False) * upward


def rope_tables(positions, head):
    freqs = 10000.0 ** (-jnp.arange(0, head, 2).astype(jnp.float32) / head)
    angles = positions.astype(jnp.float32)[:, None] * freqs[None, :]
    angles = jnp.concatenate([angles, angles], axis=-1)[:, None, :]
    return (jnp.cos(angles), jnp.sin(angles))


def rotary(value, cosine, sine):
    half = value.shape[-1] // 2
    turned = jnp.concatenate([-value[..., half:], value[..., :half]], axis=-1)
    return value * cosine + turned * sine


def rotary_back(grad, cosine, sine):
    half = grad.shape[-1] // 2
    turned = grad * sine
    return grad * cosine + jnp.concatenate([turned[..., half:], -turned[..., :half]], axis=-1)


def window_mask(base, total, tiles, window):
    half = window // 2
    row = jnp.arange(window)[:, None]
    col = jnp.arange(2 * window)[None, :]
    band = (col >= row) & (col <= row + window)
    place = base + jnp.arange(tiles)[:, None] * window + jnp.arange(2 * window)[None, :] - half
    inside = (place >= 0) & (place < total)
    return (band[None, :, :] & inside[:, None, :])[None, :, None, :, :]


def key_tiles(padded, tiles, window):
    blocks = padded.reshape(padded.shape[0], tiles + 1, window, padded.shape[-1])
    return jnp.concatenate([blocks[:, :-1], blocks[:, 1:]], axis=2)


def swapped(value, axis, bit):
    count = lax.axis_size(axis)
    return lax.ppermute(value, axis, [(i, i ^ bit) for i in range(count)])


def rounded(value):
    return lax.optimization_barrier(value.astype(jnp.bfloat16))


def added(one, other):
    return rounded(one.astype(jnp.float32) + other.astype(jnp.float32))


def folded(value, axis, bit, dim):
    side = (lax.axis_index(axis) // bit) % 2
    size = value.shape[dim] // 2
    kept = lax.dynamic_slice_in_dim(value, side * size, size, axis=dim)
    sent = lax.dynamic_slice_in_dim(value, (1 - side) * size, size, axis=dim)
    return added(kept, swapped(sent, axis, bit))


def unfolded(value, axis, bit, dim):
    side = (lax.axis_index(axis) // bit) % 2
    other = swapped(value, axis, bit)
    low = jnp.where(side == 0, value, other)
    high = jnp.where(side == 0, other, value)
    return jnp.concatenate([low, high], axis=dim)


def reduced(grad):
    shards = lax.axis_size("wshard")
    blocks = lax.axis_size("seq")
    value = rounded(grad)
    rows = value.shape[0] // shards
    bits = [1 << i for i in range(shards.bit_length() - 1)]
    value = value.reshape((2,) * len(bits) + (rows, value.shape[1]))
    for place, bit in enumerate(bits):
        value = folded(value, "wshard", bit, len(bits) - 1 - place)
    value = value.reshape(rows, value.shape[-1])
    halvings = [(1, 0), (2, 1)]
    for bit, dim in halvings:
        value = folded(value, "seq", bit, dim)
    bit = 4
    while bit < blocks:
        value = added(value, swapped(value, "seq", bit))
        bit *= 2
    for bit, dim in reversed(halvings):
        value = unfolded(value, "seq", bit, dim)
    return value.astype(jnp.float32)


def adamw(master, grad, first, second, rate):
    moment = 0.9 * first + 0.1 * grad
    square = 0.98 * second + 0.02 * grad * grad
    fixed_first = moment / (1.0 - 0.9**STEP)
    fixed_second = square / (1.0 - 0.98**STEP)
    update = fixed_first / (jnp.sqrt(fixed_second) + 1e-06) + 1e-05 * master
    return (master - rate * update, moment, square)


def on_device(
    tokens,
    cotangent,
    qkv_master,
    proj_master,
    wide_master,
    down_master,
    norm_gains,
    qkv_first,
    proj_first,
    wide_first,
    down_first,
    gains_first,
    qkv_second,
    proj_second,
    wide_second,
    down_second,
    gains_second,
):
    sequences, local_len, width = tokens.shape
    half = WINDOW // 2
    tiles = local_len // WINDOW
    scale = HEAD ** (-0.5)
    half_float_type = jnp.bfloat16
    single_float_type = jnp.float32
    query_key_value_weight, projection_weight, wide_weight, down_weight, gains_low = (
        lax.all_gather(qkv_master.astype(half_float_type), "wshard", axis=0, tiled=True),
        lax.all_gather(proj_master.astype(half_float_type), "wshard", axis=0, tiled=True),
        lax.all_gather(wide_master.astype(half_float_type), "wshard", axis=0, tiled=True),
        lax.all_gather(down_master.astype(half_float_type), "wshard", axis=0, tiled=True),
        lax.all_gather(norm_gains.astype(half_float_type), "wshard", axis=1, tiled=True),
    )
    gains = gains_low.astype(single_float_type)
    base = lax.axis_index("seq") * local_len
    total = local_len * lax.axis_size("seq")
    cosine, sine = rope_tables(base + jnp.arange(local_len, dtype=jnp.int32), HEAD)
    normed, norm_back1 = jax.vjp(layer_norm, tokens, gains[0])
    normed_rows_low = normed.astype(half_float_type)
    query_key_value = jnp.einsum(
        "bnh,hm->bnm",
        normed_rows_low,
        query_key_value_weight,
        preferred_element_type=single_float_type,
    )
    query = query_key_value[..., :width].reshape(sequences, local_len, HEADS, HEAD)
    key = query_key_value[..., width : 2 * width].reshape(sequences, local_len, HEADS, HEAD)
    query_b = rotary(query, cosine, sine).astype(half_float_type)
    key_b = rotary(key, cosine, sine).astype(half_float_type).reshape(sequences, local_len, width)
    value_b = query_key_value[..., 2 * width :].astype(half_float_type)
    keyval = jnp.concatenate([key_b, value_b], axis=-1)
    padded = extended(keyval, (("seq", 1),), half)
    mask = window_mask(base, total, tiles, WINDOW)
    both_keys = key_tiles(padded, tiles, WINDOW)
    keys = both_keys[..., :width].reshape(sequences, tiles, 2 * WINDOW, HEADS, HEAD)
    values = both_keys[..., width:].reshape(sequences, tiles, 2 * WINDOW, HEADS, HEAD)
    query_tiles = query_b.reshape(sequences, tiles, WINDOW, HEADS, HEAD)
    raw = jnp.einsum(
        "snqhe,snkhe->snhqk", query_tiles, keys, preferred_element_type=single_float_type
    )
    masked = jnp.where(mask, raw * scale, -1e30)
    top = jnp.max(masked, axis=-1, keepdims=True)
    log_total = top + jnp.log(jnp.sum(jnp.exp(masked - top), axis=-1, keepdims=True))
    prob = jnp.exp(masked - log_total)
    attended = jnp.einsum(
        "snhqk,snkhe->snqhe",
        prob.astype(half_float_type),
        values,
        preferred_element_type=single_float_type,
    )
    attention_rows_low = attended.reshape(sequences, local_len, width).astype(half_float_type)
    hidden_state_rows = tokens + jnp.einsum(
        "mrw,wc->mrc",
        attention_rows_low,
        projection_weight,
        preferred_element_type=single_float_type,
    )
    normed2, norm_back2 = jax.vjp(layer_norm, hidden_state_rows, gains[1])
    normed_rows_low2 = normed2.astype(half_float_type)
    joined_sides = jnp.einsum(
        "zrm,mu->zru", normed_rows_low2, wide_weight, preferred_element_type=single_float_type
    )
    inner, inner_back = jax.vjp(geglu, joined_sides[..., :FF], joined_sides[..., FF:])
    inner_rows_low = inner.astype(half_float_type)
    layer_output = hidden_state_rows + jnp.einsum(
        "xmb,bi->xmi", inner_rows_low, down_weight, preferred_element_type=single_float_type
    )
    output_gradient_low = cotangent.astype(half_float_type)
    down_weight_gradient = jnp.einsum(
        "wqu,wqk->uk", inner_rows_low, output_gradient_low, preferred_element_type=single_float_type
    )
    inner_gradient = jnp.einsum(
        "eug,hg->euh", output_gradient_low, down_weight, preferred_element_type=single_float_type
    )
    d_gate, d_up = inner_back(inner_gradient)
    joined_sides_gradient = jnp.concatenate([d_gate, d_up], axis=-1).astype(half_float_type)
    wide_weight_gradient = jnp.einsum(
        "itr,ity->ry",
        normed_rows_low2,
        joined_sides_gradient,
        preferred_element_type=single_float_type,
    )
    normed_gradient2 = jnp.einsum(
        "itj,nj->itn", joined_sides_gradient, wide_weight, preferred_element_type=single_float_type
    )
    d_hidden_part, gain_grad2 = norm_back2(normed_gradient2)
    d_hidden = cotangent + d_hidden_part
    attention_gradient = d_hidden.astype(half_float_type)
    projection_weight_gradient = jnp.einsum(
        "bui,buj->ij",
        attention_rows_low,
        attention_gradient,
        preferred_element_type=single_float_type,
    )
    output_gradient = jnp.einsum(
        "qjv,ov->qjo",
        attention_gradient,
        projection_weight,
        preferred_element_type=single_float_type,
    ).astype(half_float_type)
    out_tiles = output_gradient.reshape(sequences, tiles, WINDOW, HEADS, HEAD)
    raw = jnp.einsum(
        "snqhe,snkhe->snhqk", query_tiles, keys, preferred_element_type=single_float_type
    )
    prob = jnp.exp(jnp.where(mask, raw * scale, -1e30) - log_total)
    d_values = jnp.einsum(
        "snhqk,snqhe->snkhe",
        prob.astype(half_float_type),
        out_tiles,
        preferred_element_type=single_float_type,
    )
    d_prob = jnp.einsum(
        "snqhe,snkhe->snhqk", out_tiles, values, preferred_element_type=single_float_type
    )
    delta = jnp.sum(prob * d_prob, axis=-1, keepdims=True)
    d_score = (prob * (d_prob - delta)).astype(half_float_type)
    d_query = (
        jnp.einsum("snhqk,snkhe->snqhe", d_score, keys, preferred_element_type=single_float_type)
        * scale
    )
    d_keys = (
        jnp.einsum(
            "snhqk,snqhe->snkhe", d_score, query_tiles, preferred_element_type=single_float_type
        )
        * scale
    )
    d_tiles = jnp.concatenate(
        [
            d_keys.reshape(sequences, tiles, 2 * WINDOW, width),
            d_values.reshape(sequences, tiles, 2 * WINDOW, width),
        ],
        axis=-1,
    )
    d_padded = jnp.pad(d_tiles[:, :, :WINDOW], ((0, 0), (0, 1), (0, 0), (0, 0))) + jnp.pad(
        d_tiles[:, :, WINDOW:], ((0, 0), (1, 0), (0, 0), (0, 0))
    )
    d_padded = d_padded.reshape(sequences, local_len + WINDOW, 2 * width)
    from_right = passed_along(d_padded[:, :half].astype(jnp.bfloat16), "seq", -1).astype(
        jnp.float32
    )
    from_left = passed_along(d_padded[:, half + local_len :].astype(jnp.bfloat16), "seq", 1).astype(
        jnp.float32
    )
    owned = (
        d_padded[:, half : half + local_len]
        + jnp.pad(from_left, ((0, 0), (0, local_len - half), (0, 0)))
        + jnp.pad(from_right, ((0, 0), (local_len - half, 0), (0, 0)))
    )
    d_key = owned[..., :width].reshape(sequences, local_len, HEADS, HEAD)
    d_query_pre = rotary_back(d_query.reshape(sequences, local_len, HEADS, HEAD), cosine, sine)
    d_key_pre = rotary_back(d_key, cosine, sine)
    query_key_value_gradient = jnp.concatenate(
        [
            d_query_pre.reshape(sequences, local_len, width),
            d_key_pre.reshape(sequences, local_len, width),
            owned[..., width:],
        ],
        axis=-1,
    ).astype(half_float_type)
    query_key_value_weight_gradient = jnp.einsum(
        "qmf,qmv->fv",
        normed_rows_low,
        query_key_value_gradient,
        preferred_element_type=single_float_type,
    )
    normed_gradient = jnp.einsum(
        "awb,kb->awk",
        query_key_value_gradient,
        query_key_value_weight,
        preferred_element_type=single_float_type,
    )
    d_tokens_part, gain_grad1 = norm_back1(normed_gradient)
    input_grad = d_hidden + d_tokens_part
    gains_grad = jnp.stack([gain_grad1, gain_grad2])
    gains_sum = lax.psum(gains_grad, ("seq", "wshard"))
    column = lax.axis_index("wshard") * gains_first.shape[1]
    owned_grads = (
        reduced(query_key_value_weight_gradient),
        reduced(projection_weight_gradient),
        reduced(wide_weight_gradient),
        reduced(down_weight_gradient),
        lax.dynamic_slice_in_dim(gains_sum, column, gains_first.shape[1], axis=1),
    )
    rates = (
        2.0 * D ** (-0.5),
        2.0 * max(D // WINDOW, 1) ** (-0.5),
        2.0 * D ** (-0.5),
        2.0 * FF ** (-0.5),
        1.0,
    )
    masters = (qkv_master, proj_master, wide_master, down_master, norm_gains)
    firsts = (qkv_first, proj_first, wide_first, down_first, gains_first)
    seconds = (qkv_second, proj_second, wide_second, down_second, gains_second)
    results = [adamw(masters[i], owned_grads[i], firsts[i], seconds[i], rates[i]) for i in range(5)]
    return (
        layer_output,
        input_grad,
        results[0][0],
        results[1][0],
        results[2][0],
        results[3][0],
        results[4][0],
        results[0][1],
        results[1][1],
        results[2][1],
        results[3][1],
        results[4][1],
        results[0][2],
        results[1][2],
        results[2][2],
        results[3][2],
        results[4][2],
    )


def solution(mesh):
    placed = (
        P("wshard", "seq", None),
        P("wshard", "seq", None),
        P("wshard", None),
        P("wshard", None),
        P("wshard", None),
        P("wshard", None),
        P(None, "wshard"),
        P("wshard", None),
        P("wshard", None),
        P("wshard", None),
        P("wshard", None),
        P(None, "wshard"),
        P("wshard", None),
        P("wshard", None),
        P("wshard", None),
        P("wshard", None),
        P(None, "wshard"),
    )
    return jax.shard_map(
        on_device,
        mesh=mesh,
        in_specs=placed,
        out_specs=(
            P("wshard", "seq", None),
            P("wshard", "seq", None),
            P("wshard", None),
            P("wshard", None),
            P("wshard", None),
            P("wshard", None),
            P(None, "wshard"),
            P("wshard", None),
            P("wshard", None),
            P("wshard", None),
            P("wshard", None),
            P(None, "wshard"),
            P("wshard", None),
            P("wshard", None),
            P("wshard", None),
            P("wshard", None),
            P(None, "wshard"),
        ),
        check_vma=False,
    )
```

```python
import jax
import jax.numpy as jnp
from jax import lax
from jax.experimental import pallas as pl
from jax.experimental.pallas import tpu as pltpu
from jax.sharding import PartitionSpec as P

D = 768
HEADS = 12
HEAD = 64
FF = 1152
WINDOW = 128
STEP = 10
HALF = WINDOW // 2
SPAN = 2 * WINDOW
LANES = 128
PAIRS = D // LANES
GROUP = 2
LOW = jnp.bfloat16
WIDE = jnp.float32
MIB = 1 << 20


def dot(one, other, dims=((1,), (0,))):
    return lax.dot_general(one, other, (dims, ((), ())), preferred_element_type=WIDE)


def normalised(value):
    centred = value - jnp.mean(value, axis=-1, keepdims=True)
    inverse = lax.rsqrt(jnp.mean(centred * centred, axis=-1, keepdims=True) + 1e-05)
    return centred * inverse, inverse


def normalised_back(d_normed, gain, xhat, inverse):
    d_xhat = d_normed * gain
    mean = jnp.mean(d_xhat, axis=-1, keepdims=True)
    slope = jnp.mean(d_xhat * xhat, axis=-1, keepdims=True)
    return inverse * (d_xhat - mean - xhat * slope)


def lane_of(rows):
    return lax.broadcasted_iota(jnp.int32, (rows, LANES), 1)


def half_swapped(value):
    first = lane_of(value.shape[0]) % HEAD < HEAD // 2
    ahead = pltpu.roll(value, LANES - HEAD // 2, 1)
    behind = pltpu.roll(value, HEAD // 2, 1)
    return jnp.where(first, ahead, behind)


def turned(value, cosine, sine):
    return value * cosine + half_swapped(value) * sine


def turned_back(value, cosine, sine):
    return value * cosine - half_swapped(value) * sine


def by_head(value):
    first = lane_of(value.shape[0]) < HEAD
    zero = jnp.zeros_like(value)
    return jnp.concatenate([jnp.where(first, value, zero), jnp.where(first, zero, value)], axis=0)


def side_by_side(value):
    rows = value.shape[0] // 2
    return jnp.where(lane_of(rows) < HEAD, value[:rows], value[rows:])


def pair(index, start=0):
    return slice(start + index * LANES, start + (index + 1) * LANES)


def project_kernel(tokens, gains, weight, cosine, sine, normed, query, keyval):
    rows = GROUP * WINDOW
    xhat, _ = normalised(tokens[...].reshape(rows, D))
    low = (xhat * gains[0:1, :]).astype(LOW)
    normed[...] = low.reshape(GROUP, WINDOW, D)
    mine = slice(HALF, HALF + WINDOW)
    cos, sin = cosine[mine], sine[mine]
    out = dot(low, weight[:, :D])
    for one in range(GROUP):
        for p in range(PAIRS):
            part = out[one * WINDOW : (one + 1) * WINDOW, pair(p)]
            query[one, :, pair(p)] = (turned(part, cos, sin) * HEAD**-0.5).astype(LOW)
    out = dot(low, weight[:, D : 2 * D])
    for one in range(GROUP):
        for p in range(PAIRS):
            part = out[one * WINDOW : (one + 1) * WINDOW, pair(p)]
            keyval[one, :, pair(p)] = turned(part, cos, sin).astype(LOW)
    out = dot(low, weight[:, 2 * D :])
    keyval[:, :, D:] = out.astype(LOW).reshape(GROUP, WINDOW, D)


def attend_kernel(
    tokens, normed, left, right, gains, query, keyval, weight, proj, cosine, sine, cap,
    normed_ext, keyval_ext, probs, attended, hidden,
):
    gain = gains[0:1, :]
    ends = []
    for one in range(GROUP):
        low_left = (left[one].astype(WIDE) * gain).astype(LOW)
        low_right = (right[one].astype(WIDE) * gain).astype(LOW)
        normed_ext[one, :HALF] = low_left
        normed_ext[one, HALF : HALF + WINDOW] = normed[one]
        normed_ext[one, HALF + WINDOW :] = low_right
        ends += [low_left, low_right]
    ends = jnp.concatenate(ends, axis=0)
    cos = jnp.concatenate([cosine[:HALF], cosine[HALF + WINDOW :]], axis=0)
    sin = jnp.concatenate([sine[:HALF], sine[HALF + WINDOW :]], axis=0)
    keys = dot(ends, weight[:, D : 2 * D])
    values = dot(ends, weight[:, 2 * D :]).astype(LOW)
    for one in range(GROUP):
        keyval_ext[one, HALF : HALF + WINDOW] = keyval[one]
        rows = slice(one * WINDOW, (one + 1) * WINDOW)
        keyval_ext[one, :HALF, D:] = values[rows][:HALF]
        keyval_ext[one, HALF + WINDOW :, D:] = values[rows][HALF:]
        for p in range(PAIRS):
            key = turned(keys[rows, pair(p)], cos, sin).astype(LOW)
            keyval_ext[one, :HALF, pair(p)] = key[:HALF]
            keyval_ext[one, HALF + WINDOW :, pair(p)] = key[HALF:]
    limit = jnp.concatenate([cap[...], cap[...]], axis=0)
    for one in range(GROUP):
        for p in range(PAIRS):
            asked = by_head(query[one, :, pair(p)])
            scores = dot(asked, keyval_ext[one, :, pair(p)], ((1,), (1,)))
            scores = jnp.minimum(scores, limit)
            top = jnp.max(scores, axis=-1, keepdims=True)
            grown = jnp.exp(scores - top)
            prob = grown * (1.0 / jnp.sum(grown, axis=-1, keepdims=True))
            prob = prob.astype(LOW)
            probs[one, p] = prob
            found = dot(prob, keyval_ext[one, :, pair(p, D)])
            attended[one, :, pair(p)] = side_by_side(found).astype(LOW)
    rows = GROUP * WINDOW
    out = dot(attended[...].reshape(rows, D), proj[...])
    hidden[...] = tokens[...] + out.reshape(GROUP, WINDOW, D)


def feed_kernel(
    hidden, cotangent, gains, wide, down, proj,
    layer_output, d_hidden, d_attn, d_out, normed, inner, d_both, low_cotangent, gain_grad,
):
    rows = GROUP * WINDOW
    state = hidden[...].reshape(rows, D)
    gain = gains[1:2, :]
    xhat, inverse = normalised(state)
    low = (xhat * gain).astype(LOW)
    normed[...] = low
    above = cotangent[...].reshape(rows, D)
    dy = above.astype(LOW)
    low_cotangent[...] = dy
    start = 0
    while start < FF:
        size = min(256, FF - start)
        cols = slice(start, start + size)
        other = slice(FF + start, FF + start + size)
        gate = dot(low, wide[:, cols])
        upward = dot(low, wide[:, other])
        d_inner = dot(dy, down[cols, :], ((1,), (1,)))
        area = 0.5 + 0.5 * lax.erf(gate * (0.5**0.5))
        shaped = gate * area
        slope = area + gate * (jnp.exp(-0.5 * gate * gate) * 0.3989422804014327)
        inner[:, cols] = (shaped * upward).astype(LOW)
        d_both[:, cols] = (d_inner * upward * slope).astype(LOW)
        d_both[:, other] = (d_inner * shaped).astype(LOW)
        start += size
    layer_output[...] = (state + dot(inner[...], down[...])).reshape(GROUP, WINDOW, D)
    d_normed = dot(d_both[...], wide[...], ((1,), (1,)))
    part = jnp.sum(d_normed * xhat, axis=0, keepdims=True)

    @pl.when(pl.program_id(0) == 0)
    def _():
        gain_grad[...] = part

    @pl.when(pl.program_id(0) > 0)
    def _():
        gain_grad[...] += part

    back = above + normalised_back(d_normed, gain, xhat, inverse)
    d_hidden[...] = back.reshape(GROUP, WINDOW, D)
    back = back.astype(LOW)
    d_attn[...] = back
    d_out[...] = dot(back, proj[...], ((1,), (1,))).astype(LOW).reshape(GROUP, WINDOW, D)


def attend_back_kernel(
    query, keyval, probs, d_out, weight, cosine, sine,
    d_query, d_keyval, d_normed, d_left, d_right,
):
    mine = slice(HALF, HALF + WINDOW)
    cos, sin = cosine[mine], sine[mine]
    for one in range(GROUP):
        for p in range(PAIRS):
            asked = by_head(query[one, :, pair(p)])
            key = keyval[one, :, pair(p)]
            grad = by_head(d_out[one, :, pair(p)])
            low_prob = probs[one, p]
            prob = low_prob.astype(WIDE)
            d_prob = dot(grad, keyval[one, :, pair(p, D)], ((1,), (1,)))
            delta = jnp.sum(prob * d_prob, axis=-1, keepdims=True)
            d_score = (prob * (d_prob - delta)).astype(LOW)
            d_q = side_by_side(dot(d_score, key)) * HEAD**-0.5
            d_query[one, :, pair(p)] = turned_back(d_q, cos, sin).astype(LOW)
            d_k = dot(d_score, asked, ((0,), (0,)))
            d_keyval[one, :, pair(p)] = turned_back(d_k, cosine[...], sine[...]).astype(LOW)
            d_v = dot(low_prob, grad, ((0,), (0,)))
            d_keyval[one, :, pair(p, D)] = d_v.astype(LOW)
    rows = GROUP * SPAN
    both = dot(d_keyval[...].reshape(rows, 2 * D), weight[:, D:], ((1,), (1,)))
    own = dot(d_query[...].reshape(GROUP * WINDOW, D), weight[:, :D], ((1,), (1,)))
    for one in range(GROUP):
        part = both[one * SPAN : (one + 1) * SPAN]
        d_left[one] = part[:HALF].astype(LOW)
        d_right[one] = part[HALF + WINDOW :].astype(LOW)
        d_normed[one] = part[mine] + own[one * WINDOW : (one + 1) * WINDOW]


def enter_kernel(tokens, gains, d_normed, from_left, from_right, d_hidden, input_grad, gain_grad):
    rows = GROUP * WINDOW
    xhat, inverse = normalised(tokens[...].reshape(rows, D))
    parts = []
    for one in range(GROUP):
        parts += [
            d_normed[one, :HALF] + from_left[one].astype(WIDE),
            d_normed[one, HALF:] + from_right[one].astype(WIDE),
        ]
    grad = jnp.concatenate(parts, axis=0)
    part = jnp.sum(grad * xhat, axis=0, keepdims=True)

    @pl.when(pl.program_id(0) == 0)
    def _():
        gain_grad[...] = part

    @pl.when(pl.program_id(0) > 0)
    def _():
        gain_grad[...] += part

    back = normalised_back(grad, gains[0:1, :], xhat, inverse)
    input_grad[...] = d_hidden[...] + back.reshape(GROUP, WINDOW, D)


def whole(shape):
    return pl.BlockSpec(shape, lambda i: (0,) * len(shape))


def blocked(shape):
    return pl.BlockSpec((GROUP,) + tuple(shape[1:]), lambda i: (i,) + (0,) * (len(shape) - 1))


def rowed(shape):
    return pl.BlockSpec((GROUP * WINDOW,) + tuple(shape[1:]), lambda i: (i, 0))


def called(kernel, sequences, operands, results, flops, limit):
    arrays = [array for array, _ in operands]
    moved = sum(array.size * array.dtype.itemsize for array in arrays)
    moved += sum(
        jax.ShapeDtypeStruct(shape, kind).size * jnp.dtype(kind).itemsize for shape, kind, _ in results
    )
    return pl.pallas_call(
        kernel,
        grid=(sequences // GROUP,),
        in_specs=[spec(array.shape) for array, spec in operands],
        out_specs=[spec(shape) for shape, _, spec in results],
        out_shape=[jax.ShapeDtypeStruct(shape, kind) for shape, kind, _ in results],
        compiler_params=pltpu.CompilerParams(
            dimension_semantics=("arbitrary",), vmem_limit_bytes=limit * MIB
        ),
        cost_estimate=pl.CostEstimate(flops=flops, bytes_accessed=moved, transcendentals=0),
    )(*arrays)


def swapped(value, axis, bit):
    count = lax.axis_size(axis)
    return lax.ppermute(value, axis, [(i, i ^ bit) for i in range(count)])


def rounded(value):
    return lax.optimization_barrier(value.astype(jnp.bfloat16))


def added(one, other):
    return rounded(one.astype(jnp.float32) + other.astype(jnp.float32))


def folded(value, axis, bit, dim):
    side = (lax.axis_index(axis) // bit) % 2
    size = value.shape[dim] // 2
    kept = lax.dynamic_slice_in_dim(value, side * size, size, axis=dim)
    sent = lax.dynamic_slice_in_dim(value, (1 - side) * size, size, axis=dim)
    return added(kept, swapped(sent, axis, bit))


def unfolded(value, axis, bit, dim):
    side = (lax.axis_index(axis) // bit) % 2
    other = swapped(value, axis, bit)
    low = jnp.where(side == 0, value, other)
    high = jnp.where(side == 0, other, value)
    return jnp.concatenate([low, high], axis=dim)


def reduced(grad):
    shards = lax.axis_size("wshard")
    blocks = lax.axis_size("seq")
    value = rounded(grad)
    rows = value.shape[0] // shards
    bits = [1 << i for i in range(shards.bit_length() - 1)]
    value = value.reshape((2,) * len(bits) + (rows, value.shape[1]))
    for place, bit in enumerate(bits):
        value = folded(value, "wshard", bit, len(bits) - 1 - place)
    value = value.reshape(rows, value.shape[-1])
    halvings = [(1, 0), (2, 1)]
    for bit, dim in halvings:
        value = folded(value, "seq", bit, dim)
    bit = 4
    while bit < blocks:
        value = added(value, swapped(value, "seq", bit))
        bit *= 2
    for bit, dim in reversed(halvings):
        value = unfolded(value, "seq", bit, dim)
    return value.astype(jnp.float32)


def adamw(master, grad, first, second, rate):
    moment = 0.9 * first + 0.1 * grad
    square = 0.98 * second + 0.02 * grad * grad
    fixed_first = moment / (1.0 - 0.9**STEP)
    fixed_second = square / (1.0 - 0.98**STEP)
    update = fixed_first / (jnp.sqrt(fixed_second) + 1e-06) + 1e-05 * master
    return (master - rate * update, moment, square)


def gathered(shard, axis=0):
    shards = lax.axis_size("wshard")
    place = lax.axis_index("wshard")
    size = shard.shape[axis]
    shape = list(shard.shape)
    shape[axis] = size * shards
    pieces = {0: shard}
    bit = shards // 2
    while bit:
        for known in list(pieces):
            pieces[known | bit] = swapped(pieces[known], "wshard", bit)
        bit //= 2
    total = jnp.zeros(shape, shard.dtype)
    for known, piece in pieces.items():
        total = lax.dynamic_update_slice_in_dim(total, piece, (place ^ known) * size, axis)
    return total


def behind(value, other):
    return lax.optimization_barrier((value, other))


def summed_everywhere(rows):
    shards = lax.axis_size("wshard")
    size = rows.shape[1] // shards
    bit = 1
    while bit < shards:
        rows = rows + swapped(rows, "wshard", bit)
        bit *= 2
    rows = lax.dynamic_slice_in_dim(rows, lax.axis_index("wshard") * size, size, axis=1)
    bit = 1
    while bit < lax.axis_size("seq"):
        rows = rows + swapped(rows, "seq", bit)
        bit *= 2
    return rows


def tables(base, total):
    places = base - HALF + jnp.arange(SPAN, dtype=jnp.int32)
    freqs = 10000.0 ** (-jnp.arange(0, HEAD, 2).astype(WIDE) / HEAD)
    angles = places.astype(WIDE)[:, None] * freqs[None, :]
    cosine, sine = jnp.cos(angles), jnp.sin(angles)
    cosine = jnp.concatenate([cosine] * 4, axis=1)
    sine = jnp.concatenate([-sine, sine] * 2, axis=1)
    row = jnp.arange(WINDOW)[:, None]
    col = jnp.arange(SPAN)[None, :]
    seen = (col >= row) & (col <= row + WINDOW) & (places >= 0)[None, :] & (places < total)[None, :]
    return cosine, sine, jnp.where(seen, 3e38, -1e30).astype(WIDE)


def on_device(
    tokens,
    cotangent,
    qkv_master,
    proj_master,
    wide_master,
    down_master,
    norm_gains,
    qkv_first,
    proj_first,
    wide_first,
    down_first,
    gains_first,
    qkv_second,
    proj_second,
    wide_second,
    down_second,
    gains_second,
):
    sequences, local_len, width = tokens.shape
    blocks = lax.axis_size("seq")
    base = lax.axis_index("seq") * local_len
    to_right = [(i, i + 1) for i in range(blocks - 1)]
    to_left = [(i + 1, i) for i in range(blocks - 1)]

    low_qkv = qkv_master.astype(LOW)
    ends = normalised(tokens)[0].astype(LOW)
    left = lax.ppermute(ends[:, local_len - HALF :], "seq", to_right)
    right = lax.ppermute(ends[:, :HALF], "seq", to_left)
    gains = gathered(norm_gains.astype(LOW), axis=1).astype(WIDE)
    qkv = gathered(low_qkv)
    proj = gathered(proj_master.astype(LOW))
    wide = gathered(wide_master.astype(LOW))
    down = gathered(down_master.astype(LOW))
    cosine, sine, cap = tables(base, local_len * blocks)

    cells = sequences * local_len
    spread = (sequences, local_len, D)
    halo = (sequences, HALF, D)
    normed, query, keyval = called(
        project_kernel,
        sequences,
        [(tokens, blocked), (gains, whole), (qkv, whole), (cosine, whole), (sine, whole)],
        [(spread, LOW, blocked), (spread, LOW, blocked), ((sequences, local_len, 2 * D), LOW, blocked)],
        2 * cells * D * 3 * D,
        40,
    )
    normed_ext, keyval_ext, probs, attended, hidden = called(
        attend_kernel,
        sequences,
        [
            (tokens, blocked), (normed, blocked), (left, blocked), (right, blocked), (gains, whole),
            (query, blocked), (keyval, blocked), (qkv, whole), (proj, whole),
            (cosine, whole), (sine, whole), (cap, whole),
        ],
        [
            ((sequences, SPAN, D), LOW, blocked),
            ((sequences, SPAN, 2 * D), LOW, blocked),
            ((sequences, PAIRS, SPAN, SPAN), LOW, blocked),
            (spread, LOW, blocked),
            (spread, WIDE, blocked),
        ],
        2 * cells * D * 3 * D + 8 * cells * SPAN * D,
        48,
    )
    layer_output, d_hidden, d_attn, d_out, normed2, inner, d_both, dy, gain_grad2 = called(
        feed_kernel,
        sequences,
        [
            (hidden, blocked), (cotangent, blocked), (gains, whole),
            (wide, whole), (down, whole), (proj, whole),
        ],
        [
            (spread, WIDE, blocked),
            (spread, WIDE, blocked),
            ((cells, D), LOW, rowed),
            (spread, LOW, blocked),
            ((cells, D), LOW, rowed),
            ((cells, FF), LOW, rowed),
            ((cells, 2 * FF), LOW, rowed),
            ((cells, D), LOW, rowed),
            ((1, D), WIDE, whole),
        ],
        2 * cells * D * 7 * FF,
        56,
    )
    first_rows = ((0,), (0,))
    wide_grad = dot(normed2, d_both, first_rows)
    down_grad = dot(inner, dy, first_rows)
    proj_grad = dot(attended.reshape(cells, D), d_attn, first_rows)
    d_query, d_keyval, d_normed, d_left, d_right = called(
        attend_back_kernel,
        sequences,
        [
            (query, blocked), (keyval_ext, blocked), (probs, blocked), (d_out, blocked),
            (qkv, whole), (cosine, whole), (sine, whole),
        ],
        [
            (spread, LOW, blocked),
            ((sequences, SPAN, 2 * D), LOW, blocked),
            (spread, WIDE, blocked),
            (halo, LOW, blocked),
            (halo, LOW, blocked),
        ],
        2 * cells * D * 5 * D + 16 * cells * SPAN * D,
        48,
    )
    query_grad = dot(normed.reshape(cells, D), d_query.reshape(cells, D), first_rows)
    keyval_grad = dot(
        normed_ext.reshape(2 * cells, D), d_keyval.reshape(2 * cells, 2 * D), first_rows
    )
    from_left = lax.ppermute(d_right, "seq", to_right)
    from_right = lax.ppermute(d_left, "seq", to_left)
    input_grad, gain_grad1 = called(
        enter_kernel,
        sequences,
        [
            (tokens, blocked), (gains, whole), (d_normed, blocked),
            (from_left, blocked), (from_right, blocked), (d_hidden, blocked),
        ],
        [(spread, WIDE, blocked), ((1, D), WIDE, whole)],
        20 * cells * D,
        32,
    )
    gains_grad = jnp.concatenate([gain_grad1, gain_grad2], axis=0)
    owned_grads = (
        jnp.concatenate([reduced(query_grad), reduced(keyval_grad)], axis=1),
        reduced(proj_grad),
        reduced(wide_grad),
        reduced(down_grad),
        summed_everywhere(gains_grad),
    )
    rates = (
        2.0 * D ** (-0.5),
        2.0 * max(D // WINDOW, 1) ** (-0.5),
        2.0 * D ** (-0.5),
        2.0 * FF ** (-0.5),
        1.0,
    )
    masters = (qkv_master, proj_master, wide_master, down_master, norm_gains)
    firsts = (qkv_first, proj_first, wide_first, down_first, gains_first)
    seconds = (qkv_second, proj_second, wide_second, down_second, gains_second)
    results = [adamw(masters[i], owned_grads[i], firsts[i], seconds[i], rates[i]) for i in range(5)]
    return (
        layer_output,
        input_grad,
        results[0][0],
        results[1][0],
        results[2][0],
        results[3][0],
        results[4][0],
        results[0][1],
        results[1][1],
        results[2][1],
        results[3][1],
        results[4][1],
        results[0][2],
        results[1][2],
        results[2][2],
        results[3][2],
        results[4][2],
    )


def solution(mesh):
    placed = (
        P("wshard", "seq", None),
        P("wshard", "seq", None),
        P("wshard", None),
        P("wshard", None),
        P("wshard", None),
        P("wshard", None),
        P(None, "wshard"),
        P("wshard", None),
        P("wshard", None),
        P("wshard", None),
        P("wshard", None),
        P(None, "wshard"),
        P("wshard", None),
        P("wshard", None),
        P("wshard", None),
        P("wshard", None),
        P(None, "wshard"),
    )
    return jax.shard_map(
        on_device,
        mesh=mesh,
        in_specs=placed,
        out_specs=(
            P("wshard", "seq", None),
            P("wshard", "seq", None),
            P("wshard", None),
            P("wshard", None),
            P("wshard", None),
            P("wshard", None),
            P(None, "wshard"),
            P("wshard", None),
            P("wshard", None),
            P("wshard", None),
            P("wshard", None),
            P(None, "wshard"),
            P("wshard", None),
            P("wshard", None),
            P("wshard", None),
            P("wshard", None),
            P(None, "wshard"),
        ),
        check_vma=False,
    )
```

```python
import jax
import jax.numpy as jnp
from jax import lax
from jax.experimental import pallas as pl
from jax.experimental.pallas import tpu as pltpu
from jax.sharding import PartitionSpec as P

D = 768
HEADS = 12
HEAD = 64
FF = 1152
WINDOW = 128
STEP = 10
HALF = WINDOW // 2
SPAN = 2 * WINDOW
LANES = 128
PAIRS = D // LANES
GROUP = 2
LOW = jnp.bfloat16
WIDE = jnp.float32
MIB = 1 << 20


def dot(one, other, dims=((1,), (0,))):
    return lax.dot_general(one, other, (dims, ((), ())), preferred_element_type=WIDE)


def normalised(value):
    centred = value - jnp.mean(value, axis=-1, keepdims=True)
    inverse = lax.rsqrt(jnp.mean(centred * centred, axis=-1, keepdims=True) + 1e-05)
    return centred * inverse, inverse


def normalised_back(d_normed, gain, xhat, inverse):
    d_xhat = d_normed * gain
    mean = jnp.mean(d_xhat, axis=-1, keepdims=True)
    slope = jnp.mean(d_xhat * xhat, axis=-1, keepdims=True)
    return inverse * (d_xhat - mean - xhat * slope)


def lane_of(rows):
    return lax.broadcasted_iota(jnp.int32, (rows, LANES), 1)


def half_swapped(value):
    first = lane_of(value.shape[0]) % HEAD < HEAD // 2
    ahead = pltpu.roll(value, LANES - HEAD // 2, 1)
    behind = pltpu.roll(value, HEAD // 2, 1)
    return jnp.where(first, ahead, behind)


def turned(value, cosine, sine):
    return value * cosine + half_swapped(value) * sine


def turned_back(value, cosine, sine):
    return value * cosine - half_swapped(value) * sine


def by_head(value):
    first = lane_of(value.shape[0]) < HEAD
    zero = jnp.zeros_like(value)
    return jnp.concatenate([jnp.where(first, value, zero), jnp.where(first, zero, value)], axis=0)


def side_by_side(value):
    rows = value.shape[0] // 2
    return jnp.where(lane_of(rows) < HEAD, value[:rows], value[rows:])


def pair(index, start=0):
    return slice(start + index * LANES, start + (index + 1) * LANES)


def project_kernel(tokens, gains, weight, cosine, sine, normed, query, keyval):
    rows = GROUP * WINDOW
    xhat, _ = normalised(tokens[...].reshape(rows, D))
    low = (xhat * gains[0:1, :]).astype(LOW)
    normed[...] = low.reshape(GROUP, WINDOW, D)
    mine = slice(HALF, HALF + WINDOW)
    cos, sin = cosine[mine], sine[mine]
    out = dot(low, weight[:, :D])
    for one in range(GROUP):
        for p in range(PAIRS):
            part = out[one * WINDOW : (one + 1) * WINDOW, pair(p)]
            query[one, :, pair(p)] = (turned(part, cos, sin) * HEAD**-0.5).astype(LOW)
    out = dot(low, weight[:, D : 2 * D])
    for one in range(GROUP):
        for p in range(PAIRS):
            part = out[one * WINDOW : (one + 1) * WINDOW, pair(p)]
            keyval[one, :, pair(p)] = turned(part, cos, sin).astype(LOW)
    out = dot(low, weight[:, 2 * D :])
    keyval[:, :, D:] = out.astype(LOW).reshape(GROUP, WINDOW, D)


def attend_kernel(
    tokens, normed, left, right, gains, query, keyval, weight, proj, cosine, sine, cap,
    normed_ext, keyval_ext, probs, attended, hidden,
):
    gain = gains[0:1, :]
    ends = []
    for one in range(GROUP):
        low_left = (left[one].astype(WIDE) * gain).astype(LOW)
        low_right = (right[one].astype(WIDE) * gain).astype(LOW)
        normed_ext[one, :HALF] = low_left
        normed_ext[one, HALF : HALF + WINDOW] = normed[one]
        normed_ext[one, HALF + WINDOW :] = low_right
        ends += [low_left, low_right]
    ends = jnp.concatenate(ends, axis=0)
    cos = jnp.concatenate([cosine[:HALF], cosine[HALF + WINDOW :]], axis=0)
    sin = jnp.concatenate([sine[:HALF], sine[HALF + WINDOW :]], axis=0)
    keys = dot(ends, weight[:, D : 2 * D])
    values = dot(ends, weight[:, 2 * D :]).astype(LOW)
    for one in range(GROUP):
        keyval_ext[one, HALF : HALF + WINDOW] = keyval[one]
        rows = slice(one * WINDOW, (one + 1) * WINDOW)
        keyval_ext[one, :HALF, D:] = values[rows][:HALF]
        keyval_ext[one, HALF + WINDOW :, D:] = values[rows][HALF:]
        for p in range(PAIRS):
            key = turned(keys[rows, pair(p)], cos, sin).astype(LOW)
            keyval_ext[one, :HALF, pair(p)] = key[:HALF]
            keyval_ext[one, HALF + WINDOW :, pair(p)] = key[HALF:]
    limit = jnp.concatenate([cap[...], cap[...]], axis=0)
    for one in range(GROUP):
        for p in range(PAIRS):
            asked = by_head(query[one, :, pair(p)])
            scores = dot(asked, keyval_ext[one, :, pair(p)], ((1,), (1,)))
            scores = jnp.minimum(scores, limit)
            top = jnp.max(scores, axis=-1, keepdims=True)
            grown = jnp.exp(scores - top)
            prob = grown * (1.0 / jnp.sum(grown, axis=-1, keepdims=True))
            prob = prob.astype(LOW)
            probs[one, p] = prob
            found = dot(prob, keyval_ext[one, :, pair(p, D)])
            attended[one, :, pair(p)] = side_by_side(found).astype(LOW)
    rows = GROUP * WINDOW
    out = dot(attended[...].reshape(rows, D), proj[...])
    hidden[...] = tokens[...] + out.reshape(GROUP, WINDOW, D)


def feed_kernel(
    hidden, cotangent, gains, wide, down, proj,
    layer_output, d_hidden, d_attn, d_out, normed, inner, d_both, low_cotangent, gain_grad,
):
    rows = GROUP * WINDOW
    state = hidden[...].reshape(rows, D)
    gain = gains[1:2, :]
    xhat, inverse = normalised(state)
    low = (xhat * gain).astype(LOW)
    normed[...] = low
    above = cotangent[...].reshape(rows, D)
    dy = above.astype(LOW)
    low_cotangent[...] = dy
    start = 0
    while start < FF:
        size = min(256, FF - start)
        cols = slice(start, start + size)
        other = slice(FF + start, FF + start + size)
        gate = dot(low, wide[:, cols])
        upward = dot(low, wide[:, other])
        d_inner = dot(dy, down[cols, :], ((1,), (1,)))
        area = 0.5 + 0.5 * lax.erf(gate * (0.5**0.5))
        shaped = gate * area
        slope = area + gate * (jnp.exp(-0.5 * gate * gate) * 0.3989422804014327)
        inner[:, cols] = (shaped * upward).astype(LOW)
        d_both[:, cols] = (d_inner * upward * slope).astype(LOW)
        d_both[:, other] = (d_inner * shaped).astype(LOW)
        start += size
    layer_output[...] = (state + dot(inner[...], down[...])).reshape(GROUP, WINDOW, D)
    d_normed = dot(d_both[...], wide[...], ((1,), (1,)))
    part = jnp.sum(d_normed * xhat, axis=0, keepdims=True)

    @pl.when(pl.program_id(0) == 0)
    def _():
        gain_grad[...] = part

    @pl.when(pl.program_id(0) > 0)
    def _():
        gain_grad[...] += part

    back = above + normalised_back(d_normed, gain, xhat, inverse)
    d_hidden[...] = back.reshape(GROUP, WINDOW, D)
    back = back.astype(LOW)
    d_attn[...] = back
    d_out[...] = dot(back, proj[...], ((1,), (1,))).astype(LOW).reshape(GROUP, WINDOW, D)


def scores_back(query, keys, values, probs, d_out, cosine, sine, d_query, d_keys, d_values, count):
    mine = slice(HALF, HALF + WINDOW)
    cos, sin = cosine[mine], sine[mine]
    for one in range(GROUP):
        for p in range(count):
            asked = by_head(query[one, :, pair(p)])
            key = keys[one, :, pair(p)]
            grad = by_head(d_out[one, :, pair(p)])
            low_prob = probs[one, p]
            prob = low_prob.astype(WIDE)
            d_prob = dot(grad, values[one, :, pair(p)], ((1,), (1,)))
            delta = jnp.sum(prob * d_prob, axis=-1, keepdims=True)
            d_score = (prob * (d_prob - delta)).astype(LOW)
            d_q = side_by_side(dot(d_score, key)) * HEAD**-0.5
            d_query[one, :, pair(p)] = turned_back(d_q, cos, sin).astype(LOW)
            d_k = dot(d_score, asked, ((0,), (0,)))
            d_keys[one, :, pair(p)] = turned_back(d_k, cosine[...], sine[...]).astype(LOW)
            d_v = dot(low_prob, grad, ((0,), (0,)))
            d_values[one, :, pair(p)] = d_v.astype(LOW)


def first_back_kernel(query, keys, values, probs, d_out, cosine, sine, d_query, d_keys, d_values):
    scores_back(
        query, keys, values, probs, d_out, cosine, sine, d_query, d_keys, d_values, PAIRS // 2
    )


def second_back_kernel(
    query, keys, values, probs, d_out, cosine, sine, first_query, first_keys, first_values, weight, normed_ext,
    d_query, d_keys, d_values, d_left, d_right, d_normed, gain_grad, all_query, all_keyval,
):
    scores_back(
        query, keys, values, probs, d_out, cosine, sine, d_query, d_keys, d_values, PAIRS // 2
    )
    half = D // 2
    for one in range(GROUP):
        rows = slice(one * WINDOW, (one + 1) * WINDOW)
        all_query[rows, :half] = first_query[one]
        all_query[rows, half:] = d_query[one]
        rows = slice(one * SPAN, (one + 1) * SPAN)
        all_keyval[rows, :half] = first_keys[one]
        all_keyval[rows, half:D] = d_keys[one]
        all_keyval[rows, D : D + half] = first_values[one]
        all_keyval[rows, D + half :] = d_values[one]
    both = dot(all_keyval[...], weight[:, D:], ((1,), (1,)))
    own = dot(all_query[...], weight[:, :D], ((1,), (1,)))
    total = jnp.zeros((1, D), WIDE)
    for one in range(GROUP):
        part = both[one * SPAN : (one + 1) * SPAN]
        mine = own[one * WINDOW : (one + 1) * WINDOW]
        rows = normed_ext[one].astype(WIDE)
        total += jnp.sum(part * rows, axis=0, keepdims=True)
        total += jnp.sum(mine * rows[HALF : HALF + WINDOW], axis=0, keepdims=True)
        d_left[one] = part[:HALF].astype(LOW)
        d_right[one] = part[HALF + WINDOW :].astype(LOW)
        d_normed[one] = part[HALF : HALF + WINDOW] + mine

    @pl.when(pl.program_id(0) == 0)
    def _():
        gain_grad[...] = total

    @pl.when(pl.program_id(0) > 0)
    def _():
        gain_grad[...] += total


def enter_kernel(tokens, gains, d_normed, from_left, from_right, d_hidden, input_grad):
    rows = GROUP * WINDOW
    xhat, inverse = normalised(tokens[...].reshape(rows, D))
    parts = []
    for one in range(GROUP):
        parts += [
            d_normed[one, :HALF] + from_left[one].astype(WIDE),
            d_normed[one, HALF:] + from_right[one].astype(WIDE),
        ]
    back = normalised_back(jnp.concatenate(parts, axis=0), gains[0:1, :], xhat, inverse)
    input_grad[...] = d_hidden[...] + back.reshape(GROUP, WINDOW, D)


def whole(shape):
    return pl.BlockSpec(shape, lambda i: (0,) * len(shape))


def blocked(shape):
    return pl.BlockSpec((GROUP,) + tuple(shape[1:]), lambda i: (i,) + (0,) * (len(shape) - 1))


def part_of(place):
    return lambda shape: pl.BlockSpec(
        (GROUP, shape[1], D // 2), lambda i: (i, 0, place)
    )


def pairs_of(place):
    return lambda shape: pl.BlockSpec(
        (GROUP, PAIRS // 2) + tuple(shape[2:]), lambda i: (i, place, 0, 0)
    )


def rowed(shape):
    return pl.BlockSpec((GROUP * WINDOW,) + tuple(shape[1:]), lambda i: (i, 0))


def called(kernel, sequences, operands, results, limit, scratch=()):
    arrays = [array for array, _ in operands]
    return pl.pallas_call(
        kernel,
        grid=(sequences // GROUP,),
        in_specs=[spec(array.shape) for array, spec in operands],
        out_specs=[spec(shape) for shape, _, spec in results],
        out_shape=[jax.ShapeDtypeStruct(shape, kind) for shape, kind, _ in results],
        scratch_shapes=list(scratch),
        compiler_params=pltpu.CompilerParams(
            dimension_semantics=("arbitrary",), vmem_limit_bytes=limit * MIB
        ),
        cost_estimate=pl.CostEstimate(flops=1000, bytes_accessed=1000, transcendentals=0),
    )(*arrays)


def swapped(value, axis, bit):
    count = lax.axis_size(axis)
    return lax.ppermute(value, axis, [(i, i ^ bit) for i in range(count)])


def exchanged(steps, carried=(), beside=None):
    kept, sent = [], []
    for how, value, axis, bit, dim in steps:
        if how == "fold":
            side = (lax.axis_index(axis) // bit) % 2
            size = value.shape[dim] // 2
            kept.append(lax.dynamic_slice_in_dim(value, side * size, size, axis=dim))
            value = lax.dynamic_slice_in_dim(value, (1 - side) * size, size, axis=dim)
        else:
            kept.append(None)
        sent.append(value)
    held = lax.optimization_barrier(tuple(sent) + tuple(carried))
    sent, carried = held[: len(sent)], held[len(sent) :]
    got = []
    for (how, _, axis, bit, _), value in zip(steps, sent):
        got.append(lax.ppermute(value, axis, bit) if how == "send" else swapped(value, axis, bit))
    if beside is not None:
        carried = beside(*carried)
    held = lax.optimization_barrier(tuple(got) + tuple(carried))
    got, carried = held[: len(got)], held[len(got) :]
    results = []
    for (how, _, axis, bit, dim), mine, own, other in zip(steps, kept, sent, got):
        if how == "fold":
            other = (mine.astype(WIDE) + other.astype(WIDE)).astype(LOW)
        elif how == "full":
            other = (own.astype(WIDE) + other.astype(WIDE)).astype(LOW)
        elif how == "join":
            side = (lax.axis_index(axis) // bit) % 2
            low = jnp.where(side == 0, own, other)
            high = jnp.where(side == 0, other, own)
            other = jnp.concatenate([low, high], axis=dim)
        results.append(other)
    return results, carried


def far_sum(value):
    bit = 8
    while bit < lax.axis_size("seq"):
        ((value,), _) = exchanged([("full", value, "seq", bit, 0)])
        bit *= 2
    return value


def adamw(master, grad, first, second, rate):
    moment = 0.9 * first + 0.1 * grad
    square = 0.98 * second + 0.02 * grad * grad
    fixed_first = moment / (1.0 - 0.9**STEP)
    fixed_second = square / (1.0 - 0.98**STEP)
    update = fixed_first / (jnp.sqrt(fixed_second) + 1e-06) + 1e-05 * master
    return (master - rate * update, moment, square)


def in_order(pieces):
    place = lax.axis_index("wshard")
    size = pieces[0].shape[0]
    total = jnp.zeros((size * len(pieces),) + pieces[0].shape[1:], pieces[0].dtype)
    for known, piece in enumerate(pieces):
        total = lax.dynamic_update_slice_in_dim(total, piece, (place ^ known) * size, 0)
    return total


def tables(base, total):
    places = base - HALF + jnp.arange(SPAN, dtype=jnp.int32)
    freqs = 10000.0 ** (-jnp.arange(0, HEAD, 2).astype(WIDE) / HEAD)
    angles = places.astype(WIDE)[:, None] * freqs[None, :]
    cosine, sine = jnp.cos(angles), jnp.sin(angles)
    cosine = jnp.concatenate([cosine] * 4, axis=1)
    sine = jnp.concatenate([-sine, sine] * 2, axis=1)
    row = jnp.arange(WINDOW)[:, None]
    col = jnp.arange(SPAN)[None, :]
    seen = (col >= row) & (col <= row + WINDOW) & (places >= 0)[None, :] & (places < total)[None, :]
    return cosine, sine, jnp.where(seen, 3e38, -1e30).astype(WIDE)


def on_device(
    tokens,
    cotangent,
    qkv_master,
    proj_master,
    wide_master,
    down_master,
    norm_gains,
    qkv_first,
    proj_first,
    wide_first,
    down_first,
    gains_first,
    qkv_second,
    proj_second,
    wide_second,
    down_second,
    gains_second,
):
    sequences, local_len, width = tokens.shape
    blocks = lax.axis_size("seq")
    base = lax.axis_index("seq") * local_len
    to_right = [(i, i + 1) for i in range(blocks - 1)]
    to_left = [(i + 1, i) for i in range(blocks - 1)]

    shard_rows = qkv_master.shape[0]
    own_gains = jnp.pad(norm_gains, ((0, 0), (0, qkv_master.shape[1] - norm_gains.shape[1])))
    first = jnp.concatenate([qkv_master.astype(LOW), own_gains.astype(LOW)], axis=0)
    ends = normalised(tokens)[0].astype(LOW)
    some = sequences // 2
    tails, heads = ends[:, local_len - HALF :], ends[:, :HALF]
    (first_y, first_core, left1, right1), _ = exchanged(
        [
            ("pair", first, "wshard", 2, 0),
            ("pair", first, "wshard", 1, 0),
            ("send", tails[:some], "seq", to_right, 0),
            ("send", heads[:some], "seq", to_left, 0),
        ]
    )
    rest = jnp.concatenate([proj_master.astype(LOW), down_master.astype(LOW)], axis=0)
    (first_both, rest_y, rest_core, left2, right2), _ = exchanged(
        [
            ("pair", first_y, "wshard", 1, 0),
            ("pair", rest, "wshard", 2, 0),
            ("pair", rest, "wshard", 1, 0),
            ("send", tails[some:], "seq", to_right, 0),
            ("send", heads[some:], "seq", to_left, 0),
        ]
    )
    left = jnp.concatenate([left1, left2], axis=0)
    right = jnp.concatenate([right1, right2], axis=0)
    firsts_known = (first, first_core, first_y, first_both)
    qkv = in_order([piece[:shard_rows] for piece in firsts_known])
    gains = in_order([piece[shard_rows:, : norm_gains.shape[1]].T for piece in firsts_known])
    gains = gains.T.astype(WIDE)
    cosine, sine, cap = tables(base, local_len * blocks)
    rest_both = swapped(rest_y, "wshard", 1)
    rests = (rest, rest_core, rest_y, rest_both)
    proj = in_order([piece[: proj_master.shape[0]] for piece in rests])
    down = in_order([piece[proj_master.shape[0] :] for piece in rests])

    cells = sequences * local_len
    spread = (sequences, local_len, D)
    halo = (sequences, HALF, D)
    def attention(table):
        normed, query, keyval = called(
            project_kernel,
            sequences,
            [(tokens, blocked), (gains, whole), (qkv, whole), (table, whole), (sine, whole)],
            [(spread, LOW, blocked), (spread, LOW, blocked), ((sequences, local_len, 2 * D), LOW, blocked)],
            40,
        )
        normed_ext, keyval_ext, probs, attended, hidden = called(
            attend_kernel,
            sequences,
            [
                (tokens, blocked), (normed, blocked), (left, blocked), (right, blocked), (gains, whole),
                (query, blocked), (keyval, blocked), (qkv, whole), (proj, whole),
                (table, whole), (sine, whole), (cap, whole),
            ],
            [
                ((sequences, SPAN, D), LOW, blocked),
                ((sequences, SPAN, 2 * D), LOW, blocked),
                ((sequences, PAIRS, SPAN, SPAN), LOW, blocked),
                (spread, LOW, blocked),
                (spread, WIDE, blocked),
            ],
            48,
        )
        return hidden, attended, normed, query, normed_ext, keyval_ext, probs

    low_wide = wide_master.astype(LOW)
    (wide_y, wide_core), attention_results = exchanged(
        [("pair", low_wide, "wshard", 2, 0), ("pair", low_wide, "wshard", 1, 0)], (cosine,), attention
    )
    hidden, attended, normed, query, normed_ext, keyval_ext, probs = attention_results
    ((wide_both,), _) = exchanged([("pair", wide_y, "wshard", 1, 0)])
    wide = in_order([low_wide, wide_core, wide_y, wide_both])
    layer_output, d_hidden, d_attn, d_out, normed2, inner, d_both, dy, gain_grad2 = called(
        feed_kernel,
        sequences,
        [
            (hidden, blocked), (cotangent, blocked), (gains, whole),
            (wide, whole), (down, whole), (proj, whole),
        ],
        [
            (spread, WIDE, blocked),
            (spread, WIDE, blocked),
            ((cells, D), LOW, rowed),
            (spread, LOW, blocked),
            ((cells, D), LOW, rowed),
            ((cells, FF), LOW, rowed),
            ((cells, 2 * FF), LOW, rowed),
            ((cells, D), LOW, rowed),
            ((1, D), WIDE, whole),
        ],
        56,
    )
    first_rows = ((0,), (0,))
    shards = lax.axis_size("wshard")
    quarter = lambda grad: grad.astype(LOW).reshape(2, 2, grad.shape[0] // shards, grad.shape[1])
    rest_grad = jnp.concatenate(
        [
            quarter(dot(attended.reshape(cells, D), d_attn, first_rows)),
            quarter(dot(inner, dy, first_rows)),
        ],
        axis=2,
    )
    wide_grad = quarter(dot(normed2, d_both, first_rows))
    (rest_grad, wide_grad), _ = exchanged(
        [("fold", rest_grad, "wshard", 1, 1), ("fold", wide_grad, "wshard", 1, 1)]
    )
    def back_operands(place, cosine):
        return [
            (query, part_of(place)), (keyval_ext, part_of(place)), (keyval_ext, part_of(2 + place)),
            (probs, pairs_of(place)), (d_out, part_of(place)), (cosine, whole), (sine, whole),
        ]

    half_span = (sequences, SPAN, D // 2)
    back_results = [
        ((sequences, local_len, D // 2), LOW, blocked),
        (half_span, LOW, blocked),
        (half_span, LOW, blocked),
    ]

    def back_weight(grads):
        flat = [grad.reshape(-1, D // 2) for grad in grads]
        own = dot(normed.reshape(cells, D), flat[0], first_rows)
        rows = normed_ext.reshape(2 * cells, D)
        grads = [own.astype(LOW)] + [dot(rows, grad, first_rows).astype(LOW) for grad in flat[1:]]
        return quarter(jnp.concatenate(grads, axis=1))

    (rest_grad, wide_grad), back_first = exchanged(
        [("fold", rest_grad, "seq", 1, 2), ("fold", wide_grad, "wshard", 2, 0)],
        (cosine,),
        lambda table: called(first_back_kernel, sequences, back_operands(0, table), back_results, 40),
    )
    ((one_grad,), _) = exchanged([("fold", back_weight(back_first), "wshard", 1, 1)])
    (wide_grad, rest_grad, one_grad), back_second = exchanged(
        [
            ("fold", wide_grad, "seq", 2, 2),
            ("fold", rest_grad, "wshard", 2, 0),
            ("fold", one_grad, "wshard", 2, 0),
        ],
        (cosine,),
        lambda table: called(
            second_back_kernel,
            sequences,
            back_operands(1, table)
            + [(grad, blocked) for grad in back_first]
            + [(qkv, whole), (normed_ext, blocked)],
            back_results
            + [(halo, LOW, blocked), (halo, LOW, blocked), (spread, WIDE, blocked), ((1, D), WIDE, whole)],
            48,
            [pltpu.VMEM((GROUP * WINDOW, D), LOW), pltpu.VMEM((GROUP * SPAN, 2 * D), LOW)],
        ),
    )
    *back_second, d_left, d_right, d_normed, gain_grad1 = back_second
    gains_grad = jnp.concatenate([gain_grad1 / gains[0:1], gain_grad2], axis=0).astype(LOW)
    gains_grad = gains_grad.reshape(2, 2, 2, D // shards).transpose(1, 2, 0, 3)
    two_grad = back_weight(back_second)
    gains_grad = jnp.pad(gains_grad, ((0, 0),) * 3 + ((0, two_grad.shape[3] - D // shards),))
    two_grad = jnp.concatenate([two_grad, gains_grad], axis=2)

    cuts = (0, sequences * 3 // 8, sequences * 3 // 4, sequences)
    from_left, from_right = [], []

    def round_of(steps, cut=None):
        if cut is not None:
            rows = slice(cuts[cut], cuts[cut + 1])
            steps = steps + [
                ("send", d_right[rows], "seq", to_right, 0),
                ("send", d_left[rows], "seq", to_left, 0),
            ]
        results, _ = exchanged(steps)
        if cut is not None:
            from_right.append(results.pop())
            from_left.append(results.pop())
        return results

    wide_grad, one_grad, two_grad = round_of(
        [
            ("fold", wide_grad, "seq", 4, 3),
            ("fold", one_grad, "seq", 2, 3),
            ("fold", two_grad, "wshard", 1, 1),
        ],
        0,
    )
    wide_grad, rest_grad, two_grad = round_of(
        [
            ("full", wide_grad, "seq", 1, 0),
            ("fold", rest_grad, "seq", 2, 3),
            ("fold", two_grad, "wshard", 2, 0),
        ],
        1,
    )
    wide_grad = far_sum(wide_grad)
    wide_grad, one_grad, two_grad = round_of(
        [
            ("join", wide_grad, "seq", 4, 3),
            ("fold", one_grad, "seq", 4, 3),
            ("fold", two_grad, "seq", 2, 3),
        ],
        2,
    )
    wide_grad, rest_grad, one_grad, two_grad = round_of(
        [
            ("join", wide_grad, "seq", 2, 2),
            ("full", rest_grad, "seq", 4, 0),
            ("full", one_grad, "seq", 1, 0),
            ("fold", two_grad, "seq", 4, 3),
        ]
    )
    input_grad = called(
        enter_kernel,
        sequences,
        [
            (tokens, blocked), (gains, whole), (d_normed, blocked),
            (jnp.concatenate(from_left, axis=0), blocked),
            (jnp.concatenate(from_right, axis=0), blocked),
            (d_hidden, blocked),
        ],
        [(spread, WIDE, blocked)],
        32,
    )[0]
    rest_grad, one_grad = far_sum(rest_grad), far_sum(one_grad)
    rest_grad, one_grad, two_grad = round_of(
        [
            ("join", rest_grad, "seq", 2, 3),
            ("join", one_grad, "seq", 4, 3),
            ("full", two_grad, "seq", 1, 0),
        ]
    )
    two_grad = far_sum(two_grad)
    rest_grad, one_grad, two_grad = round_of(
        [
            ("join", rest_grad, "seq", 1, 2),
            ("join", one_grad, "seq", 2, 3),
            ("join", two_grad, "seq", 4, 3),
        ]
    )
    (two_grad,) = round_of([("join", two_grad, "seq", 2, 3)])
    wide_grad, rest_grad, one_grad, two_grad = (
        grad[0, 0].astype(WIDE) for grad in (wide_grad, rest_grad, one_grad, two_grad)
    )
    thirds = []
    for third in range(3):
        columns = slice(third * D // 2, (third + 1) * D // 2)
        thirds += [one_grad[:, columns], two_grad[:shard_rows, columns]]
    owned_grads = (
        jnp.concatenate(thirds, axis=1),
        rest_grad[: proj_master.shape[0]],
        wide_grad,
        rest_grad[proj_master.shape[0] :],
        two_grad[shard_rows:, : norm_gains.shape[1]],
    )
    rates = (
        2.0 * D ** (-0.5),
        2.0 * max(D // WINDOW, 1) ** (-0.5),
        2.0 * D ** (-0.5),
        2.0 * FF ** (-0.5),
        1.0,
    )
    masters = (qkv_master, proj_master, wide_master, down_master, norm_gains)
    firsts = (qkv_first, proj_first, wide_first, down_first, gains_first)
    seconds = (qkv_second, proj_second, wide_second, down_second, gains_second)
    results = [adamw(masters[i], owned_grads[i], firsts[i], seconds[i], rates[i]) for i in range(5)]
    return (
        layer_output,
        input_grad,
        results[0][0],
        results[1][0],
        results[2][0],
        results[3][0],
        results[4][0],
        results[0][1],
        results[1][1],
        results[2][1],
        results[3][1],
        results[4][1],
        results[0][2],
        results[1][2],
        results[2][2],
        results[3][2],
        results[4][2],
    )


def solution(mesh):
    placed = (
        P("wshard", "seq", None),
        P("wshard", "seq", None),
        P("wshard", None),
        P("wshard", None),
        P("wshard", None),
        P("wshard", None),
        P(None, "wshard"),
        P("wshard", None),
        P("wshard", None),
        P("wshard", None),
        P("wshard", None),
        P(None, "wshard"),
        P("wshard", None),
        P("wshard", None),
        P("wshard", None),
        P("wshard", None),
        P(None, "wshard"),
    )
    return jax.shard_map(
        on_device,
        mesh=mesh,
        in_specs=placed,
        out_specs=(
            P("wshard", "seq", None),
            P("wshard", "seq", None),
            P("wshard", None),
            P("wshard", None),
            P("wshard", None),
            P("wshard", None),
            P(None, "wshard"),
            P("wshard", None),
            P("wshard", None),
            P("wshard", None),
            P("wshard", None),
            P(None, "wshard"),
            P("wshard", None),
            P("wshard", None),
            P("wshard", None),
            P("wshard", None),
            P(None, "wshard"),
        ),
        check_vma=False,
    )
```

```python
import jax
import jax.numpy as jnp
from jax import lax
from jax.experimental import pallas as pl
from jax.experimental.pallas import tpu as pltpu
from jax.sharding import PartitionSpec as P

D = 768
HEADS = 12
HEAD = 64
FF = 1152
WINDOW = 128
STEP = 10
HALF = WINDOW // 2
SPAN = 2 * WINDOW
LANES = 128
PAIRS = D // LANES
GROUP = 2
LOW = jnp.bfloat16
WIDE = jnp.float32
SHARDS = 4
GAIN_ROWS = 32
MIB = 1 << 20


def dot(one, other, dims=((1,), (0,))):
    return lax.dot_general(one, other, (dims, ((), ())), preferred_element_type=WIDE)


def normalised(value):
    centred = value - jnp.mean(value, axis=-1, keepdims=True)
    inverse = lax.rsqrt(jnp.mean(centred * centred, axis=-1, keepdims=True) + 1e-05)
    return centred * inverse, inverse


def normalised_back(d_normed, gain, xhat, inverse):
    d_xhat = d_normed * gain
    mean = jnp.mean(d_xhat, axis=-1, keepdims=True)
    slope = jnp.mean(d_xhat * xhat, axis=-1, keepdims=True)
    return inverse * (d_xhat - mean - xhat * slope)


def lane_of(rows):
    return lax.broadcasted_iota(jnp.int32, (rows, LANES), 1)


def half_swapped(value):
    first = lane_of(value.shape[0]) % HEAD < HEAD // 2
    ahead = pltpu.roll(value, LANES - HEAD // 2, 1)
    behind = pltpu.roll(value, HEAD // 2, 1)
    return jnp.where(first, ahead, behind)


def turned(value, cosine, sine):
    return value * cosine + half_swapped(value) * sine


def turned_back(value, cosine, sine):
    return value * cosine - half_swapped(value) * sine


def by_head(value):
    first = lane_of(value.shape[0]) < HEAD
    zero = jnp.zeros_like(value)
    return jnp.concatenate([jnp.where(first, value, zero), jnp.where(first, zero, value)], axis=0)


def side_by_side(value):
    rows = value.shape[0] // 2
    return jnp.where(lane_of(rows) < HEAD, value[:rows], value[rows:])


def pair(index, start=0):
    return slice(start + index * LANES, start + (index + 1) * LANES)


def laid(place, pieces, target, size, start=0):
    @pl.when(pl.program_id(0) == 0)
    def _():
        for known, piece in enumerate(pieces):
            row = pl.multiple_of((place[0] ^ known) * size, 16)
            target[pl.ds(row, size), :] = piece[start : start + size, :]


def shipped(place, kept, sent, shard, row, columns, value):
    value = value.astype(LOW)
    lead = (place[0] // 2) ^ (shard // 2)
    mine = place[0] % 2 == shard % 2

    @pl.when(mine)
    def _():
        kept[lead, row : row + value.shape[0], columns] = value

    @pl.when(jnp.logical_not(mine))
    def _():
        sent[lead, row : row + value.shape[0], columns] = value


def shipped_rows(place, kept, sent, start, size, row, columns, value):
    end = start + value.shape[0]
    for shard in range(SHARDS):
        low, high = max(start, shard * size), min(end, (shard + 1) * size)
        if low < high:
            part = value[low - start : high - start]
            shipped(place, kept, sent, shard, row + low - shard * size, columns, part)


def project_kernel(
    place, tokens, gains, one_piece, two_piece, three_piece, four_piece, cosine, sine,
    normed, query, keyval, weight,
):
    laid(place, (one_piece, two_piece, three_piece, four_piece), weight, D // SHARDS)
    rows = GROUP * WINDOW
    xhat, _ = normalised(tokens[...].reshape(rows, D))
    low = (xhat * gains[0:1, :]).astype(LOW)
    normed[...] = low.reshape(GROUP, WINDOW, D)
    mine = slice(HALF, HALF + WINDOW)
    cos, sin = cosine[mine], sine[mine]
    out = dot(low, weight[:, :D])
    for one in range(GROUP):
        for p in range(PAIRS):
            part = out[one * WINDOW : (one + 1) * WINDOW, pair(p)]
            query[one, :, pair(p)] = (turned(part, cos, sin) * HEAD**-0.5).astype(LOW)
    out = dot(low, weight[:, D : 2 * D])
    for one in range(GROUP):
        for p in range(PAIRS):
            part = out[one * WINDOW : (one + 1) * WINDOW, pair(p)]
            keyval[one, :, pair(p)] = turned(part, cos, sin).astype(LOW)
    out = dot(low, weight[:, 2 * D :])
    keyval[:, :, D:] = out.astype(LOW).reshape(GROUP, WINDOW, D)


def attend_kernel(
    place, tokens, normed, left, right, gains, query, keyval, weight,
    one_piece, two_piece, three_piece, four_piece, cosine, sine, cap,
    normed_ext, keyval_ext, probs, attended, hidden, proj,
):
    laid(place, (one_piece, two_piece, three_piece, four_piece), proj, D // SHARDS)
    gain = gains[0:1, :]
    ends = []
    for one in range(GROUP):
        low_left = (left[one].astype(WIDE) * gain).astype(LOW)
        low_right = (right[one].astype(WIDE) * gain).astype(LOW)
        normed_ext[one, :HALF] = low_left
        normed_ext[one, HALF : HALF + WINDOW] = normed[one]
        normed_ext[one, HALF + WINDOW :] = low_right
        ends += [low_left, low_right]
    ends = jnp.concatenate(ends, axis=0)
    cos = jnp.concatenate([cosine[:HALF], cosine[HALF + WINDOW :]], axis=0)
    sin = jnp.concatenate([sine[:HALF], sine[HALF + WINDOW :]], axis=0)
    keys = dot(ends, weight[:, D : 2 * D])
    values = dot(ends, weight[:, 2 * D :]).astype(LOW)
    for one in range(GROUP):
        keyval_ext[one, HALF : HALF + WINDOW] = keyval[one]
        rows = slice(one * WINDOW, (one + 1) * WINDOW)
        keyval_ext[one, :HALF, D:] = values[rows][:HALF]
        keyval_ext[one, HALF + WINDOW :, D:] = values[rows][HALF:]
        for p in range(PAIRS):
            key = turned(keys[rows, pair(p)], cos, sin).astype(LOW)
            keyval_ext[one, :HALF, pair(p)] = key[:HALF]
            keyval_ext[one, HALF + WINDOW :, pair(p)] = key[HALF:]
    limit = jnp.concatenate([cap[...], cap[...]], axis=0)
    for one in range(GROUP):
        for p in range(PAIRS):
            asked = by_head(query[one, :, pair(p)])
            scores = dot(asked, keyval_ext[one, :, pair(p)], ((1,), (1,)))
            scores = jnp.minimum(scores, limit)
            top = jnp.max(scores, axis=-1, keepdims=True)
            grown = jnp.exp(scores - top)
            prob = grown * (1.0 / jnp.sum(grown, axis=-1, keepdims=True))
            prob = prob.astype(LOW)
            probs[one, p] = prob
            found = dot(prob, keyval_ext[one, :, pair(p, D)])
            attended[one, :, pair(p)] = side_by_side(found).astype(LOW)
    rows = GROUP * WINDOW
    out = dot(attended[...].reshape(rows, D), proj[...])
    hidden[...] = tokens[...] + out.reshape(GROUP, WINDOW, D)


def feed_kernel(
    place, hidden, cotangent, gains, proj, attended,
    wide1, wide2, wide3, wide4, down1, down2, down3, down4,
    output, d_hidden, d_out, gain_grad, kept, sent,
    wide, down, all_normed, all_inner, all_d_both, all_dy, all_d_attn,
):
    laid(place, (wide1, wide2, wide3, wide4), wide, D // SHARDS)
    laid(place, (down1, down2, down3, down4), down, FF // SHARDS, D // SHARDS)
    here = pl.ds(pl.multiple_of(pl.program_id(0) * GROUP * WINDOW, GROUP * WINDOW), GROUP * WINDOW)
    normed, inner, d_both = all_normed.at[here], all_inner.at[here], all_d_both.at[here]
    low_cotangent, d_attn = all_dy.at[here], all_d_attn.at[here]
    rows = GROUP * WINDOW
    state = hidden[...].reshape(rows, D)
    gain = gains[1:2, :]
    xhat, inverse = normalised(state)
    low = (xhat * gain).astype(LOW)
    normed[...] = low
    above = cotangent[...].reshape(rows, D)
    dy = above.astype(LOW)
    low_cotangent[...] = dy
    start = 0
    while start < FF:
        size = min(256, FF - start)
        cols = slice(start, start + size)
        other = slice(FF + start, FF + start + size)
        gate = dot(low, wide[:, cols])
        upward = dot(low, wide[:, other])
        d_inner = dot(dy, down[cols, :], ((1,), (1,)))
        area = 0.5 + 0.5 * lax.erf(gate * (0.5**0.5))
        shaped = gate * area
        slope = area + gate * (jnp.exp(-0.5 * gate * gate) * 0.3989422804014327)
        inner[:, cols] = (shaped * upward).astype(LOW)
        d_both[:, cols] = (d_inner * upward * slope).astype(LOW)
        d_both[:, other] = (d_inner * shaped).astype(LOW)
        start += size
    output[...] = (state + dot(inner[...], down[...])).reshape(GROUP, WINDOW, D)
    d_normed = dot(d_both[...], wide[...], ((1,), (1,)))
    part = jnp.sum(d_normed * xhat, axis=0, keepdims=True)

    @pl.when(pl.program_id(0) == 0)
    def _():
        gain_grad[...] = part

    @pl.when(pl.program_id(0) > 0)
    def _():
        gain_grad[...] += part

    back = above + normalised_back(d_normed, gain, xhat, inverse)
    d_hidden[...] = back.reshape(GROUP, WINDOW, D)
    back = back.astype(LOW)
    d_attn[...] = back
    d_out[...] = dot(back, proj[...], ((1,), (1,))).astype(LOW).reshape(GROUP, WINDOW, D)

    @pl.when(pl.program_id(0) == pl.num_programs(0) - 1)
    def _():
        first_rows = ((0,), (0,))
        every = slice(0, D)
        size = D // 2
        for start in range(0, D, size):
            lanes = slice(start, start + size)
            for third in range(3):
                grad = dot(all_normed[:, lanes], all_d_both[:, third * D : (third + 1) * D], first_rows)
                shipped_rows(place, kept, sent, start, D // SHARDS, third * D // SHARDS, every, grad)
            grad = dot(attended[:, lanes], all_d_attn[...], first_rows)
            shipped_rows(place, kept, sent, start, D // SHARDS, 3 * D // SHARDS, every, grad)
        for start in range(0, FF, size):
            grad = dot(all_inner[:, start : start + size], all_dy[...], first_rows)
            shipped_rows(place, kept, sent, start, FF // SHARDS, D, every, grad)


def attend_back_kernel(
    place, query, keyval, probs, d_out, weight, cosine, sine, normed_ext, gains, gain_grad2,
    d_left, d_right, d_normed, kept, sent,
    all_query, all_keyval, gain_grad1,
):
    step = pl.program_id(0)
    mine = slice(HALF, HALF + WINDOW)
    cos, sin = cosine[mine], sine[mine]
    here = pl.ds(pl.multiple_of(step * GROUP * WINDOW, GROUP * WINDOW), GROUP * WINDOW)
    d_query = all_query.at[here]
    here = pl.ds(pl.multiple_of(step * GROUP * SPAN, GROUP * SPAN), GROUP * SPAN)
    d_keyval = all_keyval.at[here]
    for one in range(GROUP):
        short = slice(one * WINDOW, (one + 1) * WINDOW)
        long = slice(one * SPAN, (one + 1) * SPAN)
        for p in range(PAIRS):
            asked = by_head(query[one, :, pair(p)])
            key = keyval[one, :, pair(p)]
            grad = by_head(d_out[one, :, pair(p)])
            low_prob = probs[one, p]
            prob = low_prob.astype(WIDE)
            d_prob = dot(grad, keyval[one, :, pair(p, D)], ((1,), (1,)))
            delta = jnp.sum(prob * d_prob, axis=-1, keepdims=True)
            d_score = (prob * (d_prob - delta)).astype(LOW)
            d_q = side_by_side(dot(d_score, key)) * HEAD**-0.5
            d_query[short, pair(p)] = turned_back(d_q, cos, sin).astype(LOW)
            d_k = dot(d_score, asked, ((0,), (0,)))
            d_keyval[long, pair(p)] = turned_back(d_k, cosine[...], sine[...]).astype(LOW)
            d_v = dot(low_prob, grad, ((0,), (0,)))
            d_keyval[long, pair(p, D)] = d_v.astype(LOW)
    both = dot(d_keyval[...], weight[:, D:], ((1,), (1,)))
    own = dot(d_query[...], weight[:, :D], ((1,), (1,)))
    total = jnp.zeros((1, D), WIDE)
    for one in range(GROUP):
        part = both[one * SPAN : (one + 1) * SPAN]
        inside = own[one * WINDOW : (one + 1) * WINDOW]
        rows = normed_ext[step * GROUP + one].astype(WIDE)
        total += jnp.sum(part * rows, axis=0, keepdims=True)
        total += jnp.sum(inside * rows[mine], axis=0, keepdims=True)
        d_left[one] = part[:HALF].astype(LOW)
        d_right[one] = part[HALF + WINDOW :].astype(LOW)
        d_normed[one] = part[mine] + inside

    @pl.when(step == 0)
    def _():
        gain_grad1[...] = total

    @pl.when(step > 0)
    def _():
        gain_grad1[...] += total

    @pl.when(step == pl.num_programs(0) - 1)
    def _():
        first_rows = ((0,), (0,))
        sequences = normed_ext.shape[0]
        size = D // 2
        for start in range(0, D, size):
            lanes = slice(start, start + size)
            rows = normed_ext[:, mine, lanes].reshape(sequences * WINDOW, size)
            grad = dot(rows, all_query[...], first_rows)
            shipped_rows(place, kept, sent, start, D // SHARDS, 0, slice(0, D), grad)
            rows = normed_ext[:, :, lanes].reshape(sequences * SPAN, size)
            for part in range(2):
                grad = dot(rows, all_keyval[:, part * D : (part + 1) * D], first_rows)
                columns = slice((part + 1) * D, (part + 2) * D)
                shipped_rows(place, kept, sent, start, D // SHARDS, 0, columns, grad)
        more = slice(D // SHARDS, D // SHARDS + GAIN_ROWS)
        first = gain_grad1[...] / gains[0:1, :]
        empty = jnp.zeros((GAIN_ROWS - 2, D), WIDE)
        both_gains = jnp.concatenate([first, gain_grad2[...], empty], axis=0).astype(LOW)
        for target in (kept, sent):
            for lead in range(2):
                target[lead, more, :] = jnp.zeros((GAIN_ROWS, 3 * D), LOW)
                target[lead, more, 3 * D // 2 : 5 * D // 2] = both_gains


def enter_kernel(tokens, gains, d_normed, from_left, from_right, d_hidden, input_grad):
    rows = GROUP * WINDOW
    xhat, inverse = normalised(tokens[...].reshape(rows, D))
    parts = []
    for one in range(GROUP):
        parts += [
            d_normed[one, :HALF] + from_left[one].astype(WIDE),
            d_normed[one, HALF:] + from_right[one].astype(WIDE),
        ]
    back = normalised_back(jnp.concatenate(parts, axis=0), gains[0:1, :], xhat, inverse)
    input_grad[...] = d_hidden[...] + back.reshape(GROUP, WINDOW, D)


def whole(shape):
    return pl.BlockSpec(shape, lambda i: (0,) * len(shape))


def once(shape):
    return pl.BlockSpec(shape, lambda i: (0,) * len(shape), pipeline_mode=pl.Buffered(1))


def once_rows(rows):
    return lambda shape: pl.BlockSpec((rows, shape[1]), lambda i: (0, 0), pipeline_mode=pl.Buffered(1))


def scalar(shape):
    return pl.BlockSpec(memory_space=pltpu.SMEM)


def blocked(shape):
    return pl.BlockSpec((GROUP,) + tuple(shape[1:]), lambda i: (i,) + (0,) * (len(shape) - 1))


def called(kernel, sequences, operands, results, limit, scratch=()):
    arrays = [array for array, _ in operands]
    return pl.pallas_call(
        kernel,
        grid=(sequences // GROUP,),
        in_specs=[spec(array.shape) for array, spec in operands],
        out_specs=[spec(shape) for shape, _, spec in results],
        out_shape=[jax.ShapeDtypeStruct(shape, kind) for shape, kind, _ in results],
        scratch_shapes=list(scratch),
        compiler_params=pltpu.CompilerParams(
            dimension_semantics=("arbitrary",), vmem_limit_bytes=limit * MIB
        ),
        cost_estimate=pl.CostEstimate(flops=1000, bytes_accessed=1000, transcendentals=0),
    )(*arrays)


def swapped(value, axis, bit):
    count = lax.axis_size(axis)
    return lax.ppermute(value, axis, [(i, i ^ bit) for i in range(count)])


def exchanged(steps, carried=(), beside=None):
    kept, sent = [], []
    for how, value, axis, bit, dim in steps:
        if how == "lead":
            kept.append(value[0])
            value = value[1]
        elif how == "fold":
            side = (lax.axis_index(axis) // bit) % 2
            size = value.shape[dim] // 2
            kept.append(lax.dynamic_slice_in_dim(value, side * size, size, axis=dim))
            value = lax.dynamic_slice_in_dim(value, (1 - side) * size, size, axis=dim)
        else:
            kept.append(None)
        sent.append(value)
    held = lax.optimization_barrier(tuple(sent) + tuple(carried))
    sent, carried = held[: len(sent)], held[len(sent) :]
    got = []
    for (how, _, axis, bit, _), value in zip(steps, sent):
        got.append(lax.ppermute(value, axis, bit) if how == "send" else swapped(value, axis, bit))
    if beside is not None:
        carried = beside(*carried)
    held = lax.optimization_barrier(tuple(got) + tuple(carried))
    got, carried = held[: len(got)], held[len(got) :]
    results = []
    for (how, _, axis, bit, dim), mine, own, other in zip(steps, kept, sent, got):
        if how in ("fold", "lead"):
            other = (mine.astype(WIDE) + other.astype(WIDE)).astype(LOW)
        elif how == "full":
            other = (own.astype(WIDE) + other.astype(WIDE)).astype(LOW)
        elif how == "join":
            side = (lax.axis_index(axis) // bit) % 2
            low = jnp.where(side == 0, own, other)
            high = jnp.where(side == 0, other, own)
            other = jnp.concatenate([low, high], axis=dim)
        results.append(other)
    return results, carried


def far_sum(value):
    bit = 8
    while bit < lax.axis_size("seq"):
        ((value,), _) = exchanged([("full", value, "seq", bit, 0)])
        bit *= 2
    return value


def adamw(master, grad, first, second, rate):
    moment = 0.9 * first + 0.1 * grad
    square = 0.98 * second + 0.02 * grad * grad
    fixed_first = moment / (1.0 - 0.9**STEP)
    fixed_second = square / (1.0 - 0.98**STEP)
    update = fixed_first / (jnp.sqrt(fixed_second) + 1e-06) + 1e-05 * master
    return (master - rate * update, moment, square)


def in_order(pieces):
    place = lax.axis_index("wshard")
    size = pieces[0].shape[0]
    total = jnp.zeros((size * len(pieces),) + pieces[0].shape[1:], pieces[0].dtype)
    for known, piece in enumerate(pieces):
        total = lax.dynamic_update_slice_in_dim(total, piece, (place ^ known) * size, 0)
    return total


def tables(base, total):
    places = base - HALF + jnp.arange(SPAN, dtype=jnp.int32)
    freqs = 10000.0 ** (-jnp.arange(0, HEAD, 2).astype(WIDE) / HEAD)
    angles = places.astype(WIDE)[:, None] * freqs[None, :]
    cosine, sine = jnp.cos(angles), jnp.sin(angles)
    cosine = jnp.concatenate([cosine] * 4, axis=1)
    sine = jnp.concatenate([-sine, sine] * 2, axis=1)
    row = jnp.arange(WINDOW)[:, None]
    col = jnp.arange(SPAN)[None, :]
    seen = (col >= row) & (col <= row + WINDOW) & (places >= 0)[None, :] & (places < total)[None, :]
    return cosine, sine, jnp.where(seen, 3e38, -1e30).astype(WIDE)


def on_device(
    tokens,
    cotangent,
    qkv_master,
    proj_master,
    wide_master,
    down_master,
    norm_gains,
    qkv_first,
    proj_first,
    wide_first,
    down_first,
    gains_first,
    qkv_second,
    proj_second,
    wide_second,
    down_second,
    gains_second,
):
    sequences, local_len, width = tokens.shape
    blocks = lax.axis_size("seq")
    base = lax.axis_index("seq") * local_len
    to_right = [(i, i + 1) for i in range(blocks - 1)]
    to_left = [(i + 1, i) for i in range(blocks - 1)]

    shard_rows = qkv_master.shape[0]
    own_gains = jnp.pad(norm_gains, ((0, 14), (0, qkv_master.shape[1] - norm_gains.shape[1])))
    first = jnp.concatenate([qkv_master.astype(LOW), own_gains.astype(LOW)], axis=0)
    ends = normalised(tokens)[0].astype(LOW)
    some = sequences * 5 // 8
    tails, heads = ends[:, local_len - HALF :], ends[:, :HALF]
    (first_y, first_core, left1, right1), _ = exchanged(
        [
            ("pair", first, "wshard", 2, 0),
            ("pair", first, "wshard", 1, 0),
            ("send", tails[:some], "seq", to_right, 0),
            ("send", heads[:some], "seq", to_left, 0),
        ]
    )
    rest = jnp.concatenate([proj_master.astype(LOW), down_master.astype(LOW)], axis=0)
    (first_both, rest_y, rest_core, left2, right2), _ = exchanged(
        [
            ("pair", first_y, "wshard", 1, 0),
            ("pair", rest, "wshard", 2, 0),
            ("pair", rest, "wshard", 1, 0),
            ("send", tails[some:], "seq", to_right, 0),
            ("send", heads[some:], "seq", to_left, 0),
        ]
    )
    left = jnp.concatenate([left1, left2], axis=0)
    right = jnp.concatenate([right1, right2], axis=0)
    firsts_known = (first, first_core, first_y, first_both)
    gains = in_order([piece[shard_rows : shard_rows + 2, : norm_gains.shape[1]].T for piece in firsts_known])
    gains = gains.T.astype(WIDE)
    cosine, sine, cap = tables(base, local_len * blocks)
    rest_both = swapped(rest_y, "wshard", 1)
    rests = (rest, rest_core, rest_y, rest_both)
    place = lax.axis_index("wshard").astype(jnp.int32).reshape(1)
    cells = sequences * local_len
    spread = (sequences, local_len, D)
    halo = (sequences, HALF, D)
    def attention(table):
        normed, query, keyval, qkv = called(
            project_kernel,
            sequences,
            [(place, scalar), (tokens, blocked), (gains, whole)]
            + [(piece, once_rows(shard_rows)) for piece in firsts_known]
            + [(table, whole), (sine, whole)],
            [
                (spread, LOW, blocked),
                (spread, LOW, blocked),
                ((sequences, local_len, 2 * D), LOW, blocked),
                ((D, 3 * D), LOW, whole),
            ],
            48,
        )
        normed_ext, keyval_ext, probs, attended, hidden, proj = called(
            attend_kernel,
            sequences,
            [
                (place, scalar), (tokens, blocked), (normed, blocked), (left, blocked), (right, blocked),
                (gains, whole), (query, blocked), (keyval, blocked), (qkv, once),
            ]
            + [(piece, once_rows(proj_master.shape[0])) for piece in rests]
            + [(table, whole), (sine, whole), (cap, whole)],
            [
                ((sequences, SPAN, D), LOW, blocked),
                ((sequences, SPAN, 2 * D), LOW, blocked),
                ((sequences, PAIRS, SPAN, SPAN), LOW, blocked),
                (spread, LOW, blocked),
                (spread, WIDE, blocked),
                ((D, D), LOW, whole),
            ],
            52,
        )
        return hidden, attended, query, normed_ext, keyval_ext, probs, qkv, proj

    low_wide = wide_master.astype(LOW)
    (wide_y, wide_core), attention_results = exchanged(
        [("pair", low_wide, "wshard", 2, 0), ("pair", low_wide, "wshard", 1, 0)], (cosine,), attention
    )
    hidden, attended, query, normed_ext, keyval_ext, probs, qkv, proj = attention_results
    ((wide_both,), _) = exchanged([("pair", wide_y, "wshard", 1, 0)])
    wides = (low_wide, wide_core, wide_y, wide_both)
    rest_rows = 3 * shard_rows + rest.shape[0]
    shares = (2, rest_rows, D)
    layer_output, d_hidden, d_out, gain_grad2, rest_kept, rest_sent = called(
        feed_kernel,
        sequences,
        [
            (place, scalar), (hidden, blocked), (cotangent, blocked), (gains, whole),
            (proj, once), (attended.reshape(cells, D), once),
        ]
        + [(piece, once) for piece in wides + rests],
        [
            (spread, WIDE, blocked),
            (spread, WIDE, blocked),
            (spread, LOW, blocked),
            ((1, D), WIDE, whole),
            (shares, LOW, whole),
            (shares, LOW, whole),
        ],
        60,
        [
            pltpu.VMEM((D, 2 * FF), LOW),
            pltpu.VMEM((FF, D), LOW),
            pltpu.VMEM((cells, D), LOW),
            pltpu.VMEM((cells, FF), LOW),
            pltpu.VMEM((cells, 2 * FF), LOW),
            pltpu.VMEM((cells, D), LOW),
            pltpu.VMEM((cells, D), LOW),
        ],
    )

    def summed(kept, got):
        return (kept.astype(WIDE) + got.astype(WIDE)).astype(LOW)

    ((rest_got,), _) = exchanged([("pair", rest_sent, "wshard", 1, 0)])
    rest_grad = summed(rest_kept, rest_got)
    shares = (2, shard_rows + GAIN_ROWS, 3 * D)
    (rest_grad,), back_results = exchanged(
        [("lead", rest_grad, "wshard", 2, 0)],
        (cosine,),
        lambda table: called(
            attend_back_kernel,
            sequences,
            [
                (place, scalar), (query, blocked), (keyval_ext, blocked), (probs, blocked),
                (d_out, blocked), (qkv, once), (table, whole), (sine, whole), (normed_ext, once),
                (gains, whole), (gain_grad2, whole),
            ],
            [
                (halo, LOW, blocked),
                (halo, LOW, blocked),
                (spread, WIDE, blocked),
                (shares, LOW, whole),
                (shares, LOW, whole),
            ],
            56,
            [
                pltpu.VMEM((cells, D), LOW),
                pltpu.VMEM((2 * cells, 2 * D), LOW),
                pltpu.VMEM((1, D), WIDE),
            ],
        ),
    )
    d_left, d_right, d_normed, kept, sent = back_results
    (got, rest_grad), _ = exchanged(
        [("pair", sent, "wshard", 1, 0), ("fold", rest_grad, "seq", 1, 0)]
    )
    both_grad = summed(kept, got)
    half = 3 * D // 2
    one_grad, two_grad = both_grad[:, :shard_rows, :half], both_grad[:, :, half:]

    cuts = (0, sequences * 3 // 8, sequences * 3 // 4, sequences)
    from_left, from_right = [], []

    def round_of(steps, cut=None):
        if cut is not None:
            rows = slice(cuts[cut], cuts[cut + 1])
            steps = steps + [
                ("send", d_right[rows], "seq", to_right, 0),
                ("send", d_left[rows], "seq", to_left, 0),
            ]
        results, _ = exchanged(steps)
        if cut is not None:
            from_right.append(results.pop())
            from_left.append(results.pop())
        return results

    rest_grad, one_grad, two_grad = round_of(
        [
            ("fold", rest_grad, "seq", 2, 0),
            ("lead", one_grad, "wshard", 2, 0),
            ("fold", two_grad, "seq", 2, 1),
        ],
        0,
    )
    rest_grad, one_grad, two_grad = round_of(
        [
            ("full", rest_grad, "seq", 4, 0),
            ("fold", one_grad, "seq", 2, 0),
            ("lead", two_grad, "wshard", 2, 0),
        ],
        1,
    )
    rest_grad = far_sum(rest_grad)
    rest_grad, one_grad, two_grad = round_of(
        [
            ("join", rest_grad, "seq", 2, 0),
            ("full", one_grad, "seq", 4, 0),
            ("full", two_grad, "seq", 1, 0),
        ],
        2,
    )
    rest_grad, one_grad, two_grad = round_of(
        [
            ("join", rest_grad, "seq", 1, 0),
            ("full", one_grad, "seq", 1, 0),
            ("full", two_grad, "seq", 4, 0),
        ]
    )
    input_grad = called(
        enter_kernel,
        sequences,
        [
            (tokens, blocked), (gains, whole), (d_normed, blocked),
            (jnp.concatenate(from_left, axis=0), blocked),
            (jnp.concatenate(from_right, axis=0), blocked),
            (d_hidden, blocked),
        ],
        [(spread, WIDE, blocked)],
        32,
    )[0]
    one_grad, two_grad = far_sum(one_grad), far_sum(two_grad)
    one_grad, two_grad = round_of([("join", one_grad, "seq", 2, 0), ("join", two_grad, "seq", 2, 0)])
    rest_grad, one_grad, two_grad = (grad.astype(WIDE) for grad in (rest_grad, one_grad, two_grad))
    gains_sum = lax.dynamic_slice_in_dim(
        two_grad[shard_rows : shard_rows + 2],
        lax.axis_index("wshard") * norm_gains.shape[1],
        norm_gains.shape[1],
        axis=1,
    )
    wide_parts = [rest_grad[third * shard_rows : (third + 1) * shard_rows] for third in range(3)]
    owned_grads = (
        jnp.concatenate([one_grad, two_grad[:shard_rows]], axis=1),
        rest_grad[3 * shard_rows : 4 * shard_rows],
        jnp.concatenate(wide_parts, axis=1),
        rest_grad[4 * shard_rows :],
        gains_sum,
    )
    rates = (
        2.0 * D ** (-0.5),
        2.0 * max(D // WINDOW, 1) ** (-0.5),
        2.0 * D ** (-0.5),
        2.0 * FF ** (-0.5),
        1.0,
    )
    masters = (qkv_master, proj_master, wide_master, down_master, norm_gains)
    firsts = (qkv_first, proj_first, wide_first, down_first, gains_first)
    seconds = (qkv_second, proj_second, wide_second, down_second, gains_second)
    results = [adamw(masters[i], owned_grads[i], firsts[i], seconds[i], rates[i]) for i in range(5)]
    return (
        layer_output,
        input_grad,
        results[0][0],
        results[1][0],
        results[2][0],
        results[3][0],
        results[4][0],
        results[0][1],
        results[1][1],
        results[2][1],
        results[3][1],
        results[4][1],
        results[0][2],
        results[1][2],
        results[2][2],
        results[3][2],
        results[4][2],
    )


def solution(mesh):
    placed = (
        P("wshard", "seq", None),
        P("wshard", "seq", None),
        P("wshard", None),
        P("wshard", None),
        P("wshard", None),
        P("wshard", None),
        P(None, "wshard"),
        P("wshard", None),
        P("wshard", None),
        P("wshard", None),
        P("wshard", None),
        P(None, "wshard"),
        P("wshard", None),
        P("wshard", None),
        P("wshard", None),
        P("wshard", None),
        P(None, "wshard"),
    )
    return jax.shard_map(
        on_device,
        mesh=mesh,
        in_specs=placed,
        out_specs=(
            P("wshard", "seq", None),
            P("wshard", "seq", None),
            P("wshard", None),
            P("wshard", None),
            P("wshard", None),
            P("wshard", None),
            P(None, "wshard"),
            P("wshard", None),
            P("wshard", None),
            P("wshard", None),
            P("wshard", None),
            P(None, "wshard"),
            P("wshard", None),
            P("wshard", None),
            P("wshard", None),
            P("wshard", None),
            P(None, "wshard"),
        ),
        check_vma=False,
    )
```

```python
import jax
import jax.numpy as jnp
from jax import lax
from jax.experimental import pallas as pl
from jax.experimental.pallas import tpu as pltpu
from jax.sharding import PartitionSpec as P

D = 768
HEADS = 12
HEAD = 64
FF = 1152
WINDOW = 128
STEP = 10
HALF = WINDOW // 2
SPAN = 2 * WINDOW
LANES = 128
PAIRS = D // LANES
GROUP = 2
LOW = jnp.bfloat16
WIDE = jnp.float32
SHARDS = 4
GAIN_ROWS = 32
MIB = 1 << 20


def dot(one, other, dims=((1,), (0,))):
    return lax.dot_general(one, other, (dims, ((), ())), preferred_element_type=WIDE)


def normalised(value):
    centred = value - jnp.mean(value, axis=-1, keepdims=True)
    inverse = lax.rsqrt(jnp.mean(centred * centred, axis=-1, keepdims=True) + 1e-05)
    return centred * inverse, inverse


def normalised_back(d_normed, gain, xhat, inverse):
    d_xhat = d_normed * gain
    mean = jnp.mean(d_xhat, axis=-1, keepdims=True)
    slope = jnp.mean(d_xhat * xhat, axis=-1, keepdims=True)
    return inverse * (d_xhat - mean - xhat * slope)


def lane_of(rows):
    return lax.broadcasted_iota(jnp.int32, (rows, LANES), 1)


def half_swapped(value):
    first = lane_of(value.shape[0]) % HEAD < HEAD // 2
    ahead = pltpu.roll(value, LANES - HEAD // 2, 1)
    behind = pltpu.roll(value, HEAD // 2, 1)
    return jnp.where(first, ahead, behind)


def turned(value, cosine, sine):
    return value * cosine + half_swapped(value) * sine


def turned_back(value, cosine, sine):
    return value * cosine - half_swapped(value) * sine


def by_head(value):
    first = lane_of(value.shape[0]) < HEAD
    zero = jnp.zeros_like(value)
    return jnp.concatenate([jnp.where(first, value, zero), jnp.where(first, zero, value)], axis=0)


def side_by_side(value):
    rows = value.shape[0] // 2
    return jnp.where(lane_of(rows) < HEAD, value[:rows], value[rows:])


def pair(index, start=0):
    return slice(start + index * LANES, start + (index + 1) * LANES)


def laid(place, pieces, target, size, start=0):
    @pl.when(pl.program_id(0) == 0)
    def _():
        for known, piece in enumerate(pieces):
            row = pl.multiple_of((place[0] ^ known) * size, 16)
            target[pl.ds(row, size), :] = piece[start : start + size, :]


def shipped(place, kept, sent, shard, row, columns, value):
    value = value.astype(LOW)
    lead = (place[0] // 2) ^ (shard // 2)
    mine = place[0] % 2 == shard % 2

    @pl.when(mine)
    def _():
        kept[lead, row : row + value.shape[0], columns] = value

    @pl.when(jnp.logical_not(mine))
    def _():
        sent[lead, row : row + value.shape[0], columns] = value


def shipped_rows(place, kept, sent, start, size, row, columns, value):
    end = start + value.shape[0]
    for shard in range(SHARDS):
        low, high = max(start, shard * size), min(end, (shard + 1) * size)
        if low < high:
            part = value[low - start : high - start]
            shipped(place, kept, sent, shard, row + low - shard * size, columns, part)


def project_kernel(
    place, tokens, gains, one_piece, two_piece, three_piece, four_piece, cosine, sine,
    normed, query, keyval, weight,
):
    laid(place, (one_piece, two_piece, three_piece, four_piece), weight, D // SHARDS)
    rows = GROUP * WINDOW
    xhat, _ = normalised(tokens[...].reshape(rows, D))
    low = (xhat * gains[0:1, :]).astype(LOW)
    normed[...] = low.reshape(GROUP, WINDOW, D)
    mine = slice(HALF, HALF + WINDOW)
    cos, sin = cosine[mine], sine[mine]
    out = dot(low, weight[:, :D])
    for one in range(GROUP):
        for p in range(PAIRS):
            part = out[one * WINDOW : (one + 1) * WINDOW, pair(p)]
            query[one, :, pair(p)] = (turned(part, cos, sin) * HEAD**-0.5).astype(LOW)
    out = dot(low, weight[:, D : 2 * D])
    for one in range(GROUP):
        for p in range(PAIRS):
            part = out[one * WINDOW : (one + 1) * WINDOW, pair(p)]
            keyval[one, :, pair(p)] = turned(part, cos, sin).astype(LOW)
    out = dot(low, weight[:, 2 * D :])
    keyval[:, :, D:] = out.astype(LOW).reshape(GROUP, WINDOW, D)


def attend_kernel(
    place, tokens, normed, left, right, gains, query, keyval, weight,
    one_piece, two_piece, three_piece, four_piece, cosine, sine, cap,
    normed_ext, keyval_ext, probs, attended, hidden, proj,
):
    group = tokens.shape[0]
    laid(place, (one_piece, two_piece, three_piece, four_piece), proj, D // SHARDS)
    gain = gains[0:1, :]
    ends = []
    for one in range(group):
        low_left = (left[one].astype(WIDE) * gain).astype(LOW)
        low_right = (right[one].astype(WIDE) * gain).astype(LOW)
        normed_ext[one, :HALF] = low_left
        normed_ext[one, HALF : HALF + WINDOW] = normed[one]
        normed_ext[one, HALF + WINDOW :] = low_right
        ends += [low_left, low_right]
    ends = jnp.concatenate(ends, axis=0)
    cos = jnp.concatenate([cosine[:HALF], cosine[HALF + WINDOW :]], axis=0)
    sin = jnp.concatenate([sine[:HALF], sine[HALF + WINDOW :]], axis=0)
    keys = dot(ends, weight[:, D : 2 * D])
    values = dot(ends, weight[:, 2 * D :]).astype(LOW)
    for one in range(group):
        keyval_ext[one, HALF : HALF + WINDOW] = keyval[one]
        rows = slice(one * WINDOW, (one + 1) * WINDOW)
        keyval_ext[one, :HALF, D:] = values[rows][:HALF]
        keyval_ext[one, HALF + WINDOW :, D:] = values[rows][HALF:]
        for p in range(PAIRS):
            key = turned(keys[rows, pair(p)], cos, sin).astype(LOW)
            keyval_ext[one, :HALF, pair(p)] = key[:HALF]
            keyval_ext[one, HALF + WINDOW :, pair(p)] = key[HALF:]
    limit = jnp.concatenate([cap[...], cap[...]], axis=1)
    for one in range(group):
        for p in range(PAIRS):
            asked = by_head(query[one, :, pair(p)])
            scores = dot(keyval_ext[one, :, pair(p)], asked, ((1,), (1,)))
            scores = jnp.minimum(scores, limit)
            top = jnp.max(scores, axis=0, keepdims=True)
            grown = jnp.exp(scores - top)
            prob = grown * (1.0 / jnp.sum(grown, axis=0, keepdims=True))
            prob = prob.astype(LOW)
            probs[one, p] = prob
            found = dot(prob, keyval_ext[one, :, pair(p, D)], ((0,), (0,)))
            attended[one, :, pair(p)] = side_by_side(found).astype(LOW)
    rows = group * WINDOW
    out = dot(attended[...].reshape(rows, D), proj[...])
    hidden[...] = tokens[...] + out.reshape(group, WINDOW, D)


def feed_kernel(
    place, hidden, cotangent, gains, proj, attended,
    wide1, wide2, wide3, wide4, down1, down2, down3, down4,
    output, d_hidden, d_out, gain_grad, kept, sent,
    wide, down, all_normed, all_inner, all_d_both, all_dy, all_d_attn,
):
    laid(place, (wide1, wide2, wide3, wide4), wide, D // SHARDS)
    laid(place, (down1, down2, down3, down4), down, FF // SHARDS, D // SHARDS)
    here = pl.ds(pl.multiple_of(pl.program_id(0) * GROUP * WINDOW, GROUP * WINDOW), GROUP * WINDOW)
    normed, inner, d_both = all_normed.at[here], all_inner.at[here], all_d_both.at[here]
    low_cotangent, d_attn = all_dy.at[here], all_d_attn.at[here]
    rows = GROUP * WINDOW
    state = hidden[...].reshape(rows, D)
    gain = gains[1:2, :]
    xhat, inverse = normalised(state)
    low = (xhat * gain).astype(LOW)
    normed[...] = low
    above = cotangent[...].reshape(rows, D)
    dy = above.astype(LOW)
    low_cotangent[...] = dy
    start = 0
    while start < FF:
        size = min(256, FF - start)
        cols = slice(start, start + size)
        other = slice(FF + start, FF + start + size)
        gate = dot(low, wide[:, cols])
        upward = dot(low, wide[:, other])
        d_inner = dot(dy, down[cols, :], ((1,), (1,)))
        area = 0.5 + 0.5 * lax.erf(gate * (0.5**0.5))
        shaped = gate * area
        slope = area + gate * (jnp.exp(-0.5 * gate * gate) * 0.3989422804014327)
        inner[:, cols] = (shaped * upward).astype(LOW)
        d_both[:, cols] = (d_inner * upward * slope).astype(LOW)
        d_both[:, other] = (d_inner * shaped).astype(LOW)
        start += size
    output[...] = (state + dot(inner[...], down[...])).reshape(GROUP, WINDOW, D)
    d_normed = dot(d_both[...], wide[...], ((1,), (1,)))
    part = jnp.sum(d_normed * xhat, axis=0, keepdims=True)

    @pl.when(pl.program_id(0) == 0)
    def _():
        gain_grad[...] = part

    @pl.when(pl.program_id(0) > 0)
    def _():
        gain_grad[...] += part

    back = above + normalised_back(d_normed, gain, xhat, inverse)
    d_hidden[...] = back.reshape(GROUP, WINDOW, D)
    back = back.astype(LOW)
    d_attn[...] = back
    d_out[...] = dot(back, proj[...], ((1,), (1,))).astype(LOW).reshape(GROUP, WINDOW, D)

    @pl.when(pl.program_id(0) == pl.num_programs(0) - 1)
    def _():
        first_rows = ((0,), (0,))
        every = slice(0, D)
        size = D // 2
        for start in range(0, D, size):
            lanes = slice(start, start + size)
            for third in range(3):
                grad = dot(all_normed[:, lanes], all_d_both[:, third * D : (third + 1) * D], first_rows)
                shipped_rows(place, kept, sent, start, D // SHARDS, third * D // SHARDS, every, grad)
            grad = dot(attended[:, lanes], all_d_attn[...], first_rows)
            shipped_rows(place, kept, sent, start, D // SHARDS, 3 * D // SHARDS, every, grad)
        for start in range(0, FF, size):
            grad = dot(all_inner[:, start : start + size], all_dy[...], first_rows)
            shipped_rows(place, kept, sent, start, FF // SHARDS, D, every, grad)


def attend_back_kernel(
    place, query, keyval, probs, d_out, weight, cosine, sine, normed_ext, gains, gain_grad2,
    d_left, d_right, d_normed, kept, sent,
    all_query, all_keyval, gain_grad1,
):
    step = pl.program_id(0)
    mine = slice(HALF, HALF + WINDOW)
    cos, sin = cosine[mine], sine[mine]
    here = pl.ds(pl.multiple_of(step * GROUP * WINDOW, GROUP * WINDOW), GROUP * WINDOW)
    d_query = all_query.at[here]
    here = pl.ds(pl.multiple_of(step * GROUP * SPAN, GROUP * SPAN), GROUP * SPAN)
    d_keyval = all_keyval.at[here]
    for one in range(GROUP):
        short = slice(one * WINDOW, (one + 1) * WINDOW)
        long = slice(one * SPAN, (one + 1) * SPAN)
        for p in range(PAIRS):
            asked = by_head(query[one, :, pair(p)])
            key = keyval[one, :, pair(p)]
            grad = by_head(d_out[one, :, pair(p)])
            low_prob = probs[one, p]
            prob = low_prob.astype(WIDE)
            d_prob = dot(keyval[one, :, pair(p, D)], grad, ((1,), (1,)))
            delta = jnp.sum(prob * d_prob, axis=0, keepdims=True)
            d_score = (prob * (d_prob - delta)).astype(LOW)
            d_q = side_by_side(dot(d_score, key, ((0,), (0,)))) * HEAD**-0.5
            d_query[short, pair(p)] = turned_back(d_q, cos, sin).astype(LOW)
            d_k = dot(d_score, asked)
            d_keyval[long, pair(p)] = turned_back(d_k, cosine[...], sine[...]).astype(LOW)
            d_v = dot(low_prob, grad)
            d_keyval[long, pair(p, D)] = d_v.astype(LOW)
    both = dot(d_keyval[...], weight[:, D:], ((1,), (1,)))
    own = dot(d_query[...], weight[:, :D], ((1,), (1,)))
    total = jnp.zeros((1, D), WIDE)
    for one in range(GROUP):
        part = both[one * SPAN : (one + 1) * SPAN]
        inside = own[one * WINDOW : (one + 1) * WINDOW]
        rows = normed_ext[step * GROUP + one].astype(WIDE)
        total += jnp.sum(part * rows, axis=0, keepdims=True)
        total += jnp.sum(inside * rows[mine], axis=0, keepdims=True)
        d_left[one] = part[:HALF].astype(LOW)
        d_right[one] = part[HALF + WINDOW :].astype(LOW)
        d_normed[one] = part[mine] + inside

    @pl.when(step == 0)
    def _():
        gain_grad1[...] = total

    @pl.when(step > 0)
    def _():
        gain_grad1[...] += total

    @pl.when(step == pl.num_programs(0) - 1)
    def _():
        first_rows = ((0,), (0,))
        sequences = normed_ext.shape[0]
        size = D // 2
        for start in range(0, D, size):
            lanes = slice(start, start + size)
            rows = normed_ext[:, mine, lanes].reshape(sequences * WINDOW, size)
            grad = dot(rows, all_query[...], first_rows)
            shipped_rows(place, kept, sent, start, D // SHARDS, 0, slice(0, D), grad)
            rows = normed_ext[:, :, lanes].reshape(sequences * SPAN, size)
            for part in range(2):
                grad = dot(rows, all_keyval[:, part * D : (part + 1) * D], first_rows)
                columns = slice((part + 1) * D, (part + 2) * D)
                shipped_rows(place, kept, sent, start, D // SHARDS, 0, columns, grad)
        more = slice(D // SHARDS, D // SHARDS + GAIN_ROWS)
        first = gain_grad1[...] / gains[0:1, :]
        empty = jnp.zeros((GAIN_ROWS - 2, D), WIDE)
        both_gains = jnp.concatenate([first, gain_grad2[...], empty], axis=0).astype(LOW)
        for target in (kept, sent):
            for lead in range(2):
                target[lead, more, :] = jnp.zeros((GAIN_ROWS, 3 * D), LOW)
                target[lead, more, 3 * D // 2 : 5 * D // 2] = both_gains


def enter_kernel(tokens, gains, d_normed, from_left, from_right, d_hidden, input_grad):
    rows = GROUP * WINDOW
    xhat, inverse = normalised(tokens[...].reshape(rows, D))
    parts = []
    for one in range(GROUP):
        parts += [
            d_normed[one, :HALF] + from_left[one].astype(WIDE),
            d_normed[one, HALF:] + from_right[one].astype(WIDE),
        ]
    back = normalised_back(jnp.concatenate(parts, axis=0), gains[0:1, :], xhat, inverse)
    input_grad[...] = d_hidden[...] + back.reshape(GROUP, WINDOW, D)


def whole(shape):
    return pl.BlockSpec(shape, lambda i: (0,) * len(shape))


def once(shape):
    return pl.BlockSpec(shape, lambda i: (0,) * len(shape), pipeline_mode=pl.Buffered(1))


def once_rows(rows):
    return lambda shape: pl.BlockSpec((rows, shape[1]), lambda i: (0, 0), pipeline_mode=pl.Buffered(1))


def scalar(shape):
    return pl.BlockSpec(memory_space=pltpu.SMEM)


def blocked(shape):
    return pl.BlockSpec((GROUP,) + tuple(shape[1:]), lambda i: (i,) + (0,) * (len(shape) - 1))


def blocked_by(count):
    return lambda shape: pl.BlockSpec((count,) + tuple(shape[1:]), lambda i: (i,) + (0,) * (len(shape) - 1))


def called(kernel, sequences, operands, results, limit, scratch=(), group=GROUP):
    arrays = [array for array, _ in operands]
    return pl.pallas_call(
        kernel,
        grid=(sequences // group,),
        in_specs=[spec(array.shape) for array, spec in operands],
        out_specs=[spec(shape) for shape, _, spec in results],
        out_shape=[jax.ShapeDtypeStruct(shape, kind) for shape, kind, _ in results],
        scratch_shapes=list(scratch),
        compiler_params=pltpu.CompilerParams(
            dimension_semantics=("arbitrary",), vmem_limit_bytes=limit * MIB
        ),
        cost_estimate=pl.CostEstimate(flops=1000, bytes_accessed=1000, transcendentals=0),
    )(*arrays)


def swapped(value, axis, bit):
    count = lax.axis_size(axis)
    return lax.ppermute(value, axis, [(i, i ^ bit) for i in range(count)])


def exchanged(steps, carried=(), beside=None):
    kept, sent = [], []
    for how, value, axis, bit, dim in steps:
        if how == "lead":
            kept.append(value[0])
            value = value[1]
        elif how == "fold":
            side = (lax.axis_index(axis) // bit) % 2
            size = value.shape[dim] // 2
            kept.append(lax.dynamic_slice_in_dim(value, side * size, size, axis=dim))
            value = lax.dynamic_slice_in_dim(value, (1 - side) * size, size, axis=dim)
        else:
            kept.append(None)
        sent.append(value)
    held = lax.optimization_barrier(tuple(sent) + tuple(carried))
    sent, carried = held[: len(sent)], held[len(sent) :]
    got = []
    for (how, _, axis, bit, _), value in zip(steps, sent):
        got.append(lax.ppermute(value, axis, bit) if how == "send" else swapped(value, axis, bit))
    if beside is not None:
        carried = beside(*carried)
    held = lax.optimization_barrier(tuple(got) + tuple(carried))
    got, carried = held[: len(got)], held[len(got) :]
    results = []
    for (how, _, axis, bit, dim), mine, own, other in zip(steps, kept, sent, got):
        if how in ("fold", "lead"):
            other = (mine.astype(WIDE) + other.astype(WIDE)).astype(LOW)
        elif how == "full":
            other = (own.astype(WIDE) + other.astype(WIDE)).astype(LOW)
        elif how == "join":
            side = (lax.axis_index(axis) // bit) % 2
            low = jnp.where(side == 0, own, other)
            high = jnp.where(side == 0, other, own)
            other = jnp.concatenate([low, high], axis=dim)
        results.append(other)
    return results, carried


def far_sum(value):
    bit = 8
    while bit < lax.axis_size("seq"):
        ((value,), _) = exchanged([("full", value, "seq", bit, 0)])
        bit *= 2
    return value


def adamw(master, grad, first, second, rate):
    moment = 0.9 * first + 0.1 * grad
    square = 0.98 * second + 0.02 * grad * grad
    fixed_first = moment / (1.0 - 0.9**STEP)
    fixed_second = square / (1.0 - 0.98**STEP)
    update = fixed_first / (jnp.sqrt(fixed_second) + 1e-06) + 1e-05 * master
    return (master - rate * update, moment, square)


def in_order(pieces):
    place = lax.axis_index("wshard")
    size = pieces[0].shape[0]
    total = jnp.zeros((size * len(pieces),) + pieces[0].shape[1:], pieces[0].dtype)
    for known, piece in enumerate(pieces):
        total = lax.dynamic_update_slice_in_dim(total, piece, (place ^ known) * size, 0)
    return total


def tables(base, total):
    places = base - HALF + jnp.arange(SPAN, dtype=jnp.int32)
    freqs = 10000.0 ** (-jnp.arange(0, HEAD, 2).astype(WIDE) / HEAD)
    angles = places.astype(WIDE)[:, None] * freqs[None, :]
    cosine, sine = jnp.cos(angles), jnp.sin(angles)
    cosine = jnp.concatenate([cosine] * 4, axis=1)
    sine = jnp.concatenate([-sine, sine] * 2, axis=1)
    row = jnp.arange(WINDOW)[None, :]
    col = jnp.arange(SPAN)[:, None]
    seen = (col >= row) & (col <= row + WINDOW) & (places >= 0)[:, None] & (places < total)[:, None]
    return cosine, sine, jnp.where(seen, 3e38, -1e30).astype(WIDE)


def on_device(
    tokens,
    cotangent,
    qkv_master,
    proj_master,
    wide_master,
    down_master,
    norm_gains,
    qkv_first,
    proj_first,
    wide_first,
    down_first,
    gains_first,
    qkv_second,
    proj_second,
    wide_second,
    down_second,
    gains_second,
):
    sequences, local_len, width = tokens.shape
    blocks = lax.axis_size("seq")
    base = lax.axis_index("seq") * local_len
    to_right = [(i, i + 1) for i in range(blocks - 1)]
    to_left = [(i + 1, i) for i in range(blocks - 1)]

    shard_rows = qkv_master.shape[0]
    own_gains = jnp.pad(norm_gains, ((0, 14), (0, qkv_master.shape[1] - norm_gains.shape[1])))
    first = jnp.concatenate([qkv_master.astype(LOW), own_gains.astype(LOW)], axis=0)
    ends = normalised(tokens)[0].astype(LOW)
    some = sequences * 5 // 8
    tails, heads = ends[:, local_len - HALF :], ends[:, :HALF]
    (first_y, first_core, left1, right1), _ = exchanged(
        [
            ("pair", first, "wshard", 2, 0),
            ("pair", first, "wshard", 1, 0),
            ("send", tails[:some], "seq", to_right, 0),
            ("send", heads[:some], "seq", to_left, 0),
        ]
    )
    rest = jnp.concatenate([proj_master.astype(LOW), down_master.astype(LOW)], axis=0)
    ((first_both,), _) = exchanged([("pair", first_y, "wshard", 1, 0)])
    firsts_known = (first, first_core, first_y, first_both)
    gains = in_order([piece[shard_rows : shard_rows + 2, : norm_gains.shape[1]].T for piece in firsts_known])
    gains = gains.T.astype(WIDE)
    cosine, sine, cap = tables(base, local_len * blocks)
    place = lax.axis_index("wshard").astype(jnp.int32).reshape(1)
    cells = sequences * local_len
    spread = (sequences, local_len, D)
    halo = (sequences, HALF, D)
    def projection(table):
        return called(
            project_kernel,
            sequences,
            [(place, scalar), (tokens, blocked), (gains, whole)]
            + [(piece, once_rows(shard_rows)) for piece in firsts_known]
            + [(table, whole), (sine, whole)],
            [
                (spread, LOW, blocked),
                (spread, LOW, blocked),
                ((sequences, local_len, 2 * D), LOW, blocked),
                ((D, 3 * D), LOW, whole),
            ],
            48,
        )

    (rest_y, rest_core, left2, right2), (normed, query, keyval, qkv) = exchanged(
        [
            ("pair", rest, "wshard", 2, 0),
            ("pair", rest, "wshard", 1, 0),
            ("send", tails[some:], "seq", to_right, 0),
            ("send", heads[some:], "seq", to_left, 0),
        ],
        (cosine,),
        projection,
    )
    left = jnp.concatenate([left1, left2], axis=0)
    right = jnp.concatenate([right1, right2], axis=0)
    ((rest_both,), _) = exchanged([("pair", rest_y, "wshard", 1, 0)])
    several = blocked_by(2 * GROUP)

    def attention(table, last):
        return called(
            attend_kernel,
            sequences,
            [
                (place, scalar), (tokens, several), (normed, several), (left, several), (right, several),
                (gains, whole), (query, several), (keyval, several), (qkv, once),
            ]
            + [(piece, once_rows(proj_master.shape[0])) for piece in (rest, rest_core, rest_y, last)]
            + [(table, whole), (sine, whole), (cap, whole)],
            [
                ((sequences, SPAN, D), LOW, several),
                ((sequences, SPAN, 2 * D), LOW, several),
                ((sequences, PAIRS, SPAN, SPAN), LOW, several),
                (spread, LOW, several),
                (spread, WIDE, several),
                ((D, D), LOW, whole),
            ],
            60,
            group=2 * GROUP,
        )

    low_wide = wide_master.astype(LOW)
    (wide_y, wide_core), attention_results = exchanged(
        [("pair", low_wide, "wshard", 2, 0), ("pair", low_wide, "wshard", 1, 0)],
        (cosine, rest_both),
        attention,
    )
    rests = (rest, rest_core, rest_y, rest_both)
    normed_ext, keyval_ext, probs, attended, hidden, proj = attention_results
    ((wide_both,), _) = exchanged([("pair", wide_y, "wshard", 1, 0)])
    wides = (low_wide, wide_core, wide_y, wide_both)
    rest_rows = 3 * shard_rows + rest.shape[0]
    shares = (2, rest_rows, D)
    layer_output, d_hidden, d_out, gain_grad2, rest_kept, rest_sent = called(
        feed_kernel,
        sequences,
        [
            (place, scalar), (hidden, blocked), (cotangent, blocked), (gains, whole),
            (proj, once), (attended.reshape(cells, D), once),
        ]
        + [(piece, once) for piece in wides + rests],
        [
            (spread, WIDE, blocked),
            (spread, WIDE, blocked),
            (spread, LOW, blocked),
            ((1, D), WIDE, whole),
            (shares, LOW, whole),
            (shares, LOW, whole),
        ],
        60,
        [
            pltpu.VMEM((D, 2 * FF), LOW),
            pltpu.VMEM((FF, D), LOW),
            pltpu.VMEM((cells, D), LOW),
            pltpu.VMEM((cells, FF), LOW),
            pltpu.VMEM((cells, 2 * FF), LOW),
            pltpu.VMEM((cells, D), LOW),
            pltpu.VMEM((cells, D), LOW),
        ],
    )

    def summed(kept, got):
        return (kept.astype(WIDE) + got.astype(WIDE)).astype(LOW)

    ((rest_got,), _) = exchanged([("pair", rest_sent, "wshard", 1, 0)])
    shares = (2, shard_rows + GAIN_ROWS, 3 * D)
    (rest_last,), back_results = exchanged(
        [("pair", summed(rest_kept[1], rest_got[1]), "wshard", 2, 0)],
        (cosine,),
        lambda table: called(
            attend_back_kernel,
            sequences,
            [
                (place, scalar), (query, blocked), (keyval_ext, blocked), (probs, blocked),
                (d_out, blocked), (qkv, once), (table, whole), (sine, whole), (normed_ext, once),
                (gains, whole), (gain_grad2, whole),
            ],
            [
                (halo, LOW, blocked),
                (halo, LOW, blocked),
                (spread, WIDE, blocked),
                (shares, LOW, whole),
                (shares, LOW, whole),
            ],
            56,
            [
                pltpu.VMEM((cells, D), LOW),
                pltpu.VMEM((2 * cells, 2 * D), LOW),
                pltpu.VMEM((1, D), WIDE),
            ],
        ),
    )
    rest_grad = (rest_kept[0].astype(WIDE) + rest_got[0].astype(WIDE) + rest_last.astype(WIDE)).astype(LOW)
    near, far = rest_grad[:, : D // 2], rest_grad[:, D // 2 :]
    d_left, d_right, d_normed, kept, sent = back_results
    (got, near, far), _ = exchanged(
        [
            ("pair", sent, "wshard", 1, 0),
            ("fold", near, "seq", 1, 0),
            ("fold", far, "seq", 2, 0),
        ]
    )
    both_grad = summed(kept, got)
    half = 3 * D // 2
    one_grad, two_grad = both_grad[:, :shard_rows, :half], both_grad[:, :, half:]

    cuts = (0, sequences * 3 // 8, sequences * 3 // 4, sequences)
    from_left, from_right = [], []

    def round_of(steps, cut=None):
        if cut is not None:
            rows = slice(cuts[cut], cuts[cut + 1])
            steps = steps + [
                ("send", d_right[rows], "seq", to_right, 0),
                ("send", d_left[rows], "seq", to_left, 0),
            ]
        results, _ = exchanged(steps)
        if cut is not None:
            from_right.append(results.pop())
            from_left.append(results.pop())
        return results

    near, far, one_grad, two_grad = round_of(
        [
            ("fold", near, "seq", 2, 0),
            ("fold", far, "seq", 4, 0),
            ("lead", one_grad, "wshard", 2, 0),
            ("fold", two_grad, "seq", 2, 1),
        ],
        0,
    )
    near, far, one_grad, two_grad = round_of(
        [
            ("full", near, "seq", 4, 0),
            ("full", far, "seq", 1, 0),
            ("fold", one_grad, "seq", 2, 0),
            ("lead", two_grad, "wshard", 2, 0),
        ],
        1,
    )
    near, far = far_sum(near), far_sum(far)
    near, far, one_grad, two_grad = round_of(
        [
            ("join", near, "seq", 2, 0),
            ("join", far, "seq", 4, 0),
            ("full", one_grad, "seq", 4, 0),
            ("full", two_grad, "seq", 1, 0),
        ],
        2,
    )
    near, far, one_grad, two_grad = round_of(
        [
            ("join", near, "seq", 1, 0),
            ("join", far, "seq", 2, 0),
            ("full", one_grad, "seq", 1, 0),
            ("full", two_grad, "seq", 4, 0),
        ]
    )
    rest_grad = jnp.concatenate([near, far], axis=1)
    input_grad = called(
        enter_kernel,
        sequences,
        [
            (tokens, blocked), (gains, whole), (d_normed, blocked),
            (jnp.concatenate(from_left, axis=0), blocked),
            (jnp.concatenate(from_right, axis=0), blocked),
            (d_hidden, blocked),
        ],
        [(spread, WIDE, blocked)],
        32,
    )[0]
    one_grad, two_grad = far_sum(one_grad), far_sum(two_grad)
    one_grad, two_grad = round_of([("join", one_grad, "seq", 2, 0), ("join", two_grad, "seq", 2, 0)])
    rest_grad, one_grad, two_grad = (grad.astype(WIDE) for grad in (rest_grad, one_grad, two_grad))
    gains_sum = lax.dynamic_slice_in_dim(
        two_grad[shard_rows : shard_rows + 2],
        lax.axis_index("wshard") * norm_gains.shape[1],
        norm_gains.shape[1],
        axis=1,
    )
    wide_parts = [rest_grad[third * shard_rows : (third + 1) * shard_rows] for third in range(3)]
    owned_grads = (
        jnp.concatenate([one_grad, two_grad[:shard_rows]], axis=1),
        rest_grad[3 * shard_rows : 4 * shard_rows],
        jnp.concatenate(wide_parts, axis=1),
        rest_grad[4 * shard_rows :],
        gains_sum,
    )
    rates = (
        2.0 * D ** (-0.5),
        2.0 * max(D // WINDOW, 1) ** (-0.5),
        2.0 * D ** (-0.5),
        2.0 * FF ** (-0.5),
        1.0,
    )
    masters = (qkv_master, proj_master, wide_master, down_master, norm_gains)
    firsts = (qkv_first, proj_first, wide_first, down_first, gains_first)
    seconds = (qkv_second, proj_second, wide_second, down_second, gains_second)
    results = [adamw(masters[i], owned_grads[i], firsts[i], seconds[i], rates[i]) for i in range(5)]
    return (
        layer_output,
        input_grad,
        results[0][0],
        results[1][0],
        results[2][0],
        results[3][0],
        results[4][0],
        results[0][1],
        results[1][1],
        results[2][1],
        results[3][1],
        results[4][1],
        results[0][2],
        results[1][2],
        results[2][2],
        results[3][2],
        results[4][2],
    )


def solution(mesh):
    placed = (
        P("wshard", "seq", None),
        P("wshard", "seq", None),
        P("wshard", None),
        P("wshard", None),
        P("wshard", None),
        P("wshard", None),
        P(None, "wshard"),
        P("wshard", None),
        P("wshard", None),
        P("wshard", None),
        P("wshard", None),
        P(None, "wshard"),
        P("wshard", None),
        P("wshard", None),
        P("wshard", None),
        P("wshard", None),
        P(None, "wshard"),
    )
    return jax.shard_map(
        on_device,
        mesh=mesh,
        in_specs=placed,
        out_specs=(
            P("wshard", "seq", None),
            P("wshard", "seq", None),
            P("wshard", None),
            P("wshard", None),
            P("wshard", None),
            P("wshard", None),
            P(None, "wshard"),
            P("wshard", None),
            P("wshard", None),
            P("wshard", None),
            P("wshard", None),
            P(None, "wshard"),
            P("wshard", None),
            P("wshard", None),
            P("wshard", None),
            P("wshard", None),
            P(None, "wshard"),
        ),
        check_vma=False,
    )
```

```python
import jax
import jax.numpy as jnp
from jax import lax
from jax.experimental import pallas as pl
from jax.experimental.pallas import tpu as pltpu
from jax.sharding import PartitionSpec as P

D = 768
HEADS = 12
HEAD = 64
FF = 1152
WINDOW = 128
STEP = 10
HALF = WINDOW // 2
SPAN = 2 * WINDOW
LANES = 128
PAIRS = D // LANES
GROUP = 2
LOW = jnp.bfloat16
WIDE = jnp.float32
SHARDS = 4
GAIN_ROWS = 32
MIB = 1 << 20


def dot(one, other, dims=((1,), (0,))):
    return lax.dot_general(one, other, (dims, ((), ())), preferred_element_type=WIDE)


def normalised(value):
    centred = value - jnp.mean(value, axis=-1, keepdims=True)
    inverse = lax.rsqrt(jnp.mean(centred * centred, axis=-1, keepdims=True) + 1e-05)
    return centred * inverse, inverse


def normalised_back(d_normed, gain, xhat, inverse):
    d_xhat = d_normed * gain
    mean = jnp.mean(d_xhat, axis=-1, keepdims=True)
    slope = jnp.mean(d_xhat * xhat, axis=-1, keepdims=True)
    return inverse * (d_xhat - mean - xhat * slope)


def lane_of(rows):
    return lax.broadcasted_iota(jnp.int32, (rows, LANES), 1)


def half_swapped(value):
    first = lane_of(value.shape[0]) % HEAD < HEAD // 2
    ahead = pltpu.roll(value, LANES - HEAD // 2, 1)
    behind = pltpu.roll(value, HEAD // 2, 1)
    return jnp.where(first, ahead, behind)


def turned(value, cosine, sine):
    return value * cosine + half_swapped(value) * sine


def turned_back(value, cosine, sine):
    return value * cosine - half_swapped(value) * sine


def by_head(value):
    first = lane_of(value.shape[0]) < HEAD
    zero = jnp.zeros_like(value)
    return jnp.concatenate([jnp.where(first, value, zero), jnp.where(first, zero, value)], axis=0)


def side_by_side(value):
    rows = value.shape[0] // 2
    return jnp.where(lane_of(rows) < HEAD, value[:rows], value[rows:])


def pair(index, start=0):
    return slice(start + index * LANES, start + (index + 1) * LANES)


def laid(place, pieces, target, size, start=0):
    @pl.when(pl.program_id(0) == 0)
    def _():
        for known, piece in enumerate(pieces):
            row = pl.multiple_of((place[0] ^ known) * size, 16)
            target[pl.ds(row, size), :] = piece[start : start + size, :]


def shipped(place, kept, sent, shard, row, columns, value):
    value = value.astype(LOW)
    lead = (place[0] // 2) ^ (shard // 2)
    mine = place[0] % 2 == shard % 2

    @pl.when(mine)
    def _():
        kept[lead, row : row + value.shape[0], columns] = value

    @pl.when(jnp.logical_not(mine))
    def _():
        sent[lead, row : row + value.shape[0], columns] = value


def shipped_rows(place, kept, sent, start, size, row, columns, value):
    end = start + value.shape[0]
    for shard in range(SHARDS):
        low, high = max(start, shard * size), min(end, (shard + 1) * size)
        if low < high:
            part = value[low - start : high - start]
            shipped(place, kept, sent, shard, row + low - shard * size, columns, part)


def project_kernel(
    place, tokens, gains, one_piece, two_piece, three_piece, four_piece, cosine, sine,
    normed, query, keyval, weight,
):
    laid(place, (one_piece, two_piece, three_piece, four_piece), weight, D // SHARDS)
    rows = GROUP * WINDOW
    xhat, _ = normalised(tokens[...].reshape(rows, D))
    low = (xhat * gains[0:1, :]).astype(LOW)
    normed[...] = low.reshape(GROUP, WINDOW, D)
    mine = slice(HALF, HALF + WINDOW)
    cos, sin = cosine[mine], sine[mine]
    out = dot(low, weight[:, :D])
    for one in range(GROUP):
        for p in range(PAIRS):
            part = out[one * WINDOW : (one + 1) * WINDOW, pair(p)]
            query[one, :, pair(p)] = (turned(part, cos, sin) * HEAD**-0.5).astype(LOW)
    out = dot(low, weight[:, D : 2 * D])
    for one in range(GROUP):
        for p in range(PAIRS):
            part = out[one * WINDOW : (one + 1) * WINDOW, pair(p)]
            keyval[one, :, pair(p)] = turned(part, cos, sin).astype(LOW)
    out = dot(low, weight[:, 2 * D :])
    keyval[:, :, D:] = out.astype(LOW).reshape(GROUP, WINDOW, D)


def attend_kernel(
    place, tokens, normed, left, right, gains, query, keyval, weight,
    one_piece, two_piece, three_piece, four_piece, cosine, sine, cap,
    normed_ext, keyval_ext, probs, attended, hidden, proj,
):
    group = tokens.shape[0]
    laid(place, (one_piece, two_piece, three_piece, four_piece), proj, D // SHARDS)
    gain = gains[0:1, :]
    ends = []
    for one in range(group):
        low_left = (left[one].astype(WIDE) * gain).astype(LOW)
        low_right = (right[one].astype(WIDE) * gain).astype(LOW)
        normed_ext[one, :HALF] = low_left
        normed_ext[one, HALF : HALF + WINDOW] = normed[one]
        normed_ext[one, HALF + WINDOW :] = low_right
        ends += [low_left, low_right]
    ends = jnp.concatenate(ends, axis=0)
    cos = jnp.concatenate([cosine[:HALF], cosine[HALF + WINDOW :]], axis=0)
    sin = jnp.concatenate([sine[:HALF], sine[HALF + WINDOW :]], axis=0)
    keys = dot(ends, weight[:, D : 2 * D])
    values = dot(ends, weight[:, 2 * D :]).astype(LOW)
    for one in range(group):
        keyval_ext[one, HALF : HALF + WINDOW] = keyval[one]
        rows = slice(one * WINDOW, (one + 1) * WINDOW)
        keyval_ext[one, :HALF, D:] = values[rows][:HALF]
        keyval_ext[one, HALF + WINDOW :, D:] = values[rows][HALF:]
        for p in range(PAIRS):
            key = turned(keys[rows, pair(p)], cos, sin).astype(LOW)
            keyval_ext[one, :HALF, pair(p)] = key[:HALF]
            keyval_ext[one, HALF + WINDOW :, pair(p)] = key[HALF:]
    limit = jnp.concatenate([cap[...], cap[...]], axis=1)
    for one in range(group):
        for p in range(PAIRS):
            asked = by_head(query[one, :, pair(p)])
            scores = dot(keyval_ext[one, :, pair(p)], asked, ((1,), (1,)))
            scores = jnp.minimum(scores, limit)
            top = jnp.max(scores, axis=0, keepdims=True)
            grown = jnp.exp(scores - top)
            prob = grown * (1.0 / jnp.sum(grown, axis=0, keepdims=True))
            prob = prob.astype(LOW)
            probs[one, p] = prob
            found = dot(prob, keyval_ext[one, :, pair(p, D)], ((0,), (0,)))
            attended[one, :, pair(p)] = side_by_side(found).astype(LOW)
    rows = group * WINDOW
    out = dot(attended[...].reshape(rows, D), proj[...])
    hidden[...] = tokens[...] + out.reshape(group, WINDOW, D)


def feed_kernel(
    place, hidden, cotangent, gains, proj, attended,
    wide1, wide2, wide3, wide4, down1, down2, down3, down4,
    output, d_hidden, d_out, gain_grad, kept, sent,
    wide, down, all_normed, all_inner, all_d_both, all_dy, all_d_attn,
):
    laid(place, (wide1, wide2, wide3, wide4), wide, D // SHARDS)
    laid(place, (down1, down2, down3, down4), down, FF // SHARDS, D // SHARDS)
    here = pl.ds(pl.multiple_of(pl.program_id(0) * GROUP * WINDOW, GROUP * WINDOW), GROUP * WINDOW)
    normed, inner, d_both = all_normed.at[here], all_inner.at[here], all_d_both.at[here]
    low_cotangent, d_attn = all_dy.at[here], all_d_attn.at[here]
    rows = GROUP * WINDOW
    state = hidden[...].reshape(rows, D)
    gain = gains[1:2, :]
    xhat, inverse = normalised(state)
    low = (xhat * gain).astype(LOW)
    normed[...] = low
    above = cotangent[...].reshape(rows, D)
    dy = above.astype(LOW)
    low_cotangent[...] = dy
    start = 0
    while start < FF:
        size = min(256, FF - start)
        cols = slice(start, start + size)
        other = slice(FF + start, FF + start + size)
        gate = dot(low, wide[:, cols])
        upward = dot(low, wide[:, other])
        d_inner = dot(dy, down[cols, :], ((1,), (1,)))
        area = 0.5 + 0.5 * lax.erf(gate * (0.5**0.5))
        shaped = gate * area
        slope = area + gate * (jnp.exp(-0.5 * gate * gate) * 0.3989422804014327)
        inner[:, cols] = (shaped * upward).astype(LOW)
        d_both[:, cols] = (d_inner * upward * slope).astype(LOW)
        d_both[:, other] = (d_inner * shaped).astype(LOW)
        start += size
    output[...] = (state + dot(inner[...], down[...])).reshape(GROUP, WINDOW, D)
    d_normed = dot(d_both[...], wide[...], ((1,), (1,)))
    part = jnp.sum(d_normed * xhat, axis=0, keepdims=True)

    @pl.when(pl.program_id(0) == 0)
    def _():
        gain_grad[...] = part

    @pl.when(pl.program_id(0) > 0)
    def _():
        gain_grad[...] += part

    back = above + normalised_back(d_normed, gain, xhat, inverse)
    d_hidden[...] = back.reshape(GROUP, WINDOW, D)
    back = back.astype(LOW)
    d_attn[...] = back
    d_out[...] = dot(back, proj[...], ((1,), (1,))).astype(LOW).reshape(GROUP, WINDOW, D)

    @pl.when(pl.program_id(0) == pl.num_programs(0) - 1)
    def _():
        first_rows = ((0,), (0,))
        every = slice(0, D)
        size = D // 2
        for start in range(0, D, size):
            lanes = slice(start, start + size)
            for third in range(3):
                grad = dot(all_normed[:, lanes], all_d_both[:, third * D : (third + 1) * D], first_rows)
                shipped_rows(place, kept, sent, start, D // SHARDS, third * D // SHARDS, every, grad)
            grad = dot(attended[:, lanes], all_d_attn[...], first_rows)
            shipped_rows(place, kept, sent, start, D // SHARDS, 3 * D // SHARDS, every, grad)
        for start in range(0, FF, size):
            grad = dot(all_inner[:, start : start + size], all_dy[...], first_rows)
            shipped_rows(place, kept, sent, start, FF // SHARDS, D, every, grad)


def back_step(
    query, keyval, probs, d_out, weight, cosine, sine, normed_ext, start,
    d_left, d_right, d_normed, all_query, all_keyval, gain_grad,
):
    step = pl.program_id(0)
    mine = slice(HALF, HALF + WINDOW)
    cos, sin = cosine[mine], sine[mine]
    here = pl.ds(pl.multiple_of(step * GROUP * WINDOW, GROUP * WINDOW), GROUP * WINDOW)
    d_query = all_query.at[here]
    here = pl.ds(pl.multiple_of(step * GROUP * SPAN, GROUP * SPAN), GROUP * SPAN)
    d_keyval = all_keyval.at[here]
    for one in range(GROUP):
        short = slice(one * WINDOW, (one + 1) * WINDOW)
        long = slice(one * SPAN, (one + 1) * SPAN)
        for p in range(PAIRS):
            asked = by_head(query[one, :, pair(p)])
            key = keyval[one, :, pair(p)]
            grad = by_head(d_out[one, :, pair(p)])
            low_prob = probs[one, p]
            prob = low_prob.astype(WIDE)
            d_prob = dot(keyval[one, :, pair(p, D)], grad, ((1,), (1,)))
            delta = jnp.sum(prob * d_prob, axis=0, keepdims=True)
            d_score = (prob * (d_prob - delta)).astype(LOW)
            d_q = side_by_side(dot(d_score, key, ((0,), (0,)))) * HEAD**-0.5
            d_query[short, pair(p)] = turned_back(d_q, cos, sin).astype(LOW)
            d_k = dot(d_score, asked)
            d_keyval[long, pair(p)] = turned_back(d_k, cosine[...], sine[...]).astype(LOW)
            d_v = dot(low_prob, grad)
            d_keyval[long, pair(p, D)] = d_v.astype(LOW)
    both = dot(d_keyval[...], weight[:, D:], ((1,), (1,)))
    own = dot(d_query[...], weight[:, :D], ((1,), (1,)))
    total = jnp.zeros((1, D), WIDE)
    for one in range(GROUP):
        part = both[one * SPAN : (one + 1) * SPAN]
        inside = own[one * WINDOW : (one + 1) * WINDOW]
        rows = normed_ext[start + one].astype(WIDE)
        total += jnp.sum(part * rows, axis=0, keepdims=True)
        total += jnp.sum(inside * rows[mine], axis=0, keepdims=True)
        d_left[one] = part[:HALF].astype(LOW)
        d_right[one] = part[HALF + WINDOW :].astype(LOW)
        d_normed[one] = part[mine] + inside

    @pl.when(step == 0)
    def _():
        gain_grad[...] = total

    @pl.when(step > 0)
    def _():
        gain_grad[...] += total


def first_back_kernel(
    query, keyval, probs, d_out, weight, cosine, sine, normed_ext,
    d_left, d_right, d_normed, all_query, all_keyval, gain_grad,
):
    back_step(
        query, keyval, probs, d_out, weight, cosine, sine, normed_ext, 0,
        d_left, d_right, d_normed, all_query, all_keyval, gain_grad,
    )


def second_back_kernel(
    place, query, keyval, probs, d_out, weight, cosine, sine, normed_ext, gains, gain_grad2,
    first_query, first_keyval, first_gain, earlier,
    d_left, d_right, d_normed, kept, sent,
    all_query, all_keyval, gain_grad1,
):
    del earlier
    mine = slice(HALF, HALF + WINDOW)
    start = normed_ext.shape[0] // 2 + pl.program_id(0) * GROUP
    back_step(
        query, keyval, probs, d_out, weight, cosine, sine, normed_ext, start,
        d_left, d_right, d_normed, all_query, all_keyval, gain_grad1,
    )

    @pl.when(pl.program_id(0) == pl.num_programs(0) - 1)
    def _():
        first_rows = ((0,), (0,))
        some = normed_ext.shape[0] // 2
        parts = ((slice(0, some), first_query, first_keyval), (slice(some, 2 * some), all_query, all_keyval))
        size = D // 2
        for start in range(0, D, size):
            lanes = slice(start, start + size)
            grad = 0.0
            for some_rows, part_query, _ in parts:
                rows = normed_ext[some_rows, mine, lanes].reshape(some * WINDOW, size)
                grad += dot(rows, part_query[...], first_rows)
            shipped_rows(place, kept, sent, start, D // SHARDS, 0, slice(0, D), grad)
            for part in range(2):
                grad = 0.0
                for some_rows, _, part_keyval in parts:
                    rows = normed_ext[some_rows, :, lanes].reshape(some * SPAN, size)
                    grad += dot(rows, part_keyval[:, part * D : (part + 1) * D], first_rows)
                columns = slice((part + 1) * D, (part + 2) * D)
                shipped_rows(place, kept, sent, start, D // SHARDS, 0, columns, grad)
        more = slice(D // SHARDS, D // SHARDS + GAIN_ROWS)
        first = (first_gain[...] + gain_grad1[...]) / gains[0:1, :]
        empty = jnp.zeros((GAIN_ROWS - 2, D), WIDE)
        both_gains = jnp.concatenate([first, gain_grad2[...], empty], axis=0).astype(LOW)
        for target in (kept, sent):
            for lead in range(2):
                target[lead, more, :] = jnp.zeros((GAIN_ROWS, 3 * D), LOW)
                target[lead, more, 3 * D // 2 : 5 * D // 2] = both_gains


def enter_kernel(tokens, gains, d_normed, from_left, from_right, d_hidden, input_grad):
    rows = GROUP * WINDOW
    xhat, inverse = normalised(tokens[...].reshape(rows, D))
    parts = []
    for one in range(GROUP):
        parts += [
            d_normed[one, :HALF] + from_left[one].astype(WIDE),
            d_normed[one, HALF:] + from_right[one].astype(WIDE),
        ]
    back = normalised_back(jnp.concatenate(parts, axis=0), gains[0:1, :], xhat, inverse)
    input_grad[...] = d_hidden[...] + back.reshape(GROUP, WINDOW, D)


def whole(shape):
    return pl.BlockSpec(shape, lambda i: (0,) * len(shape))


def once(shape):
    return pl.BlockSpec(shape, lambda i: (0,) * len(shape), pipeline_mode=pl.Buffered(1))


def once_rows(rows):
    return lambda shape: pl.BlockSpec((rows, shape[1]), lambda i: (0, 0), pipeline_mode=pl.Buffered(1))


def scalar(shape):
    return pl.BlockSpec(memory_space=pltpu.SMEM)


def blocked(shape):
    return pl.BlockSpec((GROUP,) + tuple(shape[1:]), lambda i: (i,) + (0,) * (len(shape) - 1))


def blocked_by(count):
    return lambda shape: pl.BlockSpec((count,) + tuple(shape[1:]), lambda i: (i,) + (0,) * (len(shape) - 1))


def later(steps):
    return lambda shape: pl.BlockSpec(
        (GROUP,) + tuple(shape[1:]), lambda i: (i + steps,) + (0,) * (len(shape) - 1)
    )


def anywhere(shape):
    return pl.BlockSpec(memory_space=pl.ANY)


def called(kernel, sequences, operands, results, limit, scratch=(), group=GROUP, aliases=None):
    arrays = [array for array, _ in operands]
    return pl.pallas_call(
        kernel,
        grid=(sequences // group,),
        in_specs=[spec(array.shape) for array, spec in operands],
        out_specs=[spec(shape) for shape, _, spec in results],
        out_shape=[jax.ShapeDtypeStruct(shape, kind) for shape, kind, _ in results],
        scratch_shapes=list(scratch),
        input_output_aliases=aliases or {},
        compiler_params=pltpu.CompilerParams(
            dimension_semantics=("arbitrary",), vmem_limit_bytes=limit * MIB
        ),
        cost_estimate=pl.CostEstimate(flops=1000, bytes_accessed=1000, transcendentals=0),
    )(*arrays)


def swapped(value, axis, bit):
    count = lax.axis_size(axis)
    return lax.ppermute(value, axis, [(i, i ^ bit) for i in range(count)])


def exchanged(steps, carried=(), beside=None):
    kept, sent = [], []
    for how, value, axis, bit, dim in steps:
        if how == "lead":
            kept.append(value[0])
            value = value[1]
        elif how == "fold":
            side = (lax.axis_index(axis) // bit) % 2
            size = value.shape[dim] // 2
            kept.append(lax.dynamic_slice_in_dim(value, side * size, size, axis=dim))
            value = lax.dynamic_slice_in_dim(value, (1 - side) * size, size, axis=dim)
        else:
            kept.append(None)
        sent.append(value)
    held = lax.optimization_barrier(tuple(sent) + tuple(carried))
    sent, carried = held[: len(sent)], held[len(sent) :]
    got = []
    for (how, _, axis, bit, _), value in zip(steps, sent):
        got.append(lax.ppermute(value, axis, bit) if how == "send" else swapped(value, axis, bit))
    if beside is not None:
        carried = beside(*carried)
    held = lax.optimization_barrier(tuple(got) + tuple(carried))
    got, carried = held[: len(got)], held[len(got) :]
    results = []
    for (how, _, axis, bit, dim), mine, own, other in zip(steps, kept, sent, got):
        if how in ("fold", "lead"):
            other = (mine.astype(WIDE) + other.astype(WIDE)).astype(LOW)
        elif how == "full":
            other = (own.astype(WIDE) + other.astype(WIDE)).astype(LOW)
        elif how == "join":
            side = (lax.axis_index(axis) // bit) % 2
            low = jnp.where(side == 0, own, other)
            high = jnp.where(side == 0, other, own)
            other = jnp.concatenate([low, high], axis=dim)
        results.append(other)
    return results, carried


def far_sum(value):
    bit = 8
    while bit < lax.axis_size("seq"):
        ((value,), _) = exchanged([("full", value, "seq", bit, 0)])
        bit *= 2
    return value


def adamw(master, grad, first, second, rate):
    moment = 0.9 * first + 0.1 * grad
    square = 0.98 * second + 0.02 * grad * grad
    fixed_first = moment / (1.0 - 0.9**STEP)
    fixed_second = square / (1.0 - 0.98**STEP)
    update = fixed_first / (jnp.sqrt(fixed_second) + 1e-06) + 1e-05 * master
    return (master - rate * update, moment, square)


def in_order(pieces):
    place = lax.axis_index("wshard")
    size = pieces[0].shape[0]
    total = jnp.zeros((size * len(pieces),) + pieces[0].shape[1:], pieces[0].dtype)
    for known, piece in enumerate(pieces):
        total = lax.dynamic_update_slice_in_dim(total, piece, (place ^ known) * size, 0)
    return total


def tables(base, total):
    places = base - HALF + jnp.arange(SPAN, dtype=jnp.int32)
    freqs = 10000.0 ** (-jnp.arange(0, HEAD, 2).astype(WIDE) / HEAD)
    angles = places.astype(WIDE)[:, None] * freqs[None, :]
    cosine, sine = jnp.cos(angles), jnp.sin(angles)
    cosine = jnp.concatenate([cosine] * 4, axis=1)
    sine = jnp.concatenate([-sine, sine] * 2, axis=1)
    row = jnp.arange(WINDOW)[None, :]
    col = jnp.arange(SPAN)[:, None]
    seen = (col >= row) & (col <= row + WINDOW) & (places >= 0)[:, None] & (places < total)[:, None]
    return cosine, sine, jnp.where(seen, 3e38, -1e30).astype(WIDE)


def on_device(
    tokens,
    cotangent,
    qkv_master,
    proj_master,
    wide_master,
    down_master,
    norm_gains,
    qkv_first,
    proj_first,
    wide_first,
    down_first,
    gains_first,
    qkv_second,
    proj_second,
    wide_second,
    down_second,
    gains_second,
):
    sequences, local_len, width = tokens.shape
    blocks = lax.axis_size("seq")
    base = lax.axis_index("seq") * local_len
    to_right = [(i, i + 1) for i in range(blocks - 1)]
    to_left = [(i + 1, i) for i in range(blocks - 1)]

    shard_rows = qkv_master.shape[0]
    own_gains = jnp.pad(norm_gains, ((0, 14), (0, qkv_master.shape[1] - norm_gains.shape[1])))
    first = jnp.concatenate([qkv_master.astype(LOW), own_gains.astype(LOW)], axis=0)
    ends = normalised(tokens)[0].astype(LOW)
    some = sequences * 5 // 8
    tails, heads = ends[:, local_len - HALF :], ends[:, :HALF]
    (first_y, first_core, left1, right1), _ = exchanged(
        [
            ("pair", first, "wshard", 2, 0),
            ("pair", first, "wshard", 1, 0),
            ("send", tails[:some], "seq", to_right, 0),
            ("send", heads[:some], "seq", to_left, 0),
        ]
    )
    rest = jnp.concatenate([proj_master.astype(LOW), down_master.astype(LOW)], axis=0)
    ((first_both,), _) = exchanged([("pair", first_y, "wshard", 1, 0)])
    firsts_known = (first, first_core, first_y, first_both)
    gains = in_order([piece[shard_rows : shard_rows + 2, : norm_gains.shape[1]].T for piece in firsts_known])
    gains = gains.T.astype(WIDE)
    cosine, sine, cap = tables(base, local_len * blocks)
    place = lax.axis_index("wshard").astype(jnp.int32).reshape(1)
    cells = sequences * local_len
    spread = (sequences, local_len, D)
    halo = (sequences, HALF, D)
    def projection(table):
        return called(
            project_kernel,
            sequences,
            [(place, scalar), (tokens, blocked), (gains, whole)]
            + [(piece, once_rows(shard_rows)) for piece in firsts_known]
            + [(table, whole), (sine, whole)],
            [
                (spread, LOW, blocked),
                (spread, LOW, blocked),
                ((sequences, local_len, 2 * D), LOW, blocked),
                ((D, 3 * D), LOW, whole),
            ],
            48,
        )

    (rest_y, rest_core, left2, right2), (normed, query, keyval, qkv) = exchanged(
        [
            ("pair", rest, "wshard", 2, 0),
            ("pair", rest, "wshard", 1, 0),
            ("send", tails[some:], "seq", to_right, 0),
            ("send", heads[some:], "seq", to_left, 0),
        ],
        (cosine,),
        projection,
    )
    left = jnp.concatenate([left1, left2], axis=0)
    right = jnp.concatenate([right1, right2], axis=0)
    ((rest_both,), _) = exchanged([("pair", rest_y, "wshard", 1, 0)])
    several = blocked_by(2 * GROUP)

    def attention(table, last):
        return called(
            attend_kernel,
            sequences,
            [
                (place, scalar), (tokens, several), (normed, several), (left, several), (right, several),
                (gains, whole), (query, several), (keyval, several), (qkv, once),
            ]
            + [(piece, once_rows(proj_master.shape[0])) for piece in (rest, rest_core, rest_y, last)]
            + [(table, whole), (sine, whole), (cap, whole)],
            [
                ((sequences, SPAN, D), LOW, several),
                ((sequences, SPAN, 2 * D), LOW, several),
                ((sequences, PAIRS, SPAN, SPAN), LOW, several),
                (spread, LOW, several),
                (spread, WIDE, several),
                ((D, D), LOW, whole),
            ],
            60,
            group=2 * GROUP,
        )

    low_wide = wide_master.astype(LOW)
    (wide_y, wide_core), attention_results = exchanged(
        [("pair", low_wide, "wshard", 2, 0), ("pair", low_wide, "wshard", 1, 0)],
        (cosine, rest_both),
        attention,
    )
    rests = (rest, rest_core, rest_y, rest_both)
    normed_ext, keyval_ext, probs, attended, hidden, proj = attention_results
    ((wide_both,), _) = exchanged([("pair", wide_y, "wshard", 1, 0)])
    wides = (low_wide, wide_core, wide_y, wide_both)
    rest_rows = 3 * shard_rows + rest.shape[0]
    shares = (2, rest_rows, D)
    layer_output, d_hidden, d_out, gain_grad2, rest_kept, rest_sent = called(
        feed_kernel,
        sequences,
        [
            (place, scalar), (hidden, blocked), (cotangent, blocked), (gains, whole),
            (proj, once), (attended.reshape(cells, D), once),
        ]
        + [(piece, once) for piece in wides + rests],
        [
            (spread, WIDE, blocked),
            (spread, WIDE, blocked),
            (spread, LOW, blocked),
            ((1, D), WIDE, whole),
            (shares, LOW, whole),
            (shares, LOW, whole),
        ],
        60,
        [
            pltpu.VMEM((D, 2 * FF), LOW),
            pltpu.VMEM((FF, D), LOW),
            pltpu.VMEM((cells, D), LOW),
            pltpu.VMEM((cells, FF), LOW),
            pltpu.VMEM((cells, 2 * FF), LOW),
            pltpu.VMEM((cells, D), LOW),
            pltpu.VMEM((cells, D), LOW),
        ],
    )

    def summed(kept, got):
        return (kept.astype(WIDE) + got.astype(WIDE)).astype(LOW)

    ((rest_got,), _) = exchanged([("pair", rest_sent, "wshard", 1, 0)])
    shares = (2, shard_rows + GAIN_ROWS, 3 * D)
    rest_grad = summed(rest_kept, rest_got)
    near, far = rest_grad[:, :, : D // 2], rest_grad[:, :, D // 2 :]
    part = sequences // 2
    half_halo = (part, HALF, D)
    half_rows = part * local_len

    def first_back(table):
        return called(
            first_back_kernel,
            part,
            [
                (query, blocked), (keyval_ext, blocked), (probs, blocked), (d_out, blocked),
                (qkv, once), (table, whole), (sine, whole), (normed_ext, blocked),
            ],
            [
                (half_halo, LOW, blocked),
                (half_halo, LOW, blocked),
                (spread, WIDE, blocked),
                ((half_rows, D), LOW, whole),
                ((2 * half_rows, 2 * D), LOW, whole),
                ((1, D), WIDE, whole),
            ],
            56,
        )

    (near, far), first_results = exchanged(
        [("lead", near, "wshard", 2, 0), ("fold", far, "seq", 2, 1)], (cosine,), first_back
    )
    d_left, d_right, d_normed, first_query, first_keyval, first_gain = first_results
    after = later(part // GROUP)

    def second_back(table):
        return called(
            second_back_kernel,
            part,
            [
                (place, scalar), (query, after), (keyval_ext, after), (probs, after), (d_out, after),
                (qkv, once), (table, whole), (sine, whole), (normed_ext, once), (gains, whole),
                (gain_grad2, whole), (first_query, once), (first_keyval, once), (first_gain, whole),
                (d_normed, anywhere),
            ],
            [
                (half_halo, LOW, blocked),
                (half_halo, LOW, blocked),
                (spread, WIDE, after),
                (shares, LOW, whole),
                (shares, LOW, whole),
            ],
            60,
            [
                pltpu.VMEM((half_rows, D), LOW),
                pltpu.VMEM((2 * half_rows, 2 * D), LOW),
                pltpu.VMEM((1, D), WIDE),
            ],
            aliases={14: 2},
        )

    (near, far, left_one, right_one), second_results = exchanged(
        [
            ("fold", near, "seq", 1, 0),
            ("lead", far, "wshard", 2, 0),
            ("send", d_right, "seq", to_right, 0),
            ("send", d_left, "seq", to_left, 0),
        ],
        (cosine,),
        second_back,
    )
    d_left, d_right, d_normed, kept, sent = second_results
    (got, near, far), _ = exchanged(
        [
            ("pair", sent, "wshard", 1, 0),
            ("fold", near, "seq", 2, 0),
            ("fold", far, "seq", 1, 0),
        ]
    )
    both_grad = summed(kept, got)
    half = 3 * D // 2
    one_grad, two_grad = both_grad[:, :shard_rows, :half], both_grad[:, :, half:]

    cuts = (0, part // 2, part)
    from_left, from_right = [left_one], [right_one]

    def round_of(steps, cut=None):
        if cut is not None:
            rows = slice(cuts[cut], cuts[cut + 1])
            steps = steps + [
                ("send", d_right[rows], "seq", to_right, 0),
                ("send", d_left[rows], "seq", to_left, 0),
            ]
        results, _ = exchanged(steps)
        if cut is not None:
            from_right.append(results.pop())
            from_left.append(results.pop())
        return results

    near, one_grad, two_grad = round_of(
        [
            ("full", near, "seq", 4, 0),
            ("lead", one_grad, "wshard", 2, 0),
            ("fold", two_grad, "seq", 2, 1),
        ],
        0,
    )
    far, one_grad, two_grad = round_of(
        [
            ("full", far, "seq", 4, 0),
            ("fold", one_grad, "seq", 2, 0),
            ("lead", two_grad, "wshard", 2, 0),
        ],
        1,
    )
    near, far = far_sum(near), far_sum(far)
    near, far, one_grad, two_grad = round_of(
        [
            ("join", near, "seq", 2, 0),
            ("join", far, "seq", 1, 0),
            ("full", one_grad, "seq", 4, 0),
            ("full", two_grad, "seq", 1, 0),
        ]
    )
    near, far, one_grad, two_grad = round_of(
        [
            ("join", near, "seq", 1, 0),
            ("join", far, "seq", 2, 0),
            ("full", one_grad, "seq", 1, 0),
            ("full", two_grad, "seq", 4, 0),
        ]
    )
    rest_grad = jnp.concatenate([near, far], axis=1)
    input_grad = called(
        enter_kernel,
        sequences,
        [
            (tokens, blocked), (gains, whole), (d_normed, blocked),
            (jnp.concatenate(from_left, axis=0), blocked),
            (jnp.concatenate(from_right, axis=0), blocked),
            (d_hidden, blocked),
        ],
        [(spread, WIDE, blocked)],
        32,
    )[0]
    one_grad, two_grad = far_sum(one_grad), far_sum(two_grad)
    one_grad, two_grad = round_of([("join", one_grad, "seq", 2, 0), ("join", two_grad, "seq", 2, 0)])
    rest_grad, one_grad, two_grad = (grad.astype(WIDE) for grad in (rest_grad, one_grad, two_grad))
    gains_sum = lax.dynamic_slice_in_dim(
        two_grad[shard_rows : shard_rows + 2],
        lax.axis_index("wshard") * norm_gains.shape[1],
        norm_gains.shape[1],
        axis=1,
    )
    wide_parts = [rest_grad[third * shard_rows : (third + 1) * shard_rows] for third in range(3)]
    owned_grads = (
        jnp.concatenate([one_grad, two_grad[:shard_rows]], axis=1),
        rest_grad[3 * shard_rows : 4 * shard_rows],
        jnp.concatenate(wide_parts, axis=1),
        rest_grad[4 * shard_rows :],
        gains_sum,
    )
    rates = (
        2.0 * D ** (-0.5),
        2.0 * max(D // WINDOW, 1) ** (-0.5),
        2.0 * D ** (-0.5),
        2.0 * FF ** (-0.5),
        1.0,
    )
    masters = (qkv_master, proj_master, wide_master, down_master, norm_gains)
    firsts = (qkv_first, proj_first, wide_first, down_first, gains_first)
    seconds = (qkv_second, proj_second, wide_second, down_second, gains_second)
    results = [adamw(masters[i], owned_grads[i], firsts[i], seconds[i], rates[i]) for i in range(5)]
    return (
        layer_output,
        input_grad,
        results[0][0],
        results[1][0],
        results[2][0],
        results[3][0],
        results[4][0],
        results[0][1],
        results[1][1],
        results[2][1],
        results[3][1],
        results[4][1],
        results[0][2],
        results[1][2],
        results[2][2],
        results[3][2],
        results[4][2],
    )


def solution(mesh):
    placed = (
        P("wshard", "seq", None),
        P("wshard", "seq", None),
        P("wshard", None),
        P("wshard", None),
        P("wshard", None),
        P("wshard", None),
        P(None, "wshard"),
        P("wshard", None),
        P("wshard", None),
        P("wshard", None),
        P("wshard", None),
        P(None, "wshard"),
        P("wshard", None),
        P("wshard", None),
        P("wshard", None),
        P("wshard", None),
        P(None, "wshard"),
    )
    return jax.shard_map(
        on_device,
        mesh=mesh,
        in_specs=placed,
        out_specs=(
            P("wshard", "seq", None),
            P("wshard", "seq", None),
            P("wshard", None),
            P("wshard", None),
            P("wshard", None),
            P("wshard", None),
            P(None, "wshard"),
            P("wshard", None),
            P("wshard", None),
            P("wshard", None),
            P("wshard", None),
            P(None, "wshard"),
            P("wshard", None),
            P("wshard", None),
            P("wshard", None),
            P("wshard", None),
            P(None, "wshard"),
        ),
        check_vma=False,
    )
```

```python
import jax
import jax.numpy as jnp
from jax import lax
from jax.experimental import pallas as pl
from jax.experimental.pallas import tpu as pltpu
from jax.sharding import PartitionSpec as P

D = 768
HEADS = 12
HEAD = 64
FF = 1152
WINDOW = 128
STEP = 10
HALF = WINDOW // 2
SPAN = 2 * WINDOW
LANES = 128
PAIRS = D // LANES
GROUP = 2
LOW = jnp.bfloat16
WIDE = jnp.float32
SHARDS = 4
GAIN_ROWS = 32
MIB = 1 << 20


def dot(one, other, dims=((1,), (0,))):
    return lax.dot_general(one, other, (dims, ((), ())), preferred_element_type=WIDE)


def normalised(value):
    centred = value - jnp.mean(value, axis=-1, keepdims=True)
    inverse = lax.rsqrt(jnp.mean(centred * centred, axis=-1, keepdims=True) + 1e-05)
    return centred * inverse, inverse


def normalised_back(d_normed, gain, xhat, inverse):
    d_xhat = d_normed * gain
    mean = jnp.mean(d_xhat, axis=-1, keepdims=True)
    slope = jnp.mean(d_xhat * xhat, axis=-1, keepdims=True)
    return inverse * (d_xhat - mean - xhat * slope)


def lane_of(rows):
    return lax.broadcasted_iota(jnp.int32, (rows, LANES), 1)


def half_swapped(value):
    first = lane_of(value.shape[0]) % HEAD < HEAD // 2
    ahead = pltpu.roll(value, LANES - HEAD // 2, 1)
    behind = pltpu.roll(value, HEAD // 2, 1)
    return jnp.where(first, ahead, behind)


def turned(value, cosine, sine):
    return value * cosine + half_swapped(value) * sine


def turned_back(value, cosine, sine):
    return value * cosine - half_swapped(value) * sine


def by_head(value):
    first = lane_of(value.shape[0]) < HEAD
    zero = jnp.zeros_like(value)
    return jnp.concatenate([jnp.where(first, value, zero), jnp.where(first, zero, value)], axis=0)


def side_by_side(value):
    rows = value.shape[0] // 2
    return jnp.where(lane_of(rows) < HEAD, value[:rows], value[rows:])


def pair(index, start=0):
    return slice(start + index * LANES, start + (index + 1) * LANES)


def laid(place, pieces, target, size, start=0):
    @pl.when(pl.program_id(0) == 0)
    def _():
        for known, piece in enumerate(pieces):
            row = pl.multiple_of((place[0] ^ known) * size, 16)
            target[pl.ds(row, size), :] = piece[start : start + size, :]


def shipped(place, packed, shard, row, columns, value):
    lead = (place[0] // 2) ^ (shard // 2)
    whose = (place[0] % 2) ^ (shard % 2)
    packed[whose, lead, row : row + value.shape[0], columns] = value.astype(LOW)


def handed(packed, kept, sent, semaphores):
    copies = [
        pltpu.make_async_copy(packed.at[whose], target, semaphores.at[whose])
        for whose, target in enumerate((kept, sent))
    ]
    for copy in copies:
        copy.start()
    for copy in copies:
        copy.wait()


def shipped_rows(place, packed, start, size, row, columns, value):
    end = start + value.shape[0]
    for shard in range(SHARDS):
        low, high = max(start, shard * size), min(end, (shard + 1) * size)
        if low < high:
            part = value[low - start : high - start]
            shipped(place, packed, shard, row + low - shard * size, columns, part)


def project_kernel(
    place, tokens, gains, one_piece, two_piece, three_piece, four_piece, cosine, sine,
    normed, query, keyval, weight,
):
    laid(place, (one_piece, two_piece, three_piece, four_piece), weight, D // SHARDS)
    rows = GROUP * WINDOW
    xhat, _ = normalised(tokens[...].reshape(rows, D))
    low = (xhat * gains[0:1, :]).astype(LOW)
    normed[...] = low.reshape(GROUP, WINDOW, D)
    mine = slice(HALF, HALF + WINDOW)
    cos, sin = cosine[mine], sine[mine]
    out = dot(low, weight[:, :D])
    for one in range(GROUP):
        for p in range(PAIRS):
            part = out[one * WINDOW : (one + 1) * WINDOW, pair(p)]
            query[one, :, pair(p)] = (turned(part, cos, sin) * HEAD**-0.5).astype(LOW)
    out = dot(low, weight[:, D : 2 * D])
    for one in range(GROUP):
        for p in range(PAIRS):
            part = out[one * WINDOW : (one + 1) * WINDOW, pair(p)]
            keyval[one, :, pair(p)] = turned(part, cos, sin).astype(LOW)
    out = dot(low, weight[:, 2 * D :])
    keyval[:, :, D:] = out.astype(LOW).reshape(GROUP, WINDOW, D)


def attend_kernel(
    place, tokens, normed, left1, left2, right1, right2, gains, query, keyval, weight,
    one_piece, two_piece, three_piece, four_piece, cosine, sine, cap,
    normed_ext, keyval_ext, probs, attended, hidden, proj,
):
    group = tokens.shape[0]
    laid(place, (one_piece, two_piece, three_piece, four_piece), proj, D // SHARDS)
    gain = gains[0:1, :]
    ends = []
    for one in range(group):
        early = pl.program_id(0) == 0
        left = jnp.where(early, left1[one], left2[one])
        right = jnp.where(early, right1[one], right2[one])
        low_left = (left.astype(WIDE) * gain).astype(LOW)
        low_right = (right.astype(WIDE) * gain).astype(LOW)
        normed_ext[one, :HALF] = low_left
        normed_ext[one, HALF : HALF + WINDOW] = normed[one]
        normed_ext[one, HALF + WINDOW :] = low_right
        ends += [low_left, low_right]
    ends = jnp.concatenate(ends, axis=0)
    cos = jnp.concatenate([cosine[:HALF], cosine[HALF + WINDOW :]], axis=0)
    sin = jnp.concatenate([sine[:HALF], sine[HALF + WINDOW :]], axis=0)
    keys = dot(ends, weight[:, D : 2 * D])
    values = dot(ends, weight[:, 2 * D :]).astype(LOW)
    for one in range(group):
        keyval_ext[one, HALF : HALF + WINDOW] = keyval[one]
        rows = slice(one * WINDOW, (one + 1) * WINDOW)
        keyval_ext[one, :HALF, D:] = values[rows][:HALF]
        keyval_ext[one, HALF + WINDOW :, D:] = values[rows][HALF:]
        for p in range(PAIRS):
            key = turned(keys[rows, pair(p)], cos, sin).astype(LOW)
            keyval_ext[one, :HALF, pair(p)] = key[:HALF]
            keyval_ext[one, HALF + WINDOW :, pair(p)] = key[HALF:]
    limit = jnp.concatenate([cap[...], cap[...]], axis=1)
    for one in range(group):
        for p in range(PAIRS):
            asked = by_head(query[one, :, pair(p)])
            scores = dot(keyval_ext[one, :, pair(p)], asked, ((1,), (1,)))
            scores = jnp.minimum(scores, limit)
            top = jnp.max(scores, axis=0, keepdims=True)
            grown = jnp.exp(scores - top)
            prob = grown * (1.0 / jnp.sum(grown, axis=0, keepdims=True))
            prob = prob.astype(LOW)
            probs[one, p] = prob
            found = dot(prob, keyval_ext[one, :, pair(p, D)], ((0,), (0,)))
            attended[one, :, pair(p)] = side_by_side(found).astype(LOW)
    rows = group * WINDOW
    out = dot(attended[...].reshape(rows, D), proj[...])
    hidden[...] = tokens[...] + out.reshape(group, WINDOW, D)


def feed_kernel(
    place, hidden, cotangent, gains, proj, attended,
    wide1, wide2, wide3, wide4, down1, down2, down3, down4,
    output, d_hidden, d_out, gain_grad, kept, sent,
    wide, down, all_normed, all_inner, all_d_both, all_dy, all_d_attn, packed, semaphores,
):
    laid(place, (wide1, wide2, wide3, wide4), wide, D // SHARDS)
    laid(place, (down1, down2, down3, down4), down, FF // SHARDS, D // SHARDS)
    here = pl.ds(pl.multiple_of(pl.program_id(0) * GROUP * WINDOW, GROUP * WINDOW), GROUP * WINDOW)
    normed, inner, d_both = all_normed.at[here], all_inner.at[here], all_d_both.at[here]
    low_cotangent, d_attn = all_dy.at[here], all_d_attn.at[here]
    rows = GROUP * WINDOW
    state = hidden[...].reshape(rows, D)
    gain = gains[1:2, :]
    xhat, inverse = normalised(state)
    low = (xhat * gain).astype(LOW)
    normed[...] = low
    above = cotangent[...].reshape(rows, D)
    dy = above.astype(LOW)
    low_cotangent[...] = dy
    start = 0
    while start < FF:
        size = min(256, FF - start)
        cols = slice(start, start + size)
        other = slice(FF + start, FF + start + size)
        gate = dot(low, wide[:, cols])
        upward = dot(low, wide[:, other])
        d_inner = dot(dy, down[cols, :], ((1,), (1,)))
        area = 0.5 + 0.5 * lax.erf(gate * (0.5**0.5))
        shaped = gate * area
        slope = area + gate * (jnp.exp(-0.5 * gate * gate) * 0.3989422804014327)
        inner[:, cols] = (shaped * upward).astype(LOW)
        d_both[:, cols] = (d_inner * upward * slope).astype(LOW)
        d_both[:, other] = (d_inner * shaped).astype(LOW)
        start += size
    output[...] = (state + dot(inner[...], down[...])).reshape(GROUP, WINDOW, D)
    d_normed = dot(d_both[...], wide[...], ((1,), (1,)))
    part = jnp.sum(d_normed * xhat, axis=0, keepdims=True)

    @pl.when(pl.program_id(0) == 0)
    def _():
        gain_grad[...] = part

    @pl.when(pl.program_id(0) > 0)
    def _():
        gain_grad[...] += part

    back = above + normalised_back(d_normed, gain, xhat, inverse)
    d_hidden[...] = back.reshape(GROUP, WINDOW, D)
    back = back.astype(LOW)
    d_attn[...] = back
    d_out[...] = dot(back, proj[...], ((1,), (1,))).astype(LOW).reshape(GROUP, WINDOW, D)

    @pl.when(pl.program_id(0) == pl.num_programs(0) - 1)
    def _():
        first_rows = ((0,), (0,))
        every = slice(0, D)
        size = D // 2
        for start in range(0, D, size):
            lanes = slice(start, start + size)
            for third in range(3):
                grad = dot(all_normed[:, lanes], all_d_both[:, third * D : (third + 1) * D], first_rows)
                shipped_rows(place, packed, start, D // SHARDS, third * D // SHARDS, every, grad)
            grad = dot(attended[:, lanes], all_d_attn[...], first_rows)
            shipped_rows(place, packed, start, D // SHARDS, 3 * D // SHARDS, every, grad)
        for start in range(0, FF, size):
            grad = dot(all_inner[:, start : start + size], all_dy[...], first_rows)
            shipped_rows(place, packed, start, FF // SHARDS, D, every, grad)
        handed(packed, kept, sent, semaphores)


def back_step(
    query, keyval, probs, d_out, weight, cosine, sine, normed_ext, start,
    d_left, d_right, d_normed, all_query, all_keyval, gain_grad,
):
    step = pl.program_id(0)
    mine = slice(HALF, HALF + WINDOW)
    cos, sin = cosine[mine], sine[mine]
    here = pl.ds(pl.multiple_of(step * GROUP * WINDOW, GROUP * WINDOW), GROUP * WINDOW)
    d_query = all_query.at[here]
    here = pl.ds(pl.multiple_of(step * GROUP * SPAN, GROUP * SPAN), GROUP * SPAN)
    d_keyval = all_keyval.at[here]
    for one in range(GROUP):
        short = slice(one * WINDOW, (one + 1) * WINDOW)
        long = slice(one * SPAN, (one + 1) * SPAN)
        for p in range(PAIRS):
            asked = by_head(query[one, :, pair(p)])
            key = keyval[one, :, pair(p)]
            grad = by_head(d_out[one, :, pair(p)])
            low_prob = probs[one, p]
            prob = low_prob.astype(WIDE)
            d_prob = dot(keyval[one, :, pair(p, D)], grad, ((1,), (1,)))
            delta = jnp.sum(prob * d_prob, axis=0, keepdims=True)
            d_score = (prob * (d_prob - delta)).astype(LOW)
            d_q = side_by_side(dot(d_score, key, ((0,), (0,)))) * HEAD**-0.5
            d_query[short, pair(p)] = turned_back(d_q, cos, sin).astype(LOW)
            d_k = dot(d_score, asked)
            d_keyval[long, pair(p)] = turned_back(d_k, cosine[...], sine[...]).astype(LOW)
            d_v = dot(low_prob, grad)
            d_keyval[long, pair(p, D)] = d_v.astype(LOW)
    both = dot(d_keyval[...], weight[:, D:], ((1,), (1,)))
    own = dot(d_query[...], weight[:, :D], ((1,), (1,)))
    total = jnp.zeros((1, D), WIDE)
    for one in range(GROUP):
        part = both[one * SPAN : (one + 1) * SPAN]
        inside = own[one * WINDOW : (one + 1) * WINDOW]
        rows = normed_ext[start + one].astype(WIDE)
        total += jnp.sum(part * rows, axis=0, keepdims=True)
        total += jnp.sum(inside * rows[mine], axis=0, keepdims=True)
        d_left[one] = part[:HALF].astype(LOW)
        d_right[one] = part[HALF + WINDOW :].astype(LOW)
        d_normed[one] = part[mine] + inside

    @pl.when(step == 0)
    def _():
        gain_grad[...] = total

    @pl.when(step > 0)
    def _():
        gain_grad[...] += total


def first_back_kernel(
    query, keyval, probs, d_out, weight, cosine, sine, normed_ext,
    d_left, d_right, d_normed, all_query, all_keyval, gain_grad,
):
    back_step(
        query, keyval, probs, d_out, weight, cosine, sine, normed_ext, 0,
        d_left, d_right, d_normed, all_query, all_keyval, gain_grad,
    )


def second_back_kernel(
    place, query, keyval, probs, d_out, weight, cosine, sine, normed_ext, gains, gain_grad2,
    first_query, first_keyval, first_gain, earlier,
    d_left, d_right, d_normed, kept, sent,
    all_query, all_keyval, gain_grad1, packed, semaphores,
):
    del earlier
    mine = slice(HALF, HALF + WINDOW)
    start = normed_ext.shape[0] // 2 + pl.program_id(0) * GROUP
    back_step(
        query, keyval, probs, d_out, weight, cosine, sine, normed_ext, start,
        d_left, d_right, d_normed, all_query, all_keyval, gain_grad1,
    )

    @pl.when(pl.program_id(0) == pl.num_programs(0) - 1)
    def _():
        first_rows = ((0,), (0,))
        some = normed_ext.shape[0] // 2
        parts = ((slice(0, some), first_query, first_keyval), (slice(some, 2 * some), all_query, all_keyval))
        size = D // 2
        for start in range(0, D, size):
            lanes = slice(start, start + size)
            grad = 0.0
            for some_rows, part_query, _ in parts:
                rows = normed_ext[some_rows, mine, lanes].reshape(some * WINDOW, size)
                grad += dot(rows, part_query[...], first_rows)
            shipped_rows(place, packed, start, D // SHARDS, 0, slice(0, D), grad)
            for part in range(2):
                grad = 0.0
                for some_rows, _, part_keyval in parts:
                    rows = normed_ext[some_rows, :, lanes].reshape(some * SPAN, size)
                    grad += dot(rows, part_keyval[:, part * D : (part + 1) * D], first_rows)
                columns = slice((part + 1) * D, (part + 2) * D)
                shipped_rows(place, packed, start, D // SHARDS, 0, columns, grad)
        more = slice(D // SHARDS, D // SHARDS + GAIN_ROWS)
        first = (first_gain[...] + gain_grad1[...]) / gains[0:1, :]
        empty = jnp.zeros((GAIN_ROWS - 2, D), WIDE)
        both_gains = jnp.concatenate([first, gain_grad2[...], empty], axis=0).astype(LOW)
        for whose in range(2):
            for lead in range(2):
                packed[whose, lead, more, :] = jnp.zeros((GAIN_ROWS, 3 * D), LOW)
                packed[whose, lead, more, 3 * D // 2 : 5 * D // 2] = both_gains
        handed(packed, kept, sent, semaphores)


def enter_kernel(tokens, gains, d_normed, from_left, from_right, d_hidden, input_grad):
    rows = GROUP * WINDOW
    xhat, inverse = normalised(tokens[...].reshape(rows, D))
    parts = []
    for one in range(GROUP):
        parts += [
            d_normed[one, :HALF] + from_left[one].astype(WIDE),
            d_normed[one, HALF:] + from_right[one].astype(WIDE),
        ]
    back = normalised_back(jnp.concatenate(parts, axis=0), gains[0:1, :], xhat, inverse)
    input_grad[...] = d_hidden[...] + back.reshape(GROUP, WINDOW, D)


def whole(shape):
    return pl.BlockSpec(shape, lambda i: (0,) * len(shape))


def once(shape):
    return pl.BlockSpec(shape, lambda i: (0,) * len(shape), pipeline_mode=pl.Buffered(1))


def once_rows(rows):
    return lambda shape: pl.BlockSpec((rows, shape[1]), lambda i: (0, 0), pipeline_mode=pl.Buffered(1))


def scalar(shape):
    return pl.BlockSpec(memory_space=pltpu.SMEM)


def blocked(shape):
    return pl.BlockSpec((GROUP,) + tuple(shape[1:]), lambda i: (i,) + (0,) * (len(shape) - 1))


def blocked_by(count):
    return lambda shape: pl.BlockSpec((count,) + tuple(shape[1:]), lambda i: (i,) + (0,) * (len(shape) - 1))


def later(steps):
    return lambda shape: pl.BlockSpec(
        (GROUP,) + tuple(shape[1:]), lambda i: (i + steps,) + (0,) * (len(shape) - 1)
    )


def anywhere(shape):
    return pl.BlockSpec(memory_space=pl.ANY)


def called(kernel, sequences, operands, results, limit, scratch=(), group=GROUP, aliases=None):
    arrays = [array for array, _ in operands]
    return pl.pallas_call(
        kernel,
        grid=(sequences // group,),
        in_specs=[spec(array.shape) for array, spec in operands],
        out_specs=[spec(shape) for shape, _, spec in results],
        out_shape=[jax.ShapeDtypeStruct(shape, kind) for shape, kind, _ in results],
        scratch_shapes=list(scratch),
        input_output_aliases=aliases or {},
        compiler_params=pltpu.CompilerParams(
            dimension_semantics=("arbitrary",), vmem_limit_bytes=limit * MIB
        ),
        cost_estimate=pl.CostEstimate(flops=1000, bytes_accessed=1000, transcendentals=0),
    )(*arrays)


def swapped(value, axis, bit):
    count = lax.axis_size(axis)
    return lax.ppermute(value, axis, [(i, i ^ bit) for i in range(count)])


def exchanged(steps, carried=(), beside=None):
    kept, sent = [], []
    for how, value, axis, bit, dim in steps:
        if how == "lead":
            kept.append(value[0])
            value = value[1]
        elif how == "fold":
            side = (lax.axis_index(axis) // bit) % 2
            size = value.shape[dim] // 2
            kept.append(lax.dynamic_slice_in_dim(value, side * size, size, axis=dim))
            value = lax.dynamic_slice_in_dim(value, (1 - side) * size, size, axis=dim)
        else:
            kept.append(None)
        sent.append(value)
    held = lax.optimization_barrier(tuple(sent) + tuple(carried))
    sent, carried = held[: len(sent)], held[len(sent) :]
    got = []
    for (how, _, axis, bit, _), value in zip(steps, sent):
        got.append(lax.ppermute(value, axis, bit) if how == "send" else swapped(value, axis, bit))
    if beside is not None:
        carried = beside(*carried)
    held = lax.optimization_barrier(tuple(got) + tuple(carried))
    got, carried = held[: len(got)], held[len(got) :]
    results = []
    for (how, _, axis, bit, dim), mine, own, other in zip(steps, kept, sent, got):
        if how in ("fold", "lead"):
            other = (mine.astype(WIDE) + other.astype(WIDE)).astype(LOW)
        elif how == "full":
            other = (own.astype(WIDE) + other.astype(WIDE)).astype(LOW)
        elif how == "join":
            side = (lax.axis_index(axis) // bit) % 2
            low = jnp.where(side == 0, own, other)
            high = jnp.where(side == 0, other, own)
            other = jnp.concatenate([low, high], axis=dim)
        results.append(other)
    return results, carried


def far_sum(value):
    bit = 8
    while bit < lax.axis_size("seq"):
        ((value,), _) = exchanged([("full", value, "seq", bit, 0)])
        bit *= 2
    return value


def adamw(master, grad, first, second, rate):
    moment = 0.9 * first + 0.1 * grad
    square = 0.98 * second + 0.02 * grad * grad
    fixed_first = moment / (1.0 - 0.9**STEP)
    fixed_second = square / (1.0 - 0.98**STEP)
    update = fixed_first / (jnp.sqrt(fixed_second) + 1e-06) + 1e-05 * master
    return (master - rate * update, moment, square)


def in_order(pieces):
    place = lax.axis_index("wshard")
    size = pieces[0].shape[0]
    total = jnp.zeros((size * len(pieces),) + pieces[0].shape[1:], pieces[0].dtype)
    for known, piece in enumerate(pieces):
        total = lax.dynamic_update_slice_in_dim(total, piece, (place ^ known) * size, 0)
    return total


def tables(base, total):
    places = base - HALF + jnp.arange(SPAN, dtype=jnp.int32)
    freqs = 10000.0 ** (-jnp.arange(0, HEAD, 2).astype(WIDE) / HEAD)
    angles = places.astype(WIDE)[:, None] * freqs[None, :]
    cosine, sine = jnp.cos(angles), jnp.sin(angles)
    cosine = jnp.concatenate([cosine] * 4, axis=1)
    sine = jnp.concatenate([-sine, sine] * 2, axis=1)
    row = jnp.arange(WINDOW)[None, :]
    col = jnp.arange(SPAN)[:, None]
    seen = (col >= row) & (col <= row + WINDOW) & (places >= 0)[:, None] & (places < total)[:, None]
    return cosine, sine, jnp.where(seen, 3e38, -1e30).astype(WIDE)


def on_device(
    tokens,
    cotangent,
    qkv_master,
    proj_master,
    wide_master,
    down_master,
    norm_gains,
    qkv_first,
    proj_first,
    wide_first,
    down_first,
    gains_first,
    qkv_second,
    proj_second,
    wide_second,
    down_second,
    gains_second,
):
    sequences, local_len, width = tokens.shape
    blocks = lax.axis_size("seq")
    base = lax.axis_index("seq") * local_len
    to_right = [(i, i + 1) for i in range(blocks - 1)]
    to_left = [(i + 1, i) for i in range(blocks - 1)]

    shard_rows = qkv_master.shape[0]
    own_gains = jnp.pad(norm_gains, ((0, 14), (0, qkv_master.shape[1] - norm_gains.shape[1])))
    first = jnp.concatenate([qkv_master.astype(LOW), own_gains.astype(LOW)], axis=0)
    ends = normalised(tokens)[0].astype(LOW)
    some = sequences // 2
    tails, heads = ends[:, local_len - HALF :], ends[:, :HALF]
    first_y, first_core, left1, right1 = lax.optimization_barrier(
        (
            swapped(first, "wshard", 2),
            swapped(first, "wshard", 1),
            lax.ppermute(tails[:some], "seq", to_right),
            lax.ppermute(heads[:some], "seq", to_left),
        )
    )
    rest = jnp.concatenate([proj_master.astype(LOW), down_master.astype(LOW)], axis=0)
    ((first_both,), _) = exchanged([("pair", first_y, "wshard", 1, 0)])
    firsts_known = (first, first_core, first_y, first_both)
    gains = in_order([piece[shard_rows : shard_rows + 2, : norm_gains.shape[1]].T for piece in firsts_known])
    gains = gains.T.astype(WIDE)
    cosine, sine, cap = tables(base, local_len * blocks)
    place = lax.axis_index("wshard").astype(jnp.int32).reshape(1)
    cells = sequences * local_len
    spread = (sequences, local_len, D)
    halo = (sequences, HALF, D)
    def projection(table):
        return called(
            project_kernel,
            sequences,
            [(place, scalar), (tokens, blocked), (gains, whole)]
            + [(piece, once_rows(shard_rows)) for piece in firsts_known]
            + [(table, whole), (sine, whole)],
            [
                (spread, LOW, blocked),
                (spread, LOW, blocked),
                ((sequences, local_len, 2 * D), LOW, blocked),
                ((D, 3 * D), LOW, whole),
            ],
            48,
        )

    (rest_y, rest_core, left2, right2), (normed, query, keyval, qkv) = exchanged(
        [
            ("pair", rest, "wshard", 2, 0),
            ("pair", rest, "wshard", 1, 0),
            ("send", tails[some:], "seq", to_right, 0),
            ("send", heads[some:], "seq", to_left, 0),
        ],
        (cosine,),
        projection,
    )
    ((rest_both,), _) = exchanged([("pair", rest_y, "wshard", 1, 0)])
    several = blocked_by(some)

    def attention(table, last):
        return called(
            attend_kernel,
            sequences,
            [
                (place, scalar), (tokens, several), (normed, several), (left1, once),
                (left2, once), (right1, once), (right2, once),
                (gains, whole), (query, several), (keyval, several), (qkv, once),
            ]
            + [(piece, once_rows(proj_master.shape[0])) for piece in (rest, rest_core, rest_y, last)]
            + [(table, whole), (sine, whole), (cap, whole)],
            [
                ((sequences, SPAN, D), LOW, several),
                ((sequences, SPAN, 2 * D), LOW, several),
                ((sequences, PAIRS, SPAN, SPAN), LOW, several),
                (spread, LOW, several),
                (spread, WIDE, several),
                ((D, D), LOW, whole),
            ],
            60,
            group=some,
        )

    low_wide = wide_master.astype(LOW)
    (wide_y, wide_core), attention_results = exchanged(
        [("pair", low_wide, "wshard", 2, 0), ("pair", low_wide, "wshard", 1, 0)],
        (cosine, rest_both),
        attention,
    )
    rests = (rest, rest_core, rest_y, rest_both)
    normed_ext, keyval_ext, probs, attended, hidden, proj = attention_results
    ((wide_both,), _) = exchanged([("pair", wide_y, "wshard", 1, 0)])
    wides = (low_wide, wide_core, wide_y, wide_both)
    rest_rows = 3 * shard_rows + rest.shape[0]
    shares = (2, rest_rows, D)
    layer_output, d_hidden, d_out, gain_grad2, rest_kept, rest_sent = called(
        feed_kernel,
        sequences,
        [
            (place, scalar), (hidden, blocked), (cotangent, blocked), (gains, whole),
            (proj, once), (attended.reshape(cells, D), once),
        ]
        + [(piece, once) for piece in wides + rests],
        [
            (spread, WIDE, blocked),
            (spread, WIDE, blocked),
            (spread, LOW, blocked),
            ((1, D), WIDE, whole),
            (shares, LOW, anywhere),
            (shares, LOW, anywhere),
        ],
        60,
        [
            pltpu.VMEM((D, 2 * FF), LOW),
            pltpu.VMEM((FF, D), LOW),
            pltpu.VMEM((cells, D), LOW),
            pltpu.VMEM((cells, FF), LOW),
            pltpu.VMEM((cells, 2 * FF), LOW),
            pltpu.VMEM((cells, D), LOW),
            pltpu.VMEM((cells, D), LOW),
            pltpu.VMEM((2,) + shares, LOW),
            pltpu.SemaphoreType.DMA((2,)),
        ],
    )

    def summed(kept, got):
        return (kept.astype(WIDE) + got.astype(WIDE)).astype(LOW)

    ((rest_got,), _) = exchanged([("pair", rest_sent, "wshard", 1, 0)])
    shares = (2, shard_rows + GAIN_ROWS, 3 * D)
    rest_grad = summed(rest_kept, rest_got)
    near, far = rest_grad[:, :, : D // 2], rest_grad[:, :, D // 2 :]
    part = sequences // 2
    half_halo = (part, HALF, D)
    half_rows = part * local_len

    def first_back(table):
        return called(
            first_back_kernel,
            part,
            [
                (query, blocked), (keyval_ext, blocked), (probs, blocked), (d_out, blocked),
                (qkv, once), (table, whole), (sine, whole), (normed_ext, blocked),
            ],
            [
                (half_halo, LOW, blocked),
                (half_halo, LOW, blocked),
                (spread, WIDE, blocked),
                ((half_rows, D), LOW, whole),
                ((2 * half_rows, 2 * D), LOW, whole),
                ((1, D), WIDE, whole),
            ],
            56,
        )

    (near, far), first_results = exchanged(
        [("lead", near, "wshard", 2, 0), ("fold", far, "seq", 2, 1)], (cosine,), first_back
    )
    d_left, d_right, d_normed, first_query, first_keyval, first_gain = first_results
    after = later(part // GROUP)

    def second_back(table):
        return called(
            second_back_kernel,
            part,
            [
                (place, scalar), (query, after), (keyval_ext, after), (probs, after), (d_out, after),
                (qkv, once), (table, whole), (sine, whole), (normed_ext, once), (gains, whole),
                (gain_grad2, whole), (first_query, once), (first_keyval, once), (first_gain, whole),
                (d_normed, anywhere),
            ],
            [
                (half_halo, LOW, blocked),
                (half_halo, LOW, blocked),
                (spread, WIDE, after),
                (shares, LOW, anywhere),
                (shares, LOW, anywhere),
            ],
            60,
            [
                pltpu.VMEM((half_rows, D), LOW),
                pltpu.VMEM((2 * half_rows, 2 * D), LOW),
                pltpu.VMEM((1, D), WIDE),
                pltpu.VMEM((2,) + shares, LOW),
                pltpu.SemaphoreType.DMA((2,)),
            ],
            aliases={14: 2},
        )

    (near, far, left_one, right_one), second_results = exchanged(
        [
            ("fold", near, "seq", 1, 0),
            ("lead", far, "wshard", 2, 0),
            ("send", d_right, "seq", to_right, 0),
            ("send", d_left, "seq", to_left, 0),
        ],
        (cosine,),
        second_back,
    )
    d_left, d_right, d_normed, kept, sent = second_results
    (got, near, far), _ = exchanged(
        [
            ("pair", sent, "wshard", 1, 0),
            ("fold", near, "seq", 2, 0),
            ("fold", far, "seq", 1, 0),
        ]
    )
    both_grad = summed(kept, got)
    half = 3 * D // 2
    one_grad, two_grad = both_grad[:, :shard_rows, :half], both_grad[:, :, half:]

    cuts = (0, part // 2, part)
    from_left, from_right = [left_one], [right_one]

    def round_of(steps, cut=None):
        if cut is not None:
            rows = slice(cuts[cut], cuts[cut + 1])
            steps = steps + [
                ("send", d_right[rows], "seq", to_right, 0),
                ("send", d_left[rows], "seq", to_left, 0),
            ]
        results, _ = exchanged(steps)
        if cut is not None:
            from_right.append(results.pop())
            from_left.append(results.pop())
        return results

    near, one_grad, two_grad = round_of(
        [
            ("full", near, "seq", 4, 0),
            ("lead", one_grad, "wshard", 2, 0),
            ("fold", two_grad, "seq", 2, 1),
        ],
        0,
    )
    far, one_grad, two_grad = round_of(
        [
            ("full", far, "seq", 4, 0),
            ("fold", one_grad, "seq", 2, 0),
            ("lead", two_grad, "wshard", 2, 0),
        ],
        1,
    )
    near, far = far_sum(near), far_sum(far)
    near, far, one_grad, two_grad = round_of(
        [
            ("join", near, "seq", 2, 0),
            ("join", far, "seq", 1, 0),
            ("full", one_grad, "seq", 4, 0),
            ("full", two_grad, "seq", 1, 0),
        ]
    )
    near, far, one_grad, two_grad = round_of(
        [
            ("join", near, "seq", 1, 0),
            ("join", far, "seq", 2, 0),
            ("full", one_grad, "seq", 1, 0),
            ("full", two_grad, "seq", 4, 0),
        ]
    )
    rest_grad = jnp.concatenate([near, far], axis=1)
    input_grad = called(
        enter_kernel,
        sequences,
        [
            (tokens, blocked), (gains, whole), (d_normed, blocked),
            (jnp.concatenate(from_left, axis=0), blocked),
            (jnp.concatenate(from_right, axis=0), blocked),
            (d_hidden, blocked),
        ],
        [(spread, WIDE, blocked)],
        32,
    )[0]
    one_grad, two_grad = far_sum(one_grad), far_sum(two_grad)
    one_rows = one_grad.shape[0]
    last = lax.optimization_barrier(jnp.concatenate([one_grad, two_grad], axis=0))
    ((other,), _) = exchanged([("pair", last, "seq", 2, 0)])
    upper = (lax.axis_index("seq") // 2) % 2 == 0
    low, high = jnp.where(upper, last, other), jnp.where(upper, other, last)
    one_grad = jnp.concatenate([low[:one_rows], high[:one_rows]], axis=0)
    two_grad = jnp.concatenate([low[one_rows:], high[one_rows:]], axis=0)
    rest_grad, one_grad, two_grad = (grad.astype(WIDE) for grad in (rest_grad, one_grad, two_grad))
    gains_sum = lax.dynamic_slice_in_dim(
        two_grad[shard_rows : shard_rows + 2],
        lax.axis_index("wshard") * norm_gains.shape[1],
        norm_gains.shape[1],
        axis=1,
    )
    wide_parts = [rest_grad[third * shard_rows : (third + 1) * shard_rows] for third in range(3)]
    owned_grads = (
        jnp.concatenate([one_grad, two_grad[:shard_rows]], axis=1),
        rest_grad[3 * shard_rows : 4 * shard_rows],
        jnp.concatenate(wide_parts, axis=1),
        rest_grad[4 * shard_rows :],
        gains_sum,
    )
    rates = (
        2.0 * D ** (-0.5),
        2.0 * max(D // WINDOW, 1) ** (-0.5),
        2.0 * D ** (-0.5),
        2.0 * FF ** (-0.5),
        1.0,
    )
    masters = (qkv_master, proj_master, wide_master, down_master, norm_gains)
    firsts = (qkv_first, proj_first, wide_first, down_first, gains_first)
    seconds = (qkv_second, proj_second, wide_second, down_second, gains_second)
    results = [adamw(masters[i], owned_grads[i], firsts[i], seconds[i], rates[i]) for i in range(5)]
    return (
        layer_output,
        input_grad,
        results[0][0],
        results[1][0],
        results[2][0],
        results[3][0],
        results[4][0],
        results[0][1],
        results[1][1],
        results[2][1],
        results[3][1],
        results[4][1],
        results[0][2],
        results[1][2],
        results[2][2],
        results[3][2],
        results[4][2],
    )


def solution(mesh):
    placed = (
        P("wshard", "seq", None),
        P("wshard", "seq", None),
        P("wshard", None),
        P("wshard", None),
        P("wshard", None),
        P("wshard", None),
        P(None, "wshard"),
        P("wshard", None),
        P("wshard", None),
        P("wshard", None),
        P("wshard", None),
        P(None, "wshard"),
        P("wshard", None),
        P("wshard", None),
        P("wshard", None),
        P("wshard", None),
        P(None, "wshard"),
    )
    return jax.shard_map(
        on_device,
        mesh=mesh,
        in_specs=placed,
        out_specs=(
            P("wshard", "seq", None),
            P("wshard", "seq", None),
            P("wshard", None),
            P("wshard", None),
            P("wshard", None),
            P("wshard", None),
            P(None, "wshard"),
            P("wshard", None),
            P("wshard", None),
            P("wshard", None),
            P("wshard", None),
            P(None, "wshard"),
            P("wshard", None),
            P("wshard", None),
            P("wshard", None),
            P("wshard", None),
            P(None, "wshard"),
        ),
        check_vma=False,
    )
```

```python
import jax
import jax.numpy as jnp
from jax import lax
from jax.experimental import pallas as pl
from jax.experimental.pallas import tpu as pltpu
from jax.sharding import PartitionSpec as P

D = 768
HEADS = 12
HEAD = 64
FF = 1152
WINDOW = 128
STEP = 10
HALF = WINDOW // 2
SPAN = 2 * WINDOW
LANES = 128
PAIRS = D // LANES
GROUP = 2
LOW = jnp.bfloat16
WIDE = jnp.float32
SHARDS = 4
GAIN_ROWS = 32
MIB = 1 << 20


def dot(one, other, dims=((1,), (0,))):
    return lax.dot_general(one, other, (dims, ((), ())), preferred_element_type=WIDE)


def normalised(value):
    centred = value - jnp.mean(value, axis=-1, keepdims=True)
    inverse = lax.rsqrt(jnp.mean(centred * centred, axis=-1, keepdims=True) + 1e-05)
    return centred * inverse, inverse


def normalised_back(d_normed, gain, xhat, inverse):
    d_xhat = d_normed * gain
    mean = jnp.mean(d_xhat, axis=-1, keepdims=True)
    slope = jnp.mean(d_xhat * xhat, axis=-1, keepdims=True)
    return inverse * (d_xhat - mean - xhat * slope)


def lane_of(rows):
    return lax.broadcasted_iota(jnp.int32, (rows, LANES), 1)


def half_swapped(value):
    first = lane_of(value.shape[0]) % HEAD < HEAD // 2
    ahead = pltpu.roll(value, LANES - HEAD // 2, 1)
    behind = pltpu.roll(value, HEAD // 2, 1)
    return jnp.where(first, ahead, behind)


def turned(value, cosine, sine):
    return value * cosine + half_swapped(value) * sine


def turned_back(value, cosine, sine):
    return value * cosine - half_swapped(value) * sine


def by_head(value):
    first = lane_of(value.shape[0]) < HEAD
    zero = jnp.zeros_like(value)
    return jnp.concatenate([jnp.where(first, value, zero), jnp.where(first, zero, value)], axis=0)


def side_by_side(value):
    rows = value.shape[0] // 2
    return jnp.where(lane_of(rows) < HEAD, value[:rows], value[rows:])


def pair(index, start=0):
    return slice(start + index * LANES, start + (index + 1) * LANES)


def laid(place, pieces, target, size, start=0):
    @pl.when(pl.program_id(0) == 0)
    def _():
        for known, piece in enumerate(pieces):
            row = pl.multiple_of((place[0] ^ known) * size, 16)
            target[pl.ds(row, size), :] = piece[start : start + size, :]


def shipped(place, packed, shard, row, columns, value):
    lead = (place[0] // 2) ^ (shard // 2)
    whose = (place[0] % 2) ^ (shard % 2)
    packed[whose, lead, row : row + value.shape[0], columns] = value.astype(LOW)


def handed(packed, kept, sent, semaphores):
    copies = [
        pltpu.make_async_copy(packed.at[whose], target, semaphores.at[whose])
        for whose, target in enumerate((kept, sent))
    ]
    for copy in copies:
        copy.start()
    for copy in copies:
        copy.wait()


def shipped_rows(place, packed, start, size, row, columns, value):
    end = start + value.shape[0]
    for shard in range(SHARDS):
        low, high = max(start, shard * size), min(end, (shard + 1) * size)
        if low < high:
            part = value[low - start : high - start]
            shipped(place, packed, shard, row + low - shard * size, columns, part)


def project_kernel(
    place, tokens, gains, one_piece, two_piece, three_piece, four_piece, cosine, sine,
    normed, query, keyval, weight,
):
    laid(place, (one_piece, two_piece, three_piece, four_piece), weight, D // SHARDS)
    rows = GROUP * WINDOW
    xhat, _ = normalised(tokens[...].reshape(rows, D))
    low = (xhat * gains[0:1, :]).astype(LOW)
    normed[...] = low.reshape(GROUP, WINDOW, D)
    mine = slice(HALF, HALF + WINDOW)
    cos, sin = cosine[mine], sine[mine]
    out = dot(low, weight[:, :D])
    for one in range(GROUP):
        for p in range(PAIRS):
            part = out[one * WINDOW : (one + 1) * WINDOW, pair(p)]
            query[one, :, pair(p)] = (turned(part, cos, sin) * HEAD**-0.5).astype(LOW)
    out = dot(low, weight[:, D : 2 * D])
    for one in range(GROUP):
        for p in range(PAIRS):
            part = out[one * WINDOW : (one + 1) * WINDOW, pair(p)]
            keyval[one, :, pair(p)] = turned(part, cos, sin).astype(LOW)
    out = dot(low, weight[:, 2 * D :])
    keyval[:, :, D:] = out.astype(LOW).reshape(GROUP, WINDOW, D)


def attend_kernel(
    place, tokens, normed, left1, left2, right1, right2, gains, query, keyval, weight,
    one_piece, two_piece, three_piece, four_piece, cosine, sine, cap,
    normed_ext, keyval_ext, probs, attended, hidden, proj,
):
    group = tokens.shape[0]
    laid(place, (one_piece, two_piece, three_piece, four_piece), proj, D // SHARDS)
    gain = gains[0:1, :]
    ends = []
    for one in range(group):
        early = pl.program_id(0) == 0
        left = jnp.where(early, left1[one], left2[one])
        right = jnp.where(early, right1[one], right2[one])
        low_left = (left.astype(WIDE) * gain).astype(LOW)
        low_right = (right.astype(WIDE) * gain).astype(LOW)
        normed_ext[one, :HALF] = low_left
        normed_ext[one, HALF : HALF + WINDOW] = normed[one]
        normed_ext[one, HALF + WINDOW :] = low_right
        ends += [low_left, low_right]
    ends = jnp.concatenate(ends, axis=0)
    cos = jnp.concatenate([cosine[:HALF], cosine[HALF + WINDOW :]], axis=0)
    sin = jnp.concatenate([sine[:HALF], sine[HALF + WINDOW :]], axis=0)
    keys = dot(ends, weight[:, D : 2 * D])
    values = dot(ends, weight[:, 2 * D :]).astype(LOW)
    for one in range(group):
        keyval_ext[one, HALF : HALF + WINDOW] = keyval[one]
        rows = slice(one * WINDOW, (one + 1) * WINDOW)
        keyval_ext[one, :HALF, D:] = values[rows][:HALF]
        keyval_ext[one, HALF + WINDOW :, D:] = values[rows][HALF:]
        for p in range(PAIRS):
            key = turned(keys[rows, pair(p)], cos, sin).astype(LOW)
            keyval_ext[one, :HALF, pair(p)] = key[:HALF]
            keyval_ext[one, HALF + WINDOW :, pair(p)] = key[HALF:]
    limit = jnp.concatenate([cap[...], cap[...]], axis=1)
    for one in range(group):
        for p in range(PAIRS):
            asked = by_head(query[one, :, pair(p)])
            scores = dot(keyval_ext[one, :, pair(p)], asked, ((1,), (1,)))
            scores = jnp.minimum(scores, limit)
            top = jnp.max(scores, axis=0, keepdims=True)
            grown = jnp.exp(scores - top)
            prob = grown * (1.0 / jnp.sum(grown, axis=0, keepdims=True))
            prob = prob.astype(LOW)
            probs[one, p] = prob
            found = dot(prob, keyval_ext[one, :, pair(p, D)], ((0,), (0,)))
            attended[one, :, pair(p)] = side_by_side(found).astype(LOW)
    rows = group * WINDOW
    out = dot(attended[...].reshape(rows, D), proj[...])
    hidden[...] = tokens[...] + out.reshape(group, WINDOW, D)


def feed_kernel(
    place, hidden, cotangent, gains, proj, attended,
    wide1, wide2, wide3, wide4, down1, down2, down3, down4,
    output, d_hidden, d_out, gain_grad, kept, sent,
    wide, down, all_normed, all_inner, all_d_both, all_dy, all_d_attn, packed, semaphores,
):
    laid(place, (wide1, wide2, wide3, wide4), wide, D // SHARDS)
    laid(place, (down1, down2, down3, down4), down, FF // SHARDS, D // SHARDS)
    here = pl.ds(pl.multiple_of(pl.program_id(0) * GROUP * WINDOW, GROUP * WINDOW), GROUP * WINDOW)
    normed, inner, d_both = all_normed.at[here], all_inner.at[here], all_d_both.at[here]
    low_cotangent, d_attn = all_dy.at[here], all_d_attn.at[here]
    rows = GROUP * WINDOW
    state = hidden[...].reshape(rows, D)
    gain = gains[1:2, :]
    xhat, inverse = normalised(state)
    low = (xhat * gain).astype(LOW)
    normed[...] = low
    above = cotangent[...].reshape(rows, D)
    dy = above.astype(LOW)
    low_cotangent[...] = dy
    start = 0
    while start < FF:
        size = min(256, FF - start)
        cols = slice(start, start + size)
        other = slice(FF + start, FF + start + size)
        gate = dot(low, wide[:, cols])
        upward = dot(low, wide[:, other])
        d_inner = dot(dy, down[cols, :], ((1,), (1,)))
        area = 0.5 + 0.5 * lax.erf(gate * (0.5**0.5))
        shaped = gate * area
        slope = area + gate * (jnp.exp(-0.5 * gate * gate) * 0.3989422804014327)
        inner[:, cols] = (shaped * upward).astype(LOW)
        d_both[:, cols] = (d_inner * upward * slope).astype(LOW)
        d_both[:, other] = (d_inner * shaped).astype(LOW)
        start += size
    output[...] = (state + dot(inner[...], down[...])).reshape(GROUP, WINDOW, D)
    d_normed = dot(d_both[...], wide[...], ((1,), (1,)))
    part = jnp.sum(d_normed * xhat, axis=0, keepdims=True)

    @pl.when(pl.program_id(0) == 0)
    def _():
        gain_grad[...] = part

    @pl.when(pl.program_id(0) > 0)
    def _():
        gain_grad[...] += part

    back = above + normalised_back(d_normed, gain, xhat, inverse)
    d_hidden[...] = back.reshape(GROUP, WINDOW, D)
    back = back.astype(LOW)
    d_attn[...] = back
    d_out[...] = dot(back, proj[...], ((1,), (1,))).astype(LOW).reshape(GROUP, WINDOW, D)

    @pl.when(pl.program_id(0) == pl.num_programs(0) - 1)
    def _():
        first_rows = ((0,), (0,))
        every = slice(0, D)
        size = D // 2
        for start in range(0, D, size):
            lanes = slice(start, start + size)
            for third in range(3):
                grad = dot(all_normed[:, lanes], all_d_both[:, third * D : (third + 1) * D], first_rows)
                shipped_rows(place, packed, start, D // SHARDS, third * D // SHARDS, every, grad)
            grad = dot(attended[:, lanes], all_d_attn[...], first_rows)
            shipped_rows(place, packed, start, D // SHARDS, 3 * D // SHARDS, every, grad)
        for start in range(0, FF, size):
            grad = dot(all_inner[:, start : start + size], all_dy[...], first_rows)
            shipped_rows(place, packed, start, FF // SHARDS, D, every, grad)
        handed(packed, kept, sent, semaphores)


def back_step(
    query, keyval, probs, d_out, weight, cosine, sine, normed_ext, start,
    d_left, d_right, d_normed, all_query, all_keyval, gain_grad,
):
    step = pl.program_id(0)
    mine = slice(HALF, HALF + WINDOW)
    cos, sin = cosine[mine], sine[mine]
    here = pl.ds(pl.multiple_of(step * GROUP * WINDOW, GROUP * WINDOW), GROUP * WINDOW)
    d_query = all_query.at[here]
    here = pl.ds(pl.multiple_of(step * GROUP * SPAN, GROUP * SPAN), GROUP * SPAN)
    d_keyval = all_keyval.at[here]
    for one in range(GROUP):
        short = slice(one * WINDOW, (one + 1) * WINDOW)
        long = slice(one * SPAN, (one + 1) * SPAN)
        for p in range(PAIRS):
            asked = by_head(query[one, :, pair(p)])
            key = keyval[one, :, pair(p)]
            grad = by_head(d_out[one, :, pair(p)])
            low_prob = probs[one, p]
            prob = low_prob.astype(WIDE)
            d_prob = dot(keyval[one, :, pair(p, D)], grad, ((1,), (1,)))
            delta = jnp.sum(prob * d_prob, axis=0, keepdims=True)
            d_score = (prob * (d_prob - delta)).astype(LOW)
            d_q = side_by_side(dot(d_score, key, ((0,), (0,)))) * HEAD**-0.5
            d_query[short, pair(p)] = turned_back(d_q, cos, sin).astype(LOW)
            d_k = dot(d_score, asked)
            d_keyval[long, pair(p)] = turned_back(d_k, cosine[...], sine[...]).astype(LOW)
            d_v = dot(low_prob, grad)
            d_keyval[long, pair(p, D)] = d_v.astype(LOW)
    both = dot(d_keyval[...], weight[:, D:], ((1,), (1,)))
    own = dot(d_query[...], weight[:, :D], ((1,), (1,)))
    total = jnp.zeros((1, D), WIDE)
    for one in range(GROUP):
        part = both[one * SPAN : (one + 1) * SPAN]
        inside = own[one * WINDOW : (one + 1) * WINDOW]
        rows = normed_ext[start + one].astype(WIDE)
        total += jnp.sum(part * rows, axis=0, keepdims=True)
        total += jnp.sum(inside * rows[mine], axis=0, keepdims=True)
        d_left[one] = part[:HALF].astype(LOW)
        d_right[one] = part[HALF + WINDOW :].astype(LOW)
        d_normed[one] = part[mine] + inside

    @pl.when(step == 0)
    def _():
        gain_grad[...] = total

    @pl.when(step > 0)
    def _():
        gain_grad[...] += total


def first_back_kernel(
    query, keyval, probs, d_out, weight, cosine, sine, normed_ext,
    d_left, d_right, d_normed, all_query, all_keyval, gain_grad,
):
    back_step(
        query, keyval, probs, d_out, weight, cosine, sine, normed_ext, 0,
        d_left, d_right, d_normed, all_query, all_keyval, gain_grad,
    )


def second_back_kernel(
    place, query, keyval, probs, d_out, weight, cosine, sine, normed_ext, gains, gain_grad2,
    first_query, first_keyval, first_gain, earlier,
    d_left, d_right, d_normed, kept, sent,
    all_query, all_keyval, gain_grad1, packed, semaphores,
):
    del earlier
    mine = slice(HALF, HALF + WINDOW)
    start = normed_ext.shape[0] // 2 + pl.program_id(0) * GROUP
    back_step(
        query, keyval, probs, d_out, weight, cosine, sine, normed_ext, start,
        d_left, d_right, d_normed, all_query, all_keyval, gain_grad1,
    )

    @pl.when(pl.program_id(0) == pl.num_programs(0) - 1)
    def _():
        first_rows = ((0,), (0,))
        some = normed_ext.shape[0] // 2
        parts = ((slice(0, some), first_query, first_keyval), (slice(some, 2 * some), all_query, all_keyval))
        size = D // 2
        for start in range(0, D, size):
            lanes = slice(start, start + size)
            grad = 0.0
            for some_rows, part_query, _ in parts:
                rows = normed_ext[some_rows, mine, lanes].reshape(some * WINDOW, size)
                grad += dot(rows, part_query[...], first_rows)
            shipped_rows(place, packed, start, D // SHARDS, 0, slice(0, D), grad)
            for part in range(2):
                grad = 0.0
                for some_rows, _, part_keyval in parts:
                    rows = normed_ext[some_rows, :, lanes].reshape(some * SPAN, size)
                    grad += dot(rows, part_keyval[:, part * D : (part + 1) * D], first_rows)
                columns = slice((part + 1) * D, (part + 2) * D)
                shipped_rows(place, packed, start, D // SHARDS, 0, columns, grad)
        more = slice(D // SHARDS, D // SHARDS + GAIN_ROWS)
        first = (first_gain[...] + gain_grad1[...]) / gains[0:1, :]
        empty = jnp.zeros((GAIN_ROWS - 2, D), WIDE)
        both_gains = jnp.concatenate([first, gain_grad2[...], empty], axis=0).astype(LOW)
        for whose in range(2):
            for lead in range(2):
                packed[whose, lead, more, :] = jnp.zeros((GAIN_ROWS, 3 * D), LOW)
                packed[whose, lead, more, 3 * D // 2 : 5 * D // 2] = both_gains
        handed(packed, kept, sent, semaphores)


def enter_kernel(tokens, gains, d_normed, from_left, from_right, d_hidden, input_grad):
    rows = GROUP * WINDOW
    xhat, inverse = normalised(tokens[...].reshape(rows, D))
    parts = []
    for one in range(GROUP):
        parts += [
            d_normed[one, :HALF] + from_left[one].astype(WIDE),
            d_normed[one, HALF:] + from_right[one].astype(WIDE),
        ]
    back = normalised_back(jnp.concatenate(parts, axis=0), gains[0:1, :], xhat, inverse)
    input_grad[...] = d_hidden[...] + back.reshape(GROUP, WINDOW, D)


def whole(shape):
    return pl.BlockSpec(shape, lambda i: (0,) * len(shape))


def once(shape):
    return pl.BlockSpec(shape, lambda i: (0,) * len(shape), pipeline_mode=pl.Buffered(1))


def once_rows(rows):
    return lambda shape: pl.BlockSpec((rows, shape[1]), lambda i: (0, 0), pipeline_mode=pl.Buffered(1))


def scalar(shape):
    return pl.BlockSpec(memory_space=pltpu.SMEM)


def blocked(shape):
    return pl.BlockSpec((GROUP,) + tuple(shape[1:]), lambda i: (i,) + (0,) * (len(shape) - 1))


def blocked_by(count):
    return lambda shape: pl.BlockSpec((count,) + tuple(shape[1:]), lambda i: (i,) + (0,) * (len(shape) - 1))


def later(steps):
    return lambda shape: pl.BlockSpec(
        (GROUP,) + tuple(shape[1:]), lambda i: (i + steps,) + (0,) * (len(shape) - 1)
    )


def anywhere(shape):
    return pl.BlockSpec(memory_space=pl.ANY)


def called(kernel, sequences, operands, results, limit, scratch=(), group=GROUP, aliases=None):
    arrays = [array for array, _ in operands]
    return pl.pallas_call(
        kernel,
        grid=(sequences // group,),
        in_specs=[spec(array.shape) for array, spec in operands],
        out_specs=[spec(shape) for shape, _, spec in results],
        out_shape=[jax.ShapeDtypeStruct(shape, kind) for shape, kind, _ in results],
        scratch_shapes=list(scratch),
        input_output_aliases=aliases or {},
        compiler_params=pltpu.CompilerParams(
            dimension_semantics=("arbitrary",), vmem_limit_bytes=limit * MIB
        ),
        cost_estimate=pl.CostEstimate(flops=1000, bytes_accessed=1000, transcendentals=0),
    )(*arrays)


def swapped(value, axis, bit):
    count = lax.axis_size(axis)
    return lax.ppermute(value, axis, [(i, i ^ bit) for i in range(count)])


def exchanged(steps, carried=(), beside=None):
    kept, sent = [], []
    for how, value, axis, bit, dim in steps:
        if how == "lead":
            kept.append(value[0])
            value = value[1]
        elif how == "fold":
            side = (lax.axis_index(axis) // bit) % 2
            size = value.shape[dim] // 2
            kept.append(lax.dynamic_slice_in_dim(value, side * size, size, axis=dim))
            value = lax.dynamic_slice_in_dim(value, (1 - side) * size, size, axis=dim)
        else:
            kept.append(None)
        sent.append(value)
    held = lax.optimization_barrier(tuple(sent) + tuple(carried))
    sent, carried = held[: len(sent)], held[len(sent) :]
    got = []
    for (how, _, axis, bit, _), value in zip(steps, sent):
        got.append(lax.ppermute(value, axis, bit) if how == "send" else swapped(value, axis, bit))
    if beside is not None:
        carried = beside(*carried)
    held = lax.optimization_barrier(tuple(got) + tuple(carried))
    got, carried = held[: len(got)], held[len(got) :]
    results = []
    for (how, _, axis, bit, dim), mine, own, other in zip(steps, kept, sent, got):
        if how in ("fold", "lead"):
            other = (mine.astype(WIDE) + other.astype(WIDE)).astype(LOW)
        elif how == "full":
            other = (own.astype(WIDE) + other.astype(WIDE)).astype(LOW)
        elif how == "join":
            side = (lax.axis_index(axis) // bit) % 2
            low = jnp.where(side == 0, own, other)
            high = jnp.where(side == 0, other, own)
            other = jnp.concatenate([low, high], axis=dim)
        results.append(other)
    return results, carried


def far_sum(value):
    bit = 8
    while bit < lax.axis_size("seq"):
        ((value,), _) = exchanged([("full", value, "seq", bit, 0)])
        bit *= 2
    return value


def adamw(master, grad, first, second, rate):
    moment = 0.9 * first + 0.1 * grad
    square = 0.98 * second + 0.02 * grad * grad
    fixed_first = moment / (1.0 - 0.9**STEP)
    fixed_second = square / (1.0 - 0.98**STEP)
    update = fixed_first / (jnp.sqrt(fixed_second) + 1e-06) + 1e-05 * master
    return (master - rate * update, moment, square)


def in_order(pieces):
    place = lax.axis_index("wshard")
    size = pieces[0].shape[0]
    total = jnp.zeros((size * len(pieces),) + pieces[0].shape[1:], pieces[0].dtype)
    for known, piece in enumerate(pieces):
        total = lax.dynamic_update_slice_in_dim(total, piece, (place ^ known) * size, 0)
    return total


def tables(base, total):
    places = base - HALF + jnp.arange(SPAN, dtype=jnp.int32)
    freqs = 10000.0 ** (-jnp.arange(0, HEAD, 2).astype(WIDE) / HEAD)
    angles = places.astype(WIDE)[:, None] * freqs[None, :]
    cosine, sine = jnp.cos(angles), jnp.sin(angles)
    cosine = jnp.concatenate([cosine] * 4, axis=1)
    sine = jnp.concatenate([-sine, sine] * 2, axis=1)
    row = jnp.arange(WINDOW)[None, :]
    col = jnp.arange(SPAN)[:, None]
    seen = (col >= row) & (col <= row + WINDOW) & (places >= 0)[:, None] & (places < total)[:, None]
    return cosine, sine, jnp.where(seen, 3e38, -1e30).astype(WIDE)


def on_device(
    tokens,
    cotangent,
    qkv_master,
    proj_master,
    wide_master,
    down_master,
    norm_gains,
    qkv_first,
    proj_first,
    wide_first,
    down_first,
    gains_first,
    qkv_second,
    proj_second,
    wide_second,
    down_second,
    gains_second,
):
    sequences, local_len, width = tokens.shape
    blocks = lax.axis_size("seq")
    base = lax.axis_index("seq") * local_len
    to_right = [(i, i + 1) for i in range(blocks - 1)]
    to_left = [(i + 1, i) for i in range(blocks - 1)]

    shard_rows = qkv_master.shape[0]
    own_gains = jnp.pad(norm_gains, ((0, 14), (0, qkv_master.shape[1] - norm_gains.shape[1])))
    first = jnp.concatenate([qkv_master.astype(LOW), own_gains.astype(LOW)], axis=0)
    ends = normalised(tokens)[0].astype(LOW)
    some = sequences // 2
    tails, heads = ends[:, local_len - HALF :], ends[:, :HALF]
    first_y, first_core, left1, right1 = lax.optimization_barrier(
        (
            swapped(first, "wshard", 2),
            swapped(first, "wshard", 1),
            lax.ppermute(tails[:some], "seq", to_right),
            lax.ppermute(heads[:some], "seq", to_left),
        )
    )
    rest = jnp.concatenate([proj_master.astype(LOW), down_master.astype(LOW)], axis=0)
    ((first_both,), _) = exchanged([("pair", first_y, "wshard", 1, 0)])
    firsts_known = (first, first_core, first_y, first_both)
    gains = in_order([piece[shard_rows : shard_rows + 2, : norm_gains.shape[1]].T for piece in firsts_known])
    gains = gains.T.astype(WIDE)
    cosine, sine, cap = tables(base, local_len * blocks)
    place = lax.axis_index("wshard").astype(jnp.int32).reshape(1)
    cells = sequences * local_len
    spread = (sequences, local_len, D)
    halo = (sequences, HALF, D)
    def projection(table):
        return called(
            project_kernel,
            sequences,
            [(place, scalar), (tokens, blocked), (gains, whole)]
            + [(piece, once_rows(shard_rows)) for piece in firsts_known]
            + [(table, whole), (sine, whole)],
            [
                (spread, LOW, blocked),
                (spread, LOW, blocked),
                ((sequences, local_len, 2 * D), LOW, blocked),
                ((D, 3 * D), LOW, whole),
            ],
            48,
        )

    (rest_y, rest_core, left2, right2), (normed, query, keyval, qkv) = exchanged(
        [
            ("pair", rest, "wshard", 2, 0),
            ("pair", rest, "wshard", 1, 0),
            ("send", tails[some:], "seq", to_right, 0),
            ("send", heads[some:], "seq", to_left, 0),
        ],
        (cosine,),
        projection,
    )
    ((rest_both,), _) = exchanged([("pair", rest_y, "wshard", 1, 0)])
    several = blocked_by(some)

    def attention(table, last):
        return called(
            attend_kernel,
            sequences,
            [
                (place, scalar), (tokens, several), (normed, several), (left1, once),
                (left2, once), (right1, once), (right2, once),
                (gains, whole), (query, several), (keyval, several), (qkv, once),
            ]
            + [(piece, once_rows(proj_master.shape[0])) for piece in (rest, rest_core, rest_y, last)]
            + [(table, whole), (sine, whole), (cap, whole)],
            [
                ((sequences, SPAN, D), LOW, several),
                ((sequences, SPAN, 2 * D), LOW, several),
                ((sequences, PAIRS, SPAN, SPAN), LOW, several),
                (spread, LOW, several),
                (spread, WIDE, several),
                ((D, D), LOW, whole),
            ],
            60,
            group=some,
        )

    low_wide = wide_master.astype(LOW)
    (wide_y, wide_core), attention_results = exchanged(
        [("pair", low_wide, "wshard", 2, 0), ("pair", low_wide, "wshard", 1, 0)],
        (cosine, rest_both),
        attention,
    )
    rests = (rest, rest_core, rest_y, rest_both)
    normed_ext, keyval_ext, probs, attended, hidden, proj = attention_results
    ((wide_both,), _) = exchanged([("pair", wide_y, "wshard", 1, 0)])
    wides = (low_wide, wide_core, wide_y, wide_both)
    rest_rows = 3 * shard_rows + rest.shape[0]
    shares = (2, rest_rows, D)
    layer_output, d_hidden, d_out, gain_grad2, rest_kept, rest_sent = called(
        feed_kernel,
        sequences,
        [
            (place, scalar), (hidden, blocked), (cotangent, blocked), (gains, whole),
            (proj, once), (attended.reshape(cells, D), once),
        ]
        + [(piece, once) for piece in wides + rests],
        [
            (spread, WIDE, blocked),
            (spread, WIDE, blocked),
            (spread, LOW, blocked),
            ((1, D), WIDE, whole),
            (shares, LOW, anywhere),
            (shares, LOW, anywhere),
        ],
        60,
        [
            pltpu.VMEM((D, 2 * FF), LOW),
            pltpu.VMEM((FF, D), LOW),
            pltpu.VMEM((cells, D), LOW),
            pltpu.VMEM((cells, FF), LOW),
            pltpu.VMEM((cells, 2 * FF), LOW),
            pltpu.VMEM((cells, D), LOW),
            pltpu.VMEM((cells, D), LOW),
            pltpu.VMEM((2,) + shares, LOW),
            pltpu.SemaphoreType.DMA((2,)),
        ],
    )

    def summed(*parts):
        return sum(part.astype(WIDE) for part in parts).astype(LOW)

    ((rest_got,), _) = exchanged([("pair", rest_sent, "wshard", 1, 0)])
    shares = (2, shard_rows + GAIN_ROWS, 3 * D)
    side = (lax.axis_index("seq") // 2) % 2

    def rows_of(value, which):
        size = value.shape[1] // 2
        width = value.shape[2] // 2
        return lax.dynamic_slice(value, (0, which * size, width), (2, size, width))

    near_sent = summed(rest_kept[1, :, : D // 2], rest_got[1, :, : D // 2])
    far_sent = summed(rows_of(rest_kept, 1 - side), rows_of(rest_got, 1 - side))
    part = sequences // 2
    half_halo = (part, HALF, D)
    half_rows = part * local_len

    def first_back(table):
        return called(
            first_back_kernel,
            part,
            [
                (query, blocked), (keyval_ext, blocked), (probs, blocked), (d_out, blocked),
                (qkv, once), (table, whole), (sine, whole), (normed_ext, blocked),
            ],
            [
                (half_halo, LOW, blocked),
                (half_halo, LOW, blocked),
                (spread, WIDE, blocked),
                ((half_rows, D), LOW, whole),
                ((2 * half_rows, 2 * D), LOW, whole),
                ((1, D), WIDE, whole),
            ],
            56,
        )

    (near, far), first_results = exchanged(
        [("pair", near_sent, "wshard", 2, 0), ("pair", far_sent, "seq", 2, 0)], (cosine,), first_back
    )
    near = summed(rest_kept[0, :, : D // 2], rest_got[0, :, : D // 2], near)
    far = summed(rows_of(rest_kept, side), rows_of(rest_got, side), far)
    d_left, d_right, d_normed, first_query, first_keyval, first_gain = first_results
    after = later(part // GROUP)

    def second_back(table):
        return called(
            second_back_kernel,
            part,
            [
                (place, scalar), (query, after), (keyval_ext, after), (probs, after), (d_out, after),
                (qkv, once), (table, whole), (sine, whole), (normed_ext, once), (gains, whole),
                (gain_grad2, whole), (first_query, once), (first_keyval, once), (first_gain, whole),
                (d_normed, anywhere),
            ],
            [
                (half_halo, LOW, blocked),
                (half_halo, LOW, blocked),
                (spread, WIDE, after),
                (shares, LOW, anywhere),
                (shares, LOW, anywhere),
            ],
            60,
            [
                pltpu.VMEM((half_rows, D), LOW),
                pltpu.VMEM((2 * half_rows, 2 * D), LOW),
                pltpu.VMEM((1, D), WIDE),
                pltpu.VMEM((2,) + shares, LOW),
                pltpu.SemaphoreType.DMA((2,)),
            ],
            aliases={14: 2},
        )

    (near, far, left_one, right_one), second_results = exchanged(
        [
            ("fold", near, "seq", 1, 0),
            ("lead", far, "wshard", 2, 0),
            ("send", d_right, "seq", to_right, 0),
            ("send", d_left, "seq", to_left, 0),
        ],
        (cosine,),
        second_back,
    )
    d_left, d_right, d_normed, kept, sent = second_results
    (got, near, far), _ = exchanged(
        [
            ("pair", sent, "wshard", 1, 0),
            ("fold", near, "seq", 2, 0),
            ("fold", far, "seq", 1, 0),
        ]
    )
    half = 3 * D // 2
    one_sent = summed(kept[1, :shard_rows, :half], got[1, :shard_rows, :half])
    two_sent = summed(rows_of(kept, 1 - side), rows_of(got, 1 - side))

    cuts = (0, part // 2, part)
    from_left, from_right = [left_one], [right_one]

    def round_of(steps, cut=None):
        if cut is not None:
            rows = slice(cuts[cut], cuts[cut + 1])
            steps = steps + [
                ("send", d_right[rows], "seq", to_right, 0),
                ("send", d_left[rows], "seq", to_left, 0),
            ]
        results, _ = exchanged(steps)
        if cut is not None:
            from_right.append(results.pop())
            from_left.append(results.pop())
        return results

    near, one_grad, two_grad = round_of(
        [
            ("full", near, "seq", 4, 0),
            ("pair", one_sent, "wshard", 2, 0),
            ("pair", two_sent, "seq", 2, 0),
        ],
        0,
    )
    one_grad = summed(kept[0, :shard_rows, :half], got[0, :shard_rows, :half], one_grad)
    two_grad = summed(rows_of(kept, side), rows_of(got, side), two_grad)
    far, one_grad, two_grad = round_of(
        [
            ("full", far, "seq", 4, 0),
            ("fold", one_grad, "seq", 2, 0),
            ("lead", two_grad, "wshard", 2, 0),
        ],
        1,
    )
    near, far = far_sum(near), far_sum(far)
    near, far, one_grad, two_grad = round_of(
        [
            ("join", near, "seq", 2, 0),
            ("join", far, "seq", 1, 0),
            ("full", one_grad, "seq", 4, 0),
            ("full", two_grad, "seq", 1, 0),
        ]
    )
    near, far, one_grad, two_grad = round_of(
        [
            ("join", near, "seq", 1, 0),
            ("join", far, "seq", 2, 0),
            ("full", one_grad, "seq", 1, 0),
            ("full", two_grad, "seq", 4, 0),
        ]
    )
    rest_grad = jnp.concatenate([near, far], axis=1)
    input_grad = called(
        enter_kernel,
        sequences,
        [
            (tokens, blocked), (gains, whole), (d_normed, blocked),
            (jnp.concatenate(from_left, axis=0), blocked),
            (jnp.concatenate(from_right, axis=0), blocked),
            (d_hidden, blocked),
        ],
        [(spread, WIDE, blocked)],
        32,
    )[0]
    one_grad, two_grad = far_sum(one_grad), far_sum(two_grad)
    one_rows = one_grad.shape[0]
    last = lax.optimization_barrier(jnp.concatenate([one_grad, two_grad], axis=0))
    ((other,), _) = exchanged([("pair", last, "seq", 2, 0)])
    upper = (lax.axis_index("seq") // 2) % 2 == 0
    low, high = jnp.where(upper, last, other), jnp.where(upper, other, last)
    one_grad = jnp.concatenate([low[:one_rows], high[:one_rows]], axis=0)
    two_grad = jnp.concatenate([low[one_rows:], high[one_rows:]], axis=0)
    rest_grad, one_grad, two_grad = (grad.astype(WIDE) for grad in (rest_grad, one_grad, two_grad))
    gains_sum = lax.dynamic_slice_in_dim(
        two_grad[shard_rows : shard_rows + 2],
        lax.axis_index("wshard") * norm_gains.shape[1],
        norm_gains.shape[1],
        axis=1,
    )
    wide_parts = [rest_grad[third * shard_rows : (third + 1) * shard_rows] for third in range(3)]
    owned_grads = (
        jnp.concatenate([one_grad, two_grad[:shard_rows]], axis=1),
        rest_grad[3 * shard_rows : 4 * shard_rows],
        jnp.concatenate(wide_parts, axis=1),
        rest_grad[4 * shard_rows :],
        gains_sum,
    )
    rates = (
        2.0 * D ** (-0.5),
        2.0 * max(D // WINDOW, 1) ** (-0.5),
        2.0 * D ** (-0.5),
        2.0 * FF ** (-0.5),
        1.0,
    )
    masters = (qkv_master, proj_master, wide_master, down_master, norm_gains)
    firsts = (qkv_first, proj_first, wide_first, down_first, gains_first)
    seconds = (qkv_second, proj_second, wide_second, down_second, gains_second)
    results = [adamw(masters[i], owned_grads[i], firsts[i], seconds[i], rates[i]) for i in range(5)]
    return (
        layer_output,
        input_grad,
        results[0][0],
        results[1][0],
        results[2][0],
        results[3][0],
        results[4][0],
        results[0][1],
        results[1][1],
        results[2][1],
        results[3][1],
        results[4][1],
        results[0][2],
        results[1][2],
        results[2][2],
        results[3][2],
        results[4][2],
    )


def solution(mesh):
    placed = (
        P("wshard", "seq", None),
        P("wshard", "seq", None),
        P("wshard", None),
        P("wshard", None),
        P("wshard", None),
        P("wshard", None),
        P(None, "wshard"),
        P("wshard", None),
        P("wshard", None),
        P("wshard", None),
        P("wshard", None),
        P(None, "wshard"),
        P("wshard", None),
        P("wshard", None),
        P("wshard", None),
        P("wshard", None),
        P(None, "wshard"),
    )
    return jax.shard_map(
        on_device,
        mesh=mesh,
        in_specs=placed,
        out_specs=(
            P("wshard", "seq", None),
            P("wshard", "seq", None),
            P("wshard", None),
            P("wshard", None),
            P("wshard", None),
            P("wshard", None),
            P(None, "wshard"),
            P("wshard", None),
            P("wshard", None),
            P("wshard", None),
            P("wshard", None),
            P(None, "wshard"),
            P("wshard", None),
            P("wshard", None),
            P("wshard", None),
            P("wshard", None),
            P(None, "wshard"),
        ),
        check_vma=False,
    )
```

```python
import jax
import jax.numpy as jnp
from jax import lax
from jax.experimental import pallas as pl
from jax.experimental.pallas import tpu as pltpu
from jax.sharding import PartitionSpec as P

D = 768
HEADS = 12
HEAD = 64
FF = 1152
WINDOW = 128
STEP = 10
HALF = WINDOW // 2
SPAN = 2 * WINDOW
LANES = 128
PAIRS = D // LANES
GROUP = 2
LOW = jnp.bfloat16
WIDE = jnp.float32
SHARDS = 4
GAIN_ROWS = 16
MIB = 1 << 20


def dot(one, other, dims=((1,), (0,))):
    return lax.dot_general(one, other, (dims, ((), ())), preferred_element_type=WIDE)


def normalised(value):
    centred = value - jnp.mean(value, axis=-1, keepdims=True)
    inverse = lax.rsqrt(jnp.mean(centred * centred, axis=-1, keepdims=True) + 1e-05)
    return centred * inverse, inverse


def normalised_back(d_normed, gain, xhat, inverse):
    d_xhat = d_normed * gain
    mean = jnp.mean(d_xhat, axis=-1, keepdims=True)
    slope = jnp.mean(d_xhat * xhat, axis=-1, keepdims=True)
    return inverse * (d_xhat - mean - xhat * slope)


def lane_of(rows):
    return lax.broadcasted_iota(jnp.int32, (rows, LANES), 1)


def half_swapped(value):
    first = lane_of(value.shape[0]) % HEAD < HEAD // 2
    ahead = pltpu.roll(value, LANES - HEAD // 2, 1)
    behind = pltpu.roll(value, HEAD // 2, 1)
    return jnp.where(first, ahead, behind)


def turned(value, cosine, sine):
    return value * cosine + half_swapped(value) * sine


def turned_back(value, cosine, sine):
    return value * cosine - half_swapped(value) * sine


def by_head(value):
    first = lane_of(value.shape[0]) < HEAD
    zero = jnp.zeros_like(value)
    return jnp.concatenate([jnp.where(first, value, zero), jnp.where(first, zero, value)], axis=0)


def side_by_side(value):
    rows = value.shape[0] // 2
    return jnp.where(lane_of(rows) < HEAD, value[:rows], value[rows:])


def pair(index, start=0):
    return slice(start + index * LANES, start + (index + 1) * LANES)


def laid(place, pieces, target, size, start=0):
    @pl.when(pl.program_id(0) == 0)
    def _():
        for known, piece in enumerate(pieces):
            row = pl.multiple_of((place[0] ^ known) * size, 16)
            target[pl.ds(row, size), :] = piece[start : start + size, :]


def shipped(place, packed, shard, row, columns, value):
    lead = (place[0] // 2) ^ (shard // 2)
    whose = (place[0] % 2) ^ (shard % 2)
    packed[whose, lead, row : row + value.shape[0], columns] = value.astype(LOW)


def handed(packed, kept, sent, semaphores):
    copies = [
        pltpu.make_async_copy(packed.at[whose], target, semaphores.at[whose])
        for whose, target in enumerate((kept, sent))
    ]
    for copy in copies:
        copy.start()
    for copy in copies:
        copy.wait()


def shipped_rows(place, packed, start, size, row, columns, value):
    end = start + value.shape[0]
    for shard in range(SHARDS):
        low, high = max(start, shard * size), min(end, (shard + 1) * size)
        if low < high:
            part = value[low - start : high - start]
            shipped(place, packed, shard, row + low - shard * size, columns, part)


def project_kernel(
    place, tokens, gains, one_piece, two_piece, three_piece, four_piece, cosine, sine,
    normed, query, keyval, weight,
):
    laid(place, (one_piece, two_piece, three_piece, four_piece), weight, D // SHARDS)
    rows = GROUP * WINDOW
    xhat, _ = normalised(tokens[...].reshape(rows, D))
    low = (xhat * gains[0:1, :]).astype(LOW)
    normed[...] = low.reshape(GROUP, WINDOW, D)
    mine = slice(HALF, HALF + WINDOW)
    cos, sin = cosine[mine], sine[mine]
    out = dot(low, weight[:, :D])
    for one in range(GROUP):
        for p in range(PAIRS):
            part = out[one * WINDOW : (one + 1) * WINDOW, pair(p)]
            query[one, :, pair(p)] = (turned(part, cos, sin) * HEAD**-0.5).astype(LOW)
    out = dot(low, weight[:, D : 2 * D])
    for one in range(GROUP):
        for p in range(PAIRS):
            part = out[one * WINDOW : (one + 1) * WINDOW, pair(p)]
            keyval[one, :, pair(p)] = turned(part, cos, sin).astype(LOW)
    out = dot(low, weight[:, 2 * D :])
    keyval[:, :, D:] = out.astype(LOW).reshape(GROUP, WINDOW, D)


def attend_kernel(
    place, tokens, normed, left1, left2, right1, right2, gains, query, keyval, weight,
    one_piece, two_piece, three_piece, four_piece, cosine, sine, cap,
    normed_ext, keyval_ext, probs, attended, hidden, proj,
):
    group = tokens.shape[0]
    laid(place, (one_piece, two_piece, three_piece, four_piece), proj, D // SHARDS)
    gain = gains[0:1, :]
    ends = []
    for one in range(group):
        early = pl.program_id(0) == 0
        left = jnp.where(early, left1[one], left2[one])
        right = jnp.where(early, right1[one], right2[one])
        low_left = (left.astype(WIDE) * gain).astype(LOW)
        low_right = (right.astype(WIDE) * gain).astype(LOW)
        normed_ext[one, :HALF] = low_left
        normed_ext[one, HALF : HALF + WINDOW] = normed[one]
        normed_ext[one, HALF + WINDOW :] = low_right
        ends += [low_left, low_right]
    ends = jnp.concatenate(ends, axis=0)
    cos = jnp.concatenate([cosine[:HALF], cosine[HALF + WINDOW :]], axis=0)
    sin = jnp.concatenate([sine[:HALF], sine[HALF + WINDOW :]], axis=0)
    keys = dot(ends, weight[:, D : 2 * D])
    values = dot(ends, weight[:, 2 * D :]).astype(LOW)
    for one in range(group):
        keyval_ext[one, HALF : HALF + WINDOW] = keyval[one]
        rows = slice(one * WINDOW, (one + 1) * WINDOW)
        keyval_ext[one, :HALF, D:] = values[rows][:HALF]
        keyval_ext[one, HALF + WINDOW :, D:] = values[rows][HALF:]
        for p in range(PAIRS):
            key = turned(keys[rows, pair(p)], cos, sin).astype(LOW)
            keyval_ext[one, :HALF, pair(p)] = key[:HALF]
            keyval_ext[one, HALF + WINDOW :, pair(p)] = key[HALF:]
    limit = jnp.concatenate([cap[...], cap[...]], axis=1)
    for one in range(group):
        for p in range(PAIRS):
            asked = by_head(query[one, :, pair(p)])
            scores = dot(keyval_ext[one, :, pair(p)], asked, ((1,), (1,)))
            scores = jnp.minimum(scores, limit)
            top = jnp.max(scores, axis=0, keepdims=True)
            grown = jnp.exp(scores - top)
            prob = grown * (1.0 / jnp.sum(grown, axis=0, keepdims=True))
            prob = prob.astype(LOW)
            probs[one, p] = prob
            found = dot(prob, keyval_ext[one, :, pair(p, D)], ((0,), (0,)))
            attended[one, :, pair(p)] = side_by_side(found).astype(LOW)
    rows = group * WINDOW
    out = dot(attended[...].reshape(rows, D), proj[...])
    hidden[...] = tokens[...] + out.reshape(group, WINDOW, D)


def feed_kernel(
    place, hidden, cotangent, gains, proj, attended,
    wide1, wide2, wide3, wide4, down1, down2, down3, down4,
    output, d_hidden, d_out, gain_grad, kept, sent,
    wide, down, all_normed, all_inner, all_d_both, all_dy, all_d_attn, packed, semaphores,
):
    laid(place, (wide1, wide2, wide3, wide4), wide, D // SHARDS)
    laid(place, (down1, down2, down3, down4), down, FF // SHARDS, D // SHARDS)
    here = pl.ds(pl.multiple_of(pl.program_id(0) * GROUP * WINDOW, GROUP * WINDOW), GROUP * WINDOW)
    normed, inner, d_both = all_normed.at[here], all_inner.at[here], all_d_both.at[here]
    low_cotangent, d_attn = all_dy.at[here], all_d_attn.at[here]
    rows = GROUP * WINDOW
    state = hidden[...].reshape(rows, D)
    gain = gains[1:2, :]
    xhat, inverse = normalised(state)
    low = (xhat * gain).astype(LOW)
    normed[...] = low
    above = cotangent[...].reshape(rows, D)
    dy = above.astype(LOW)
    low_cotangent[...] = dy
    start = 0
    while start < FF:
        size = min(256, FF - start)
        cols = slice(start, start + size)
        other = slice(FF + start, FF + start + size)
        gate = dot(low, wide[:, cols])
        upward = dot(low, wide[:, other])
        d_inner = dot(dy, down[cols, :], ((1,), (1,)))
        area = 0.5 + 0.5 * lax.erf(gate * (0.5**0.5))
        shaped = gate * area
        slope = area + gate * (jnp.exp(-0.5 * gate * gate) * 0.3989422804014327)
        inner[:, cols] = (shaped * upward).astype(LOW)
        d_both[:, cols] = (d_inner * upward * slope).astype(LOW)
        d_both[:, other] = (d_inner * shaped).astype(LOW)
        start += size
    output[...] = (state + dot(inner[...], down[...])).reshape(GROUP, WINDOW, D)
    d_normed = dot(d_both[...], wide[...], ((1,), (1,)))
    part = jnp.sum(d_normed * xhat, axis=0, keepdims=True)

    @pl.when(pl.program_id(0) == 0)
    def _():
        gain_grad[...] = part

    @pl.when(pl.program_id(0) > 0)
    def _():
        gain_grad[...] += part

    back = above + normalised_back(d_normed, gain, xhat, inverse)
    d_hidden[...] = back.reshape(GROUP, WINDOW, D)
    back = back.astype(LOW)
    d_attn[...] = back
    d_out[...] = dot(back, proj[...], ((1,), (1,))).astype(LOW).reshape(GROUP, WINDOW, D)

    @pl.when(pl.program_id(0) == pl.num_programs(0) - 1)
    def _():
        first_rows = ((0,), (0,))
        every = slice(0, D)
        size = D // 2
        for start in range(0, D, size):
            lanes = slice(start, start + size)
            for third in range(3):
                grad = dot(all_normed[:, lanes], all_d_both[:, third * D : (third + 1) * D], first_rows)
                shipped_rows(place, packed, start, D // SHARDS, third * D // SHARDS, every, grad)
            grad = dot(attended[:, lanes], all_d_attn[...], first_rows)
            shipped_rows(place, packed, start, D // SHARDS, 3 * D // SHARDS, every, grad)
        for start in range(0, FF, size):
            grad = dot(all_inner[:, start : start + size], all_dy[...], first_rows)
            shipped_rows(place, packed, start, FF // SHARDS, D, every, grad)
        handed(packed, kept, sent, semaphores)


def back_step(
    query, keyval, probs, d_out, weight, cosine, sine, normed_ext, start,
    d_left, d_right, d_normed, all_query, all_keyval, gain_grad,
):
    step = pl.program_id(0)
    mine = slice(HALF, HALF + WINDOW)
    cos, sin = cosine[mine], sine[mine]
    here = pl.ds(pl.multiple_of(step * GROUP * WINDOW, GROUP * WINDOW), GROUP * WINDOW)
    d_query = all_query.at[here]
    here = pl.ds(pl.multiple_of(step * GROUP * SPAN, GROUP * SPAN), GROUP * SPAN)
    d_keyval = all_keyval.at[here]
    for one in range(GROUP):
        short = slice(one * WINDOW, (one + 1) * WINDOW)
        long = slice(one * SPAN, (one + 1) * SPAN)
        for p in range(PAIRS):
            asked = by_head(query[one, :, pair(p)])
            key = keyval[one, :, pair(p)]
            grad = by_head(d_out[one, :, pair(p)])
            low_prob = probs[one, p]
            prob = low_prob.astype(WIDE)
            d_prob = dot(keyval[one, :, pair(p, D)], grad, ((1,), (1,)))
            delta = jnp.sum(prob * d_prob, axis=0, keepdims=True)
            d_score = (prob * (d_prob - delta)).astype(LOW)
            d_q = side_by_side(dot(d_score, key, ((0,), (0,)))) * HEAD**-0.5
            d_query[short, pair(p)] = turned_back(d_q, cos, sin).astype(LOW)
            d_k = dot(d_score, asked)
            d_keyval[long, pair(p)] = turned_back(d_k, cosine[...], sine[...]).astype(LOW)
            d_v = dot(low_prob, grad)
            d_keyval[long, pair(p, D)] = d_v.astype(LOW)
    both = dot(d_keyval[...], weight[:, D:], ((1,), (1,)))
    own = dot(d_query[...], weight[:, :D], ((1,), (1,)))
    total = jnp.zeros((1, D), WIDE)
    for one in range(GROUP):
        part = both[one * SPAN : (one + 1) * SPAN]
        inside = own[one * WINDOW : (one + 1) * WINDOW]
        rows = normed_ext[start + one].astype(WIDE)
        total += jnp.sum(part * rows, axis=0, keepdims=True)
        total += jnp.sum(inside * rows[mine], axis=0, keepdims=True)
        d_left[one] = part[:HALF].astype(LOW)
        d_right[one] = part[HALF + WINDOW :].astype(LOW)
        d_normed[one] = part[mine] + inside

    @pl.when(step == 0)
    def _():
        gain_grad[...] = total

    @pl.when(step > 0)
    def _():
        gain_grad[...] += total


def first_back_kernel(
    query, keyval, probs, d_out, weight, cosine, sine, normed_ext,
    d_left, d_right, d_normed, all_query, all_keyval, gain_grad,
):
    back_step(
        query, keyval, probs, d_out, weight, cosine, sine, normed_ext, 0,
        d_left, d_right, d_normed, all_query, all_keyval, gain_grad,
    )


def second_back_kernel(
    place, query, keyval, probs, d_out, weight, cosine, sine, normed_ext, gains, gain_grad2,
    first_query, first_keyval, first_gain, earlier,
    d_left, d_right, d_normed, kept, sent,
    all_query, all_keyval, gain_grad1, packed, semaphores,
):
    del earlier
    mine = slice(HALF, HALF + WINDOW)
    start = normed_ext.shape[0] // 2 + pl.program_id(0) * GROUP
    back_step(
        query, keyval, probs, d_out, weight, cosine, sine, normed_ext, start,
        d_left, d_right, d_normed, all_query, all_keyval, gain_grad1,
    )

    @pl.when(pl.program_id(0) == pl.num_programs(0) - 1)
    def _():
        first_rows = ((0,), (0,))
        some = normed_ext.shape[0] // 2
        parts = ((slice(0, some), first_query, first_keyval), (slice(some, 2 * some), all_query, all_keyval))
        size = D // 2
        for start in range(0, D, size):
            lanes = slice(start, start + size)
            grad = 0.0
            for some_rows, part_query, _ in parts:
                rows = normed_ext[some_rows, mine, lanes].reshape(some * WINDOW, size)
                grad += dot(rows, part_query[...], first_rows)
            shipped_rows(place, packed, start, D // SHARDS, 0, slice(0, D), grad)
            for part in range(2):
                grad = 0.0
                for some_rows, _, part_keyval in parts:
                    rows = normed_ext[some_rows, :, lanes].reshape(some * SPAN, size)
                    grad += dot(rows, part_keyval[:, part * D : (part + 1) * D], first_rows)
                columns = slice((part + 1) * D, (part + 2) * D)
                shipped_rows(place, packed, start, D // SHARDS, 0, columns, grad)
        more = slice(D // SHARDS, D // SHARDS + GAIN_ROWS)
        first = (first_gain[...] + gain_grad1[...]) / gains[0:1, :]
        empty = jnp.zeros((GAIN_ROWS - 2, D), WIDE)
        both_gains = jnp.concatenate([first, gain_grad2[...], empty], axis=0).astype(LOW)
        for whose in range(2):
            for lead in range(2):
                packed[whose, lead, more, :] = jnp.zeros((GAIN_ROWS, 3 * D), LOW)
                packed[whose, lead, more, 3 * D // 2 : 5 * D // 2] = both_gains
        handed(packed, kept, sent, semaphores)


def enter_kernel(tokens, gains, d_normed, from_left, from_right, d_hidden, input_grad):
    rows = GROUP * WINDOW
    xhat, inverse = normalised(tokens[...].reshape(rows, D))
    parts = []
    for one in range(GROUP):
        parts += [
            d_normed[one, :HALF] + from_left[one].astype(WIDE),
            d_normed[one, HALF:] + from_right[one].astype(WIDE),
        ]
    back = normalised_back(jnp.concatenate(parts, axis=0), gains[0:1, :], xhat, inverse)
    input_grad[...] = d_hidden[...] + back.reshape(GROUP, WINDOW, D)


def whole(shape):
    return pl.BlockSpec(shape, lambda i: (0,) * len(shape))


def once(shape):
    return pl.BlockSpec(shape, lambda i: (0,) * len(shape), pipeline_mode=pl.Buffered(1))


def once_rows(rows):
    return lambda shape: pl.BlockSpec((rows, shape[1]), lambda i: (0, 0), pipeline_mode=pl.Buffered(1))


def scalar(shape):
    return pl.BlockSpec(memory_space=pltpu.SMEM)


def blocked(shape):
    return pl.BlockSpec((GROUP,) + tuple(shape[1:]), lambda i: (i,) + (0,) * (len(shape) - 1))


def blocked_by(count):
    return lambda shape: pl.BlockSpec((count,) + tuple(shape[1:]), lambda i: (i,) + (0,) * (len(shape) - 1))


def later(steps):
    return lambda shape: pl.BlockSpec(
        (GROUP,) + tuple(shape[1:]), lambda i: (i + steps,) + (0,) * (len(shape) - 1)
    )


def anywhere(shape):
    return pl.BlockSpec(memory_space=pl.ANY)


def called(kernel, sequences, operands, results, limit, scratch=(), group=GROUP, aliases=None):
    arrays = [array for array, _ in operands]
    return pl.pallas_call(
        kernel,
        grid=(sequences // group,),
        in_specs=[spec(array.shape) for array, spec in operands],
        out_specs=[spec(shape) for shape, _, spec in results],
        out_shape=[jax.ShapeDtypeStruct(shape, kind) for shape, kind, _ in results],
        scratch_shapes=list(scratch),
        input_output_aliases=aliases or {},
        compiler_params=pltpu.CompilerParams(
            dimension_semantics=("arbitrary",), vmem_limit_bytes=limit * MIB
        ),
        cost_estimate=pl.CostEstimate(flops=1000, bytes_accessed=1000, transcendentals=0),
    )(*arrays)


def swapped(value, axis, bit):
    count = lax.axis_size(axis)
    return lax.ppermute(value, axis, [(i, i ^ bit) for i in range(count)])


def exchanged(steps, carried=(), beside=None):
    kept, sent = [], []
    for how, value, axis, bit, dim in steps:
        if how == "lead":
            kept.append(value[0])
            value = value[1]
        elif how == "fold":
            side = (lax.axis_index(axis) // bit) % 2
            size = value.shape[dim] // 2
            kept.append(lax.dynamic_slice_in_dim(value, side * size, size, axis=dim))
            value = lax.dynamic_slice_in_dim(value, (1 - side) * size, size, axis=dim)
        else:
            kept.append(None)
        sent.append(value)
    held = lax.optimization_barrier(tuple(sent) + tuple(carried))
    sent, carried = held[: len(sent)], held[len(sent) :]
    got = []
    for (how, _, axis, bit, _), value in zip(steps, sent):
        got.append(lax.ppermute(value, axis, bit) if how == "send" else swapped(value, axis, bit))
    if beside is not None:
        carried = beside(*carried)
    held = lax.optimization_barrier(tuple(got) + tuple(carried))
    got, carried = held[: len(got)], held[len(got) :]
    results = []
    for (how, _, axis, bit, dim), mine, own, other in zip(steps, kept, sent, got):
        if how in ("fold", "lead"):
            other = (mine.astype(WIDE) + other.astype(WIDE)).astype(LOW)
        elif how == "full":
            other = (own.astype(WIDE) + other.astype(WIDE)).astype(LOW)
        elif how == "join":
            side = (lax.axis_index(axis) // bit) % 2
            low = jnp.where(side == 0, own, other)
            high = jnp.where(side == 0, other, own)
            other = jnp.concatenate([low, high], axis=dim)
        results.append(other)
    return results, carried


def far_sum(value):
    bit = 8
    while bit < lax.axis_size("seq"):
        ((value,), _) = exchanged([("full", value, "seq", bit, 0)])
        bit *= 2
    return value


def adamw(master, grad, first, second, rate):
    moment = 0.9 * first + 0.1 * grad
    square = 0.98 * second + 0.02 * grad * grad
    fixed_first = moment / (1.0 - 0.9**STEP)
    fixed_second = square / (1.0 - 0.98**STEP)
    update = fixed_first / (jnp.sqrt(fixed_second) + 1e-06) + 1e-05 * master
    return (master - rate * update, moment, square)


def in_order(pieces):
    place = lax.axis_index("wshard")
    size = pieces[0].shape[0]
    total = jnp.zeros((size * len(pieces),) + pieces[0].shape[1:], pieces[0].dtype)
    for known, piece in enumerate(pieces):
        total = lax.dynamic_update_slice_in_dim(total, piece, (place ^ known) * size, 0)
    return total


def tables(base, total):
    places = base - HALF + jnp.arange(SPAN, dtype=jnp.int32)
    freqs = 10000.0 ** (-jnp.arange(0, HEAD, 2).astype(WIDE) / HEAD)
    angles = places.astype(WIDE)[:, None] * freqs[None, :]
    cosine, sine = jnp.cos(angles), jnp.sin(angles)
    cosine = jnp.concatenate([cosine] * 4, axis=1)
    sine = jnp.concatenate([-sine, sine] * 2, axis=1)
    row = jnp.arange(WINDOW)[None, :]
    col = jnp.arange(SPAN)[:, None]
    seen = (col >= row) & (col <= row + WINDOW) & (places >= 0)[:, None] & (places < total)[:, None]
    return cosine, sine, jnp.where(seen, 3e38, -1e30).astype(WIDE)


def on_device(
    tokens,
    cotangent,
    qkv_master,
    proj_master,
    wide_master,
    down_master,
    norm_gains,
    qkv_first,
    proj_first,
    wide_first,
    down_first,
    gains_first,
    qkv_second,
    proj_second,
    wide_second,
    down_second,
    gains_second,
):
    sequences, local_len, width = tokens.shape
    blocks = lax.axis_size("seq")
    base = lax.axis_index("seq") * local_len
    to_right = [(i, i + 1) for i in range(blocks - 1)]
    to_left = [(i + 1, i) for i in range(blocks - 1)]

    shard_rows = qkv_master.shape[0]
    own_gains = jnp.pad(norm_gains, ((0, 14), (0, qkv_master.shape[1] - norm_gains.shape[1])))
    first = jnp.concatenate([qkv_master.astype(LOW), own_gains.astype(LOW)], axis=0)
    ends = normalised(tokens)[0].astype(LOW)
    some = sequences // 2
    tails, heads = ends[:, local_len - HALF :], ends[:, :HALF]
    first_y, first_core, left1, right1 = lax.optimization_barrier(
        (
            swapped(first, "wshard", 2),
            swapped(first, "wshard", 1),
            lax.ppermute(tails[:some], "seq", to_right),
            lax.ppermute(heads[:some], "seq", to_left),
        )
    )
    rest = jnp.concatenate([proj_master.astype(LOW), down_master.astype(LOW)], axis=0)
    ((first_both,), _) = exchanged([("pair", first_y, "wshard", 1, 0)])
    firsts_known = (first, first_core, first_y, first_both)
    gains = in_order([piece[shard_rows : shard_rows + 2, : norm_gains.shape[1]].T for piece in firsts_known])
    gains = gains.T.astype(WIDE)
    cosine, sine, cap = tables(base, local_len * blocks)
    place = lax.axis_index("wshard").astype(jnp.int32).reshape(1)
    cells = sequences * local_len
    spread = (sequences, local_len, D)
    halo = (sequences, HALF, D)
    def projection(table):
        return called(
            project_kernel,
            sequences,
            [(place, scalar), (tokens, blocked), (gains, whole)]
            + [(piece, once_rows(shard_rows)) for piece in firsts_known]
            + [(table, whole), (sine, whole)],
            [
                (spread, LOW, blocked),
                (spread, LOW, blocked),
                ((sequences, local_len, 2 * D), LOW, blocked),
                ((D, 3 * D), LOW, whole),
            ],
            48,
        )

    (rest_y, rest_core, left2, right2), (normed, query, keyval, qkv) = exchanged(
        [
            ("pair", rest, "wshard", 2, 0),
            ("pair", rest, "wshard", 1, 0),
            ("send", tails[some:], "seq", to_right, 0),
            ("send", heads[some:], "seq", to_left, 0),
        ],
        (cosine,),
        projection,
    )
    ((rest_both,), _) = exchanged([("pair", rest_y, "wshard", 1, 0)])
    several = blocked_by(some)

    def attention(table, last):
        return called(
            attend_kernel,
            sequences,
            [
                (place, scalar), (tokens, several), (normed, several), (left1, once),
                (left2, once), (right1, once), (right2, once),
                (gains, whole), (query, several), (keyval, several), (qkv, once),
            ]
            + [(piece, once_rows(proj_master.shape[0])) for piece in (rest, rest_core, rest_y, last)]
            + [(table, whole), (sine, whole), (cap, whole)],
            [
                ((sequences, SPAN, D), LOW, several),
                ((sequences, SPAN, 2 * D), LOW, several),
                ((sequences, PAIRS, SPAN, SPAN), LOW, several),
                (spread, LOW, several),
                (spread, WIDE, several),
                ((D, D), LOW, whole),
            ],
            60,
            group=some,
        )

    low_wide = wide_master.astype(LOW)
    (wide_y, wide_core), attention_results = exchanged(
        [("pair", low_wide, "wshard", 2, 0), ("pair", low_wide, "wshard", 1, 0)],
        (cosine, rest_both),
        attention,
    )
    rests = (rest, rest_core, rest_y, rest_both)
    normed_ext, keyval_ext, probs, attended, hidden, proj = attention_results
    ((wide_both,), _) = exchanged([("pair", wide_y, "wshard", 1, 0)])
    wides = (low_wide, wide_core, wide_y, wide_both)
    rest_rows = 3 * shard_rows + rest.shape[0]
    shares = (2, rest_rows, D)
    layer_output, d_hidden, d_out, gain_grad2, rest_kept, rest_sent = called(
        feed_kernel,
        sequences,
        [
            (place, scalar), (hidden, blocked), (cotangent, blocked), (gains, whole),
            (proj, once), (attended.reshape(cells, D), once),
        ]
        + [(piece, once) for piece in wides + rests],
        [
            (spread, WIDE, blocked),
            (spread, WIDE, blocked),
            (spread, LOW, blocked),
            ((1, D), WIDE, whole),
            (shares, LOW, anywhere),
            (shares, LOW, anywhere),
        ],
        60,
        [
            pltpu.VMEM((D, 2 * FF), LOW),
            pltpu.VMEM((FF, D), LOW),
            pltpu.VMEM((cells, D), LOW),
            pltpu.VMEM((cells, FF), LOW),
            pltpu.VMEM((cells, 2 * FF), LOW),
            pltpu.VMEM((cells, D), LOW),
            pltpu.VMEM((cells, D), LOW),
            pltpu.VMEM((2,) + shares, LOW),
            pltpu.SemaphoreType.DMA((2,)),
        ],
    )

    def summed(*parts):
        return sum(part.astype(WIDE) for part in parts).astype(LOW)

    ((rest_got,), _) = exchanged([("pair", rest_sent, "wshard", 1, 0)])
    shares = (2, shard_rows + GAIN_ROWS, 3 * D)
    side = (lax.axis_index("seq") // 2) % 2

    def rows_of(value, which):
        size = value.shape[1] // 2
        width = value.shape[2] // 2
        return lax.dynamic_slice(value, (0, which * size, width), (2, size, width))

    near_sent = summed(rest_kept[1, :, : D // 2], rest_got[1, :, : D // 2])
    far_sent = summed(rows_of(rest_kept, 1 - side), rows_of(rest_got, 1 - side))
    part = sequences // 2
    half_halo = (part, HALF, D)
    half_rows = part * local_len

    def first_back(table):
        return called(
            first_back_kernel,
            part,
            [
                (query, blocked), (keyval_ext, blocked), (probs, blocked), (d_out, blocked),
                (qkv, once), (table, whole), (sine, whole), (normed_ext, blocked),
            ],
            [
                (half_halo, LOW, blocked),
                (half_halo, LOW, blocked),
                (spread, WIDE, blocked),
                ((half_rows, D), LOW, whole),
                ((2 * half_rows, 2 * D), LOW, whole),
                ((1, D), WIDE, whole),
            ],
            56,
        )

    (near, far), first_results = exchanged(
        [("pair", near_sent, "wshard", 2, 0), ("pair", far_sent, "seq", 2, 0)], (cosine,), first_back
    )
    near = summed(rest_kept[0, :, : D // 2], rest_got[0, :, : D // 2], near)
    far = summed(rows_of(rest_kept, side), rows_of(rest_got, side), far)
    d_left, d_right, d_normed, first_query, first_keyval, first_gain = first_results
    after = later(part // GROUP)

    def second_back(table):
        return called(
            second_back_kernel,
            part,
            [
                (place, scalar), (query, after), (keyval_ext, after), (probs, after), (d_out, after),
                (qkv, once), (table, whole), (sine, whole), (normed_ext, once), (gains, whole),
                (gain_grad2, whole), (first_query, once), (first_keyval, once), (first_gain, whole),
                (d_normed, anywhere),
            ],
            [
                (half_halo, LOW, blocked),
                (half_halo, LOW, blocked),
                (spread, WIDE, after),
                (shares, LOW, anywhere),
                (shares, LOW, anywhere),
            ],
            60,
            [
                pltpu.VMEM((half_rows, D), LOW),
                pltpu.VMEM((2 * half_rows, 2 * D), LOW),
                pltpu.VMEM((1, D), WIDE),
                pltpu.VMEM((2,) + shares, LOW),
                pltpu.SemaphoreType.DMA((2,)),
            ],
            aliases={14: 2},
        )

    (near, far, left_one, right_one), second_results = exchanged(
        [
            ("fold", near, "seq", 1, 0),
            ("lead", far, "wshard", 2, 0),
            ("send", d_right, "seq", to_right, 0),
            ("send", d_left, "seq", to_left, 0),
        ],
        (cosine,),
        second_back,
    )
    d_left, d_right, d_normed, kept, sent = second_results
    (got, near, far), _ = exchanged(
        [
            ("pair", sent, "wshard", 1, 0),
            ("fold", near, "seq", 2, 0),
            ("fold", far, "seq", 1, 0),
        ]
    )
    half = 3 * D // 2
    one_sent = summed(kept[1, :shard_rows, :half], got[1, :shard_rows, :half])
    two_sent = summed(rows_of(kept, 1 - side), rows_of(got, 1 - side))

    cuts = (0, part // 2, part)
    from_left, from_right = [left_one], [right_one]

    def round_of(steps, cut=None):
        if cut is not None:
            rows = slice(cuts[cut], cuts[cut + 1])
            steps = steps + [
                ("send", d_right[rows], "seq", to_right, 0),
                ("send", d_left[rows], "seq", to_left, 0),
            ]
        results, _ = exchanged(steps)
        if cut is not None:
            from_right.append(results.pop())
            from_left.append(results.pop())
        return results

    near, one_grad, two_grad = round_of(
        [
            ("full", near, "seq", 4, 0),
            ("pair", one_sent, "wshard", 2, 0),
            ("pair", two_sent, "seq", 2, 0),
        ],
        0,
    )
    one_grad = summed(kept[0, :shard_rows, :half], got[0, :shard_rows, :half], one_grad)
    two_grad = summed(rows_of(kept, side), rows_of(got, side), two_grad)
    far, one_grad, two_grad = round_of(
        [
            ("full", far, "seq", 4, 0),
            ("fold", one_grad, "seq", 2, 0),
            ("lead", two_grad, "wshard", 2, 0),
        ],
        1,
    )
    near, far = far_sum(near), far_sum(far)
    near, far, one_grad, two_grad = round_of(
        [
            ("join", near, "seq", 2, 0),
            ("join", far, "seq", 1, 0),
            ("full", one_grad, "seq", 4, 0),
            ("full", two_grad, "seq", 1, 0),
        ]
    )
    near, far, one_grad, two_grad = round_of(
        [
            ("join", near, "seq", 1, 0),
            ("join", far, "seq", 2, 0),
            ("full", one_grad, "seq", 1, 0),
            ("full", two_grad, "seq", 4, 0),
        ]
    )
    rest_grad = jnp.concatenate([near, far], axis=1)
    input_grad = called(
        enter_kernel,
        sequences,
        [
            (tokens, blocked), (gains, whole), (d_normed, blocked),
            (jnp.concatenate(from_left, axis=0), blocked),
            (jnp.concatenate(from_right, axis=0), blocked),
            (d_hidden, blocked),
        ],
        [(spread, WIDE, blocked)],
        32,
    )[0]
    one_grad, two_grad = far_sum(one_grad), far_sum(two_grad)
    one_rows = one_grad.shape[0]
    last = lax.optimization_barrier(jnp.concatenate([one_grad, two_grad], axis=0))
    ((other,), _) = exchanged([("pair", last, "seq", 2, 0)])
    upper = (lax.axis_index("seq") // 2) % 2 == 0
    low, high = jnp.where(upper, last, other), jnp.where(upper, other, last)
    one_grad = jnp.concatenate([low[:one_rows], high[:one_rows]], axis=0)
    two_grad = jnp.concatenate([low[one_rows:], high[one_rows:]], axis=0)
    rest_grad, one_grad, two_grad = (grad.astype(WIDE) for grad in (rest_grad, one_grad, two_grad))
    gains_sum = lax.dynamic_slice_in_dim(
        two_grad[shard_rows : shard_rows + 2],
        lax.axis_index("wshard") * norm_gains.shape[1],
        norm_gains.shape[1],
        axis=1,
    )
    wide_parts = [rest_grad[third * shard_rows : (third + 1) * shard_rows] for third in range(3)]
    owned_grads = (
        jnp.concatenate([one_grad, two_grad[:shard_rows]], axis=1),
        rest_grad[3 * shard_rows : 4 * shard_rows],
        jnp.concatenate(wide_parts, axis=1),
        rest_grad[4 * shard_rows :],
        gains_sum,
    )
    rates = (
        2.0 * D ** (-0.5),
        2.0 * max(D // WINDOW, 1) ** (-0.5),
        2.0 * D ** (-0.5),
        2.0 * FF ** (-0.5),
        1.0,
    )
    masters = (qkv_master, proj_master, wide_master, down_master, norm_gains)
    firsts = (qkv_first, proj_first, wide_first, down_first, gains_first)
    seconds = (qkv_second, proj_second, wide_second, down_second, gains_second)
    results = [adamw(masters[i], owned_grads[i], firsts[i], seconds[i], rates[i]) for i in range(5)]
    return (
        layer_output,
        input_grad,
        results[0][0],
        results[1][0],
        results[2][0],
        results[3][0],
        results[4][0],
        results[0][1],
        results[1][1],
        results[2][1],
        results[3][1],
        results[4][1],
        results[0][2],
        results[1][2],
        results[2][2],
        results[3][2],
        results[4][2],
    )


def solution(mesh):
    placed = (
        P("wshard", "seq", None),
        P("wshard", "seq", None),
        P("wshard", None),
        P("wshard", None),
        P("wshard", None),
        P("wshard", None),
        P(None, "wshard"),
        P("wshard", None),
        P("wshard", None),
        P("wshard", None),
        P("wshard", None),
        P(None, "wshard"),
        P("wshard", None),
        P("wshard", None),
        P("wshard", None),
        P("wshard", None),
        P(None, "wshard"),
    )
    return jax.shard_map(
        on_device,
        mesh=mesh,
        in_specs=placed,
        out_specs=(
            P("wshard", "seq", None),
            P("wshard", "seq", None),
            P("wshard", None),
            P("wshard", None),
            P("wshard", None),
            P("wshard", None),
            P(None, "wshard"),
            P("wshard", None),
            P("wshard", None),
            P("wshard", None),
            P("wshard", None),
            P(None, "wshard"),
            P("wshard", None),
            P("wshard", None),
            P("wshard", None),
            P("wshard", None),
            P(None, "wshard"),
        ),
        check_vma=False,
    )
```
